32 devices in a mesh: dp: 8 (over y, x, core), tensor: 4 (over z).
Axes of the slice: x: 2, y: 2, z: 4, core: 2. Of those that a mesh axis runs over, the one named last changes fastest.
Arguments:
- tokens: bfloat16 [8192, 2048], P(('dp', 'tensor')), may hold values from -6 to 6
- segments: int32 [8192], P('dp'), may hold values from 0 to 23, as said below
- cotangent: bfloat16 [8192, 2048], P(('dp', 'tensor')), may hold values from -8 to 8
- attn_norm_gain: float32 [2048], replicated, may hold values from 0.1 to 1.9
- attn_norm_shift: float32 [2048], replicated, may hold values from -3 to 3
- w_query: bfloat16 [2048, 2048], P('dp', 'tensor'), may hold values from -0.125 to 0.125
- w_key: bfloat16 [2048, 2048], P('dp', 'tensor'), may hold values from -0.125 to 0.125
- w_value: bfloat16 [2048, 4096], P('dp', 'tensor'), may hold values from -0.125 to 0.125
- w_gate: bfloat16 [2048, 4096], P('dp', 'tensor'), may hold values from -0.125 to 0.125
- w_output: bfloat16 [4096, 2048], P('tensor', 'dp'), may hold values from -0.1875 to 0.1875
- ffn_norm_gain: float32 [2048], replicated, may hold values from 0.1 to 1.9
- ffn_norm_shift: float32 [2048], replicated, may hold values from -3 to 3
- w_ffn_gate: bfloat16 [2048, 4096], P('dp', 'tensor'), may hold values from -0.125 to 0.125
- w_ffn_up: bfloat16 [2048, 4096], P('dp', 'tensor'), may hold values from -0.125 to 0.125
- w_ffn_down: bfloat16 [4096, 2048], P('tensor', 'dp'), may hold values from -0.1875 to 0.1875
Outputs:
- layer_output: bfloat16 [8192, 2048], P(('dp', 'tensor'))
- grad_tokens: float32 [8192, 2048], P(('dp', 'tensor'))
- grad_attn_gain: float32 [2048], replicated
- grad_attn_shift: float32 [2048], replicated
- grad_query: float32 [2048, 2048], P('dp', 'tensor')
- grad_key: float32 [2048, 2048], P('dp', 'tensor')
- grad_value: float32 [2048, 4096], P('dp', 'tensor')
- grad_gate: float32 [2048, 4096], P('dp', 'tensor')
- grad_output: float32 [4096, 2048], P('tensor', 'dp')
- grad_ffn_gain: float32 [2048], replicated
- grad_ffn_shift: float32 [2048], replicated
- grad_ffn_gate: float32 [2048, 4096], P('dp', 'tensor')
- grad_ffn_up: float32 [2048, 4096], P('dp', 'tensor')
- grad_ffn_down: float32 [4096, 2048], P('tensor', 'dp')
The draws below stay inside these ranges and needn't reach their ends.
Inputs may be any that keep to these rules, and one draw needn't show every extreme that they name: `segments`: segment numbers never fall; sequence s (tokens s * 1024 to (s + 1) * 1024 - 1) holds three documents numbered 3 s, 3 s + 1, 3 s + 2; the first and the last have 1024 // 16 to 127 tokens.
All inputs are finite; a program needn't handle non-finite values.
Results may differ from the reference program's by a relative error of at most 0.015.
The reference program's roundings to bfloat16 on the way (of `normed`, `weights`, `gated` and `normed_two`) count: a program that leaves them out, or rounds other values in their place, can miss the bound.
Values may be sent and summed in bfloat16 or wider, within the bound.
No kernel may reach another device: no remote copies, remote signals or barrier semaphores. Data moves between devices by JAX's collectives and lax.ppermute only.
A program may use at most 256 MiB of HBM per device.

```python
from functools import partial
import jax
import jax.numpy as jnp
from jax import lax

D = 2048
HEADS = 8
KEY_DIM = 256
VALUE_DIM = 512
FF = 4096
SEQ = 1024
TOKENS = 8192
HK = 2048
HV = 4096


def draw_segments(key, part):
    key = jax.random.fold_in(key, 3)
    sequences = TOKENS // SEQ
    first_length = jax.random.randint(key, (sequences, 1), SEQ // 16, SEQ // 8)
    last_length = jax.random.randint(jax.random.fold_in(key, 1), (sequences, 1), SEQ // 16, SEQ // 8)
    places = jnp.arange(SEQ, dtype=jnp.int32)[None, :]
    within = (places >= first_length).astype(jnp.int32) + (places >= SEQ - last_length).astype(jnp.int32)
    offset_ids = 3 * jnp.arange(sequences, dtype=jnp.int32)[:, None]
    return (offset_ids + within).reshape(TOKENS).astype(jnp.int32)


def draw_cotangent(key, part):
    key = jax.random.fold_in(key, 7)
    rising = 0.5 + jnp.arange(TOKENS, dtype=jnp.float32)[:, None] / TOKENS
    values = rising * jax.random.normal(key, (TOKENS, D), jnp.float32)
    return jnp.clip(values, -8.0, 8.0).astype(jnp.bfloat16)


def level_of(key, shape, pieces, low, largest):
    level = 1.0
    for position, blocks in pieces:
        steps = jax.random.uniform(jax.random.fold_in(jax.random.fold_in(key, 6), position), (blocks,), jnp.float32, low / len(pieces), largest / len(pieces))
        level = level * jnp.repeat(jnp.exp(steps), shape[position] // blocks).reshape((-1,) + (1,) * (len(shape) - 1 - position))
    return level


def scatter_about(key, dims, scale, reach, pieces=(), kind=jnp.bfloat16):
    values = scale * jax.random.normal(key, dims, jnp.float32)
    if pieces:
        values = values * level_of(key, dims, pieces, -0.22, 0.18)
    return jnp.clip(values, -reach, reach).astype(kind)


def setup_inputs(seed: int = 0) -> dict:
    streams_of = jax.random.split(jax.random.key(seed), 16)
    tokens = scatter_about(streams_of[0], (TOKENS, D), 1.0, 6.0, ((0, 32),))
    segments = draw_segments(jax.random.fold_in(streams_of[15], 71), 0)
    cotangent = draw_cotangent(jax.random.fold_in(streams_of[15], 71), 0)
    attn_norm_gain = jnp.clip(1.0 + 0.18 * jax.random.normal(streams_of[3], (D,), jnp.float32), 0.1, 1.9)
    attn_norm_shift = scatter_about(streams_of[4], (D,), 0.5, 3.0, (), jnp.float32)
    w_query = scatter_about(streams_of[5], (D, HK), D ** -0.5, 0.125, ((0, 8), (1, 4)))
    w_key = scatter_about(streams_of[6], (D, HK), D ** -0.5, 0.125, ((0, 8), (1, 4)))
    w_value = scatter_about(streams_of[7], (D, HV), D ** -0.5, 0.125, ((0, 8), (1, 4)))
    w_gate = scatter_about(streams_of[8], (D, HV), D ** -0.5, 0.125, ((0, 8), (1, 4)))
    w_output = scatter_about(streams_of[9], (HV, D), (HV // 4) ** -0.5, 0.1875, ((0, 4), (1, 8)))
    ffn_norm_gain = jnp.clip(1.0 + 0.18 * jax.random.normal(streams_of[10], (D,), jnp.float32), 0.1, 1.9)
    ffn_norm_shift = scatter_about(streams_of[11], (D,), 0.5, 3.0, (), jnp.float32)
    w_ffn_gate = scatter_about(streams_of[12], (D, FF), D ** -0.5, 0.125, ((0, 8), (1, 4)))
    w_ffn_up = scatter_about(streams_of[13], (D, FF), D ** -0.5, 0.125, ((0, 8), (1, 4)))
    w_ffn_down = scatter_about(streams_of[14], (FF, D), (FF // 4) ** -0.5, 0.1875, ((0, 4), (1, 8)))
    return dict(tokens=tokens, segments=segments, cotangent=cotangent, attn_norm_gain=attn_norm_gain, attn_norm_shift=attn_norm_shift, w_query=w_query, w_key=w_key, w_value=w_value, w_gate=w_gate, w_output=w_output, ffn_norm_gain=ffn_norm_gain, ffn_norm_shift=ffn_norm_shift, w_ffn_gate=w_ffn_gate, w_ffn_up=w_ffn_up, w_ffn_down=w_ffn_down)


@jax.custom_vjp
def low(v):
    return lax.optimization_barrier(v.astype(jnp.bfloat16)).astype(jnp.float32)

@jax.custom_vjp
def low_back(v):
    return v

def low_keep(v):
    return (low(v), None)

def low_pass(kept, grad):
    return (grad,)

def back_keep(v):
    return (v, None)

def back_low(kept, grad):
    return (low(grad),)
low.defvjp(low_keep, low_pass)
low_back.defvjp(back_keep, back_low)

def layer_norm(values, gain, shift):
    centred = values - lax.optimization_barrier(jnp.mean(values, -1, keepdims=True))
    spread = lax.optimization_barrier(jnp.mean(centred * centred, -1, keepdims=True))
    return centred * lax.rsqrt(spread + 1e-05) * gain + shift

def decay_table(offset, row_count, segments, decay_rates):
    seq_len = segments.shape[0]
    row_pos = offset + jnp.arange(row_count, dtype=jnp.int32)
    col_pos = jnp.arange(seq_len, dtype=jnp.int32)
    row_seg = lax.dynamic_slice_in_dim(segments, offset, row_count, 0)
    inside = (row_pos[:, None] >= col_pos[None, :]) & (row_seg[:, None] == segments[None, :])
    distance = jnp.where(inside, row_pos[:, None] - col_pos[None, :], 0).astype(jnp.float32)
    return jnp.where(inside[None], jnp.exp(distance[None] * decay_rates[:, None, None]), 0.0)

def product(left, right):
    return jnp.dot(left, right, precision=lax.Precision.HIGHEST)

def head_retention(segments, operands):
    queries, key_rows, value_rows, head_number = operands
    decay_rates = jnp.log1p(-jnp.exp2(-5.0 - head_number))[None]
    decays = decay_table(0, SEQ, segments, decay_rates)[0]
    scores = low_back(product(queries, key_rows.T))
    weights = low(scores * decays)
    retained = low_back(product(weights, value_rows))
    return retained * lax.rsqrt(lax.optimization_barrier(jnp.mean(retained * retained, -1, keepdims=True)) + 1e-06)

def forward(tokens, segments, attn_gain, attn_shift, w_query, w_key, w_value, w_gate, w_output, ffn_gain, ffn_shift, w_ffn_gate, w_ffn_up, w_ffn_down):
    normed = low(layer_norm(tokens, attn_gain, attn_shift))
    queries = low(low_back(product(normed, w_query)))
    key_rows = low(low_back(product(normed, w_key)))
    value_rows = low(low_back(product(normed, w_value)))
    gate_pre = low_back(product(normed, w_gate))
    split_query = queries.reshape(SEQ, HEADS, KEY_DIM).transpose(1, 0, 2)
    split_key = key_rows.reshape(SEQ, HEADS, KEY_DIM).transpose(1, 0, 2)
    split_value = value_rows.reshape(SEQ, HEADS, VALUE_DIM).transpose(1, 0, 2)
    head_numbers = jnp.arange(HEADS, dtype=jnp.float32)
    retained = lax.map(jax.checkpoint(partial(head_retention, segments)), (split_query, split_key, split_value, head_numbers))
    merged = retained.transpose(1, 0, 2).reshape(SEQ, HEADS * VALUE_DIM)
    gated = low(low_back(jax.nn.silu(gate_pre) * merged))
    hidden = tokens + low_back(product(gated, w_output))
    normed_two = low(layer_norm(hidden, ffn_gain, ffn_shift))
    gate_two = low_back(product(normed_two, w_ffn_gate))
    up_two = low_back(product(normed_two, w_ffn_up))
    inner_act = low(low_back(jax.nn.gelu(gate_two, approximate=False) * up_two))
    return hidden + low_back(product(inner_act, w_ffn_down))

def reference(tokens, segments, cotangent, attn_norm_gain, attn_norm_shift, w_query, w_key, w_value, w_gate, w_output, ffn_norm_gain, ffn_norm_shift, w_ffn_gate, w_ffn_up, w_ffn_down):
    params = (attn_norm_gain.astype(jnp.float32), attn_norm_shift.astype(jnp.float32), w_query.astype(jnp.float32), w_key.astype(jnp.float32), w_value.astype(jnp.float32), w_gate.astype(jnp.float32), w_output.astype(jnp.float32), ffn_norm_gain.astype(jnp.float32), ffn_norm_shift.astype(jnp.float32), w_ffn_gate.astype(jnp.float32), w_ffn_up.astype(jnp.float32), w_ffn_down.astype(jnp.float32))
    sequences = TOKENS // SEQ
    token_seqs = tokens.astype(jnp.float32).reshape(sequences, SEQ, D)
    segment_seqs = segments.reshape(sequences, SEQ)
    cot_seqs = cotangent.astype(jnp.float32).reshape(sequences, SEQ, D)

    def per_sequence(running, sliced):
        token_rows, segment_rows, cot_rows = sliced

        def apply_layer(token_in, *weights):
            return forward(token_in, segment_rows, *weights)
        result, pullback = jax.vjp(apply_layer, token_rows, *params)
        gradients = pullback(cot_rows)
        summed = tuple((before + fresh for before, fresh in zip(running, gradients[1:])))
        return (summed, (result.astype(jnp.bfloat16), gradients[0]))
    initial = tuple((jnp.zeros(weight.shape, jnp.float32) for weight in params))
    totals, (outputs, input_grads) = lax.scan(per_sequence, initial, (token_seqs, segment_seqs, cot_seqs))
    return (outputs.reshape(TOKENS, D), input_grads.reshape(TOKENS, D), totals[0], totals[1], totals[2], totals[3], totals[4], totals[5], totals[6], totals[7], totals[8], totals[9], totals[10], totals[11])
```

```python
import jax
import jax.numpy as jnp
from jax import lax
from jax.sharding import PartitionSpec as P

KEY_DIM = 256
VALUE_DIM = 512
F32 = jnp.float32
BF16 = jnp.bfloat16


def layer_norm(values, gain, shift):
    centred = values - jnp.mean(values, -1, keepdims=True)
    spread = jnp.mean(centred * centred, -1, keepdims=True)
    return centred * lax.rsqrt(spread + 1e-05) * gain + shift


def rounded(values):
    return lax.optimization_barrier(values.astype(BF16)).astype(F32)


def matmul(left, right, left_dim=1, right_dim=0):
    return lax.dot_general(
        left, right, (((left_dim,), (right_dim,)), ((), ())), preferred_element_type=F32
    )


def decay_table(offset, row_count, segments, decay_rates):
    seq_len = segments.shape[0]
    row_pos = offset + jnp.arange(row_count, dtype=jnp.int32)
    col_pos = jnp.arange(seq_len, dtype=jnp.int32)
    row_seg = lax.dynamic_slice_in_dim(segments, offset, row_count, 0)
    inside = (row_pos[:, None] >= col_pos[None, :]) & (row_seg[:, None] == segments[None, :])
    distance = jnp.where(inside, row_pos[:, None] - col_pos[None, :], 0).astype(F32)
    return jnp.where(inside[None], jnp.exp(distance[None] * decay_rates[:, None, None]), 0.0)


def gate_mix(retained, gate_pre):
    normal_heads = retained * lax.rsqrt(jnp.mean(retained * retained, -1, keepdims=True) + 1e-06)
    return jax.nn.silu(gate_pre) * normal_heads.reshape(gate_pre.shape)


def gelu_mix(gate_two, up_two):
    return jax.nn.gelu(gate_two, approximate=False) * up_two


def line_streams(block, count):
    from_left, from_right = [block], [block]
    for step in range(1, count):
        from_left.append(
            lax.ppermute(from_left[-1], "tensor", [(i, i + 1) for i in range(step - 1, count - 1)])
        )
        from_right.append(
            lax.ppermute(from_right[-1], "tensor", [(i + 1, i) for i in range(count - step)])
        )
    return from_left, from_right


def line_slots(block, count):
    place = lax.axis_index("tensor")
    from_left, from_right = line_streams(block, count)
    slots = [block]
    for slot in range(1, count):
        chosen = from_right[slot]
        for owner in range(count):
            if owner < count // 2:
                rights = count - 1 - owner
                wanted = from_right[slot] if slot <= rights else from_left[slot - rights]
            else:
                wanted = from_left[slot] if slot <= owner else from_right[slot - owner]
            if wanted is not chosen or owner > 0:
                chosen = jnp.where(place == owner, wanted, chosen)
        slots.append(chosen)
    return slots


def slot_owner(place, slot, count):
    rights = count - 1 - place
    first_half = jnp.where(slot <= rights, place + slot, place - (slot - rights))
    second_half = jnp.where(slot <= place, place - slot, place + (slot - place))
    return jnp.where(place < count // 2, first_half, second_half)


def owner_slot(place, owner, count):
    rights = count - 1 - place
    first_half = jnp.where(owner >= place, owner - place, rights + place - owner)
    second_half = jnp.where(owner <= place, place - owner, owner)
    return jnp.where(place < count // 2, first_half, second_half)


def line_scatter(block_of, count):
    place = lax.axis_index("tensor")
    to_right = to_left = None
    for step in range(1, count):
        ahead = count - step
        right_term = block_of(jnp.minimum(place + ahead, count - 1))
        left_term = block_of(jnp.maximum(place - ahead, 0))
        if to_right is not None:
            right_term = right_term + to_right.astype(F32)
            left_term = left_term + to_left.astype(F32)
        to_right = lax.ppermute(
            right_term.astype(BF16), "tensor", [(i, i + 1) for i in range(step)]
        )
        to_left = lax.ppermute(
            left_term.astype(BF16), "tensor", [(i + 1, i) for i in range(count - 1 - step, count - 1)]
        )
    total = block_of(place)
    if to_right is not None:
        total = total + (to_right.astype(F32) + to_left.astype(F32))
    return total


def sum_everywhere(values, sizes):
    for axis, size in sizes:
        bit = 1
        while bit < size:
            values = values + lax.ppermute(values, axis, [(i, i ^ bit) for i in range(size)])
            bit *= 2
    return values


def body(
    tokens,
    segments,
    cotangent,
    attn_norm_gain,
    attn_norm_shift,
    w_query,
    w_key,
    w_value,
    w_gate,
    w_output,
    ffn_norm_gain,
    ffn_norm_shift,
    w_ffn_gate,
    w_ffn_up,
    w_ffn_down,
):
    seq_len = segments.shape[0]
    rows = tokens.shape[0]
    count = seq_len // rows
    dp_count = lax.axis_size("dp")
    place = lax.axis_index("tensor")
    hk = w_query.shape[1]
    hv = w_value.shape[1]
    ff = w_ffn_gate.shape[1]
    local_heads = hk // KEY_DIM
    block_rows = min(512, seq_len)
    starts = jnp.arange(seq_len // block_rows, dtype=jnp.int32) * block_rows
    head_ids = (place * local_heads + jnp.arange(local_heads, dtype=jnp.int32)).astype(F32)
    decay_rates = jnp.log1p(-jnp.exp2(-5.0 - head_ids))

    residual = tokens.astype(F32)
    normed, first_pull = jax.vjp(layer_norm, residual, attn_norm_gain, attn_norm_shift)
    mixer_full = lax.all_gather(
        jnp.concatenate([w_query, w_key, w_value, w_gate], 1), "dp", axis=0, tiled=True
    )
    output_full = lax.all_gather(w_output.T, "dp", axis=0, tiled=True)
    ffn_full = lax.all_gather(
        jnp.concatenate([w_ffn_gate, w_ffn_up, w_ffn_down.T], 1), "dp", axis=0, tiled=True
    )
    ffn_pair, ffn_down = ffn_full[:, : 2 * ff], ffn_full[:, 2 * ff :]

    normed_slots = line_slots(normed.astype(BF16), count)
    whole_normed = jnp.zeros((count, rows, normed.shape[1]), BF16)
    projected = jnp.zeros((count, rows, 2 * hk + hv), BF16)
    gate_pre = jnp.zeros((count, rows, hv), F32)
    for slot in range(count):
        owner = slot_owner(place, slot, count)
        product = matmul(normed_slots[slot], mixer_full)
        whole_normed = lax.dynamic_update_index_in_dim(whole_normed, normed_slots[slot], owner, 0)
        projected = lax.dynamic_update_index_in_dim(
            projected, product[:, : 2 * hk + hv].astype(BF16), owner, 0
        )
        gate_pre = lax.dynamic_update_index_in_dim(gate_pre, product[:, 2 * hk + hv :], owner, 0)
    whole_normed = whole_normed.reshape(seq_len, -1)
    projected = projected.reshape(seq_len, -1)
    gate_pre = gate_pre.reshape(seq_len, -1)
    query_heads = projected[:, :hk].reshape(seq_len, local_heads, KEY_DIM)
    key_heads = projected[:, hk : 2 * hk].reshape(seq_len, local_heads, KEY_DIM)
    value_heads = projected[:, 2 * hk :].reshape(seq_len, local_heads, VALUE_DIM)

    def block_scores(offset):
        decays = decay_table(offset, block_rows, segments, decay_rates)
        query_block = lax.dynamic_slice_in_dim(query_heads, offset, block_rows, 0)
        scores = jnp.einsum("qhd,shd->hqs", query_block, key_heads, preferred_element_type=F32)
        return (decays, query_block, (scores * decays).astype(BF16))

    def forward_block(offset):
        decays, query_block, weights = block_scores(offset)
        return jnp.einsum("hqs,she->qhe", weights, value_heads, preferred_element_type=F32)

    retained = lax.map(forward_block, starts).reshape(seq_len, local_heads, VALUE_DIM)
    gated_heads, gate_pull = jax.vjp(gate_mix, retained, gate_pre)
    gated_low = gated_heads.astype(BF16)
    mixer_terms = matmul(gated_low, output_full, 1, 1).reshape(count, rows, -1)

    def pick(stacked):
        return lambda index: lax.dynamic_index_in_dim(stacked, index, 0, keepdims=False)

    hidden = residual + line_scatter(pick(mixer_terms), count)
    normed_two, second_pull = jax.vjp(layer_norm, hidden, ffn_norm_gain, ffn_norm_shift)
    two_slots = line_slots(normed_two.astype(BF16), count)
    cot_slots = line_slots(cotangent, count)

    ffn_terms, two_terms, inner_slots, pair_slots = [], [], [], []
    for slot in range(count):
        pair = matmul(two_slots[slot], ffn_pair)
        inner, inner_pull = jax.vjp(gelu_mix, pair[:, :ff], pair[:, ff:])
        inner_low = inner.astype(BF16)
        grad_inner = matmul(cot_slots[slot], ffn_down)
        grad_gate_two, grad_up_two = inner_pull(rounded(grad_inner))
        pair_low = jnp.concatenate([grad_gate_two.astype(BF16), grad_up_two.astype(BF16)], 1)
        two_terms.append(matmul(pair_low, ffn_pair, 1, 1))
        ffn_terms.append(matmul(inner_low, ffn_down, 1, 1))
        inner_slots.append(inner_low)
        pair_slots.append(pair_low)

    def pick_slot(stacked):
        return lambda owner: lax.dynamic_index_in_dim(
            stacked, owner_slot(place, owner, count), 0, keepdims=False
        )

    grad_normed_two = line_scatter(pick_slot(jnp.stack(two_terms)), count)
    grad_from_two, grad_ffn_gain_part, grad_ffn_shift_part = second_pull(grad_normed_two)
    grad_hidden = cotangent.astype(F32) + grad_from_two
    branch_slots = line_slots(grad_hidden.astype(BF16), count)
    layer_output = (hidden + line_scatter(pick_slot(jnp.stack(ffn_terms)), count)).astype(BF16)

    whole_two = jnp.concatenate(two_slots, 0)
    whole_cot = jnp.concatenate(cot_slots, 0)
    ffn_grad_part = jnp.concatenate(
        [
            matmul(whole_two, jnp.concatenate(pair_slots, 0), 0, 0).astype(BF16),
            matmul(whole_cot, jnp.concatenate(inner_slots, 0), 0, 0).astype(BF16),
        ],
        1,
    )
    ffn_grad = lax.psum_scatter(ffn_grad_part, "dp", scatter_dimension=0, tiled=True)

    grad_gated = jnp.zeros((count, rows, hv), BF16)
    whole_branch = jnp.zeros((count, rows, tokens.shape[1]), BF16)
    for slot in range(count):
        owner = slot_owner(place, slot, count)
        whole_branch = lax.dynamic_update_index_in_dim(whole_branch, branch_slots[slot], owner, 0)
        grad_gated = lax.dynamic_update_index_in_dim(
            grad_gated, matmul(branch_slots[slot], output_full).astype(BF16), owner, 0
        )
    whole_branch = whole_branch.reshape(seq_len, -1)
    grad_retained, grad_gate_pre = gate_pull(
        lax.optimization_barrier(grad_gated.reshape(seq_len, -1)).astype(F32)
    )
    retained_low = grad_retained.astype(BF16)
    grad_gate_low = grad_gate_pre.astype(BF16)
    early_grad_part = jnp.concatenate(
        [
            matmul(whole_normed, grad_gate_low, 0, 0).astype(BF16),
            matmul(whole_branch, gated_low, 0, 0).astype(BF16),
        ],
        1,
    )
    early_grad = lax.psum_scatter(early_grad_part, "dp", scatter_dimension=0, tiled=True)

    def backward_block(running, offset):
        key_total, value_total = running
        decays, query_block, weights = block_scores(offset)
        grad_block = lax.dynamic_slice_in_dim(retained_low, offset, block_rows, 0)
        grad_weights = jnp.einsum(
            "qhe,she->hqs", grad_block, value_heads, preferred_element_type=F32
        )
        grad_scores = (grad_weights * decays).astype(BF16)
        grad_query_block = jnp.einsum(
            "hqs,shd->qhd", grad_scores, key_heads, preferred_element_type=F32
        ).astype(BF16)
        key_total = key_total + jnp.einsum(
            "hqs,qhd->shd", grad_scores, query_block, preferred_element_type=F32
        )
        value_total = value_total + jnp.einsum(
            "hqs,qhe->she", weights, grad_block, preferred_element_type=F32
        )
        return ((key_total, value_total), grad_query_block)

    key_start = jnp.zeros((seq_len, local_heads, KEY_DIM), F32)
    value_start = jnp.zeros((seq_len, local_heads, VALUE_DIM), F32)
    (key_total, value_total), query_blocks = lax.scan(
        backward_block, (key_start, value_start), starts
    )
    grad_projected = jnp.concatenate(
        [
            query_blocks.reshape(seq_len, hk),
            key_total.reshape(seq_len, hk).astype(BF16),
            value_total.reshape(seq_len, hv).astype(BF16),
        ],
        1,
    )
    normed_terms = matmul(
        jnp.concatenate([grad_projected, grad_gate_low], 1), mixer_full, 1, 1
    ).reshape(count, rows, -1)
    grad_normed = line_scatter(pick(normed_terms), count)
    late_grad_part = matmul(whole_normed, grad_projected, 0, 0).astype(BF16)
    late_grad = lax.psum_scatter(late_grad_part, "dp", scatter_dimension=0, tiled=True)
    grad_from_one, grad_attn_gain_part, grad_attn_shift_part = first_pull(grad_normed)
    grad_tokens = grad_hidden + grad_from_one

    sizes = (("dp", dp_count), ("tensor", count))
    ffn_gains = sum_everywhere(jnp.stack([grad_ffn_gain_part, grad_ffn_shift_part]), sizes)
    attn_gains = sum_everywhere(jnp.stack([grad_attn_gain_part, grad_attn_shift_part]), sizes)
    late_grad = late_grad.astype(F32)
    early_grad = early_grad.astype(F32)
    ffn_grad = ffn_grad.astype(F32)
    return (
        layer_output,
        grad_tokens,
        attn_gains[0],
        attn_gains[1],
        late_grad[:, :hk],
        late_grad[:, hk : 2 * hk],
        late_grad[:, 2 * hk :],
        early_grad[:, :hv],
        early_grad[:, hv:].T,
        ffn_gains[0],
        ffn_gains[1],
        ffn_grad[:, :ff],
        ffn_grad[:, ff : 2 * ff],
        ffn_grad[:, 2 * ff :].T,
    )


def solution(mesh):
    split = P(("dp", "tensor"), None)
    weight = P("dp", "tensor")
    turned = P("tensor", "dp")
    return jax.shard_map(
        body,
        mesh=mesh,
        in_specs=(
            split, P("dp"), split, P(), P(), weight, weight, weight, weight, turned,
            P(), P(), weight, weight, turned,
        ),
        out_specs=(
            split, split, P(), P(), weight, weight, weight, weight, turned,
            P(), P(), weight, weight, turned,
        ),
        check_vma=False,
    )
```

```python
import functools

import jax
import jax.numpy as jnp
from jax import lax
from jax.experimental import pallas as pl
from jax.experimental.pallas import tpu as pltpu
from jax.sharding import PartitionSpec as P

KEY_DIM = 256
VALUE_DIM = 512
HEAD_COLS = 2 * KEY_DIM + 2 * VALUE_DIM
BLOCK = 256
F32 = jnp.float32
BF16 = jnp.bfloat16
MIB = 1024 * 1024


def layer_norm(values, gain, shift):
    centred = values - jnp.mean(values, -1, keepdims=True)
    spread = jnp.mean(centred * centred, -1, keepdims=True)
    return centred * lax.rsqrt(spread + 1e-05) * gain + shift


def matmul(left, right, left_dim=1, right_dim=0):
    return lax.dot_general(
        left, right, (((left_dim,), (right_dim,)), ((), ())), preferred_element_type=F32
    )


def after(value, *others):
    return lax.optimization_barrier((value, *others))[0]


def kernel_params(mib):
    return pltpu.CompilerParams(vmem_limit_bytes=mib * MIB)


def place_kernel(owner, rows_ref, weight_ref, *refs):
    product_ref, kept_ref = refs[-2:]
    product_ref[...] = matmul(rows_ref[...], weight_ref[...]).astype(product_ref.dtype)

    @pl.when(pl.program_id(0) == 0)
    def _():
        kept_ref[...] = rows_ref[...]


def place_product(rows, weight, owner, count, kind, buffers=None):
    height, depth = rows.shape
    width = weight.shape[1]
    step = min(512, width)
    row_spec = pl.BlockSpec((height, depth), lambda j, at: (0, 0))
    in_specs = [row_spec, pl.BlockSpec((depth, step), lambda j, at: (0, j))]
    operands = [owner.reshape(1), rows, weight]
    aliases = {}
    if buffers is not None:
        operands += list(buffers)
        in_specs += [pl.BlockSpec(memory_space=pl.ANY)] * 2
        aliases = {3: 0, 4: 1}
    return pl.pallas_call(
        place_kernel,
        grid_spec=pltpu.PrefetchScalarGridSpec(
            num_scalar_prefetch=1,
            grid=(width // step,),
            in_specs=in_specs,
            out_specs=[
                pl.BlockSpec((height, step), lambda j, at: (at[0], j)),
                pl.BlockSpec((height, depth), lambda j, at: (at[0], 0)),
            ],
        ),
        out_shape=[
            jax.ShapeDtypeStruct((count * height, width), kind),
            jax.ShapeDtypeStruct((count * height, depth), BF16),
        ],
        input_output_aliases=aliases,
        cost_estimate=pl.CostEstimate(
            flops=2 * height * depth * width,
            bytes_accessed=2 * depth * width + 8 * height * width,
            transcendentals=0,
        ),
        compiler_params=kernel_params(16),
        name="place_product",
    )(*operands)


def back_kernel(owner, rows_ref, weight_ref, out_ref):
    out_ref[...] = matmul(rows_ref[...], weight_ref[...], 1, 1).astype(out_ref.dtype)


def back_product(source, weight, owner, height):
    depth = source.shape[1]
    width = weight.shape[0]
    step = min(512, width)
    return pl.pallas_call(
        back_kernel,
        grid_spec=pltpu.PrefetchScalarGridSpec(
            num_scalar_prefetch=1,
            grid=(width // step,),
            in_specs=[
                pl.BlockSpec((height, depth), lambda j, at: (at[0], 0)),
                pl.BlockSpec((step, depth), lambda j, at: (j, 0)),
            ],
            out_specs=pl.BlockSpec((height, step), lambda j, at: (0, j)),
        ),
        out_shape=jax.ShapeDtypeStruct((height, width), BF16),
        cost_estimate=pl.CostEstimate(
            flops=2 * height * depth * width,
            bytes_accessed=2 * depth * width + 6 * height * width,
            transcendentals=0,
        ),
        compiler_params=kernel_params(16),
        name="back_product",
    )(owner.reshape(1), source, weight)


def decay_block(rate, first, seg_col, seg_row, width):
    height = seg_col.shape[0]
    down = lax.broadcasted_iota(jnp.int32, (height, 1), 0)
    across = lax.broadcasted_iota(jnp.int32, (1, width), 1)
    inside = (down + first >= across) & (seg_col == seg_row)
    factor = jnp.exp(down.astype(F32) * rate) * jnp.exp((first - across).astype(F32) * rate)
    return jnp.where(inside, factor, 0.0)


def retention_kernel(blocks, rates, seg_col, seg_row, query, key, value, gate, gated, retained, keys, values):
    head, at = pl.program_id(0), pl.program_id(1)
    height = query.shape[0]

    @pl.when(at == 0)
    def _():
        keys[...] = key[...].astype(BF16)
        values[...] = value[...].astype(BF16)

    for block in range(blocks):

        @pl.when(at == block)
        def _(block=block):
            width = (block + 1) * height
            decay = decay_block(rates[head], block * height, seg_col[...], seg_row[:, :width], width)
            scores = matmul(query[...].astype(BF16), keys[:width, :], 1, 1)
            mixed = matmul((scores * decay).astype(BF16), values[:width, :])
            retained[...] = mixed
            normal = mixed * lax.rsqrt(jnp.mean(mixed * mixed, -1, keepdims=True) + 1e-06)
            pre = gate[...]
            gated[...] = (pre * jax.nn.sigmoid(pre) * normal).astype(BF16)


def head_specs(seq_len):
    per_head = HEAD_COLS // KEY_DIM
    return [
        pl.BlockSpec(memory_space=pltpu.SMEM),
        pl.BlockSpec((BLOCK, 1), lambda h, i: (i, 0)),
        pl.BlockSpec((1, seq_len), lambda h, i: (0, 0)),
        pl.BlockSpec((BLOCK, KEY_DIM), lambda h, i: (i, per_head * h)),
        pl.BlockSpec((seq_len, KEY_DIM), lambda h, i: (0, per_head * h + 1)),
        pl.BlockSpec((seq_len, VALUE_DIM), lambda h, i: (0, 3 * h + 1)),
        pl.BlockSpec((BLOCK, VALUE_DIM), lambda h, i: (i, 3 * h + 2)),
    ]


def retention(product, segments, rates):
    seq_len = segments.shape[0]
    heads = rates.shape[0]
    blocks = seq_len // BLOCK
    out_spec = pl.BlockSpec((BLOCK, VALUE_DIM), lambda h, i: (i, h))
    return pl.pallas_call(
        functools.partial(retention_kernel, blocks),
        grid=(heads, blocks),
        in_specs=head_specs(seq_len),
        out_specs=[out_spec, out_spec],
        out_shape=[
            jax.ShapeDtypeStruct((seq_len, heads * VALUE_DIM), BF16),
            jax.ShapeDtypeStruct((seq_len, heads * VALUE_DIM), F32),
        ],
        scratch_shapes=[pltpu.VMEM((seq_len, KEY_DIM), BF16), pltpu.VMEM((seq_len, VALUE_DIM), BF16)],
        cost_estimate=pl.CostEstimate(
            flops=2 * heads * seq_len * seq_len * (KEY_DIM + VALUE_DIM),
            bytes_accessed=10 * seq_len * heads * HEAD_COLS,
            transcendentals=0,
        ),
        compiler_params=kernel_params(12 + seq_len // 64),
        name="retention",
    )(rates, segments.reshape(seq_len, 1), segments.reshape(1, seq_len), product, product, product, product)


def retention_back_kernel(
    blocks, rates, seg_col, seg_row, query, key, value, gate, retained, grad_gated, grads, keys, values, key_total, value_total
):
    head, at = pl.program_id(0), pl.program_id(1)
    height = query.shape[0]

    @pl.when(at == 0)
    def _():
        keys[...] = key[...].astype(BF16)
        values[...] = value[...].astype(BF16)
        key_total[...] = jnp.zeros_like(key_total)
        value_total[...] = jnp.zeros_like(value_total)

    for block in range(blocks):

        @pl.when(at == block)
        def _(block=block):
            width = (block + 1) * height
            here = slice(block * height, width)
            mixed = retained[...]
            scale = lax.rsqrt(jnp.mean(mixed * mixed, -1, keepdims=True) + 1e-06)
            normal = mixed * scale
            pre = gate[...]
            grad = grad_gated[...].astype(F32)
            open_part = jax.nn.sigmoid(pre)
            grads[here, 2 * KEY_DIM + VALUE_DIM :] = (
                grad * normal * (open_part * (1.0 + pre * (1.0 - open_part)))
            ).astype(BF16)
            grad_normal = grad * (pre * open_part)
            grad_mixed = (
                scale * (grad_normal - normal * jnp.mean(grad_normal * normal, -1, keepdims=True))
            ).astype(BF16)
            decay = decay_block(rates[head], block * height, seg_col[...], seg_row[:, :width], width)
            query_low = query[...].astype(BF16)
            weights = (matmul(query_low, keys[:width, :], 1, 1) * decay).astype(BF16)
            grad_scores = (matmul(grad_mixed, values[:width, :], 1, 1) * decay).astype(BF16)
            grads[here, :KEY_DIM] = matmul(grad_scores, keys[:width, :]).astype(BF16)
            key_total[:width, :] += matmul(grad_scores, query_low, 0, 0)
            value_total[:width, :] += matmul(weights, grad_mixed, 0, 0)

    @pl.when(at == blocks - 1)
    def _():
        grads[:, KEY_DIM : 2 * KEY_DIM] = key_total[...].astype(BF16)
        grads[:, 2 * KEY_DIM : 2 * KEY_DIM + VALUE_DIM] = value_total[...].astype(BF16)


def retention_back(product, segments, rates, retained, grad_gated):
    seq_len = segments.shape[0]
    heads = rates.shape[0]
    blocks = seq_len // BLOCK
    side_spec = pl.BlockSpec((BLOCK, VALUE_DIM), lambda h, i: (i, h))
    return pl.pallas_call(
        functools.partial(retention_back_kernel, blocks),
        grid=(heads, blocks),
        in_specs=head_specs(seq_len) + [side_spec, side_spec],
        out_specs=pl.BlockSpec((seq_len, HEAD_COLS), lambda h, i: (0, h)),
        out_shape=jax.ShapeDtypeStruct((seq_len, heads * HEAD_COLS), BF16),
        scratch_shapes=[
            pltpu.VMEM((seq_len, KEY_DIM), BF16),
            pltpu.VMEM((seq_len, VALUE_DIM), BF16),
            pltpu.VMEM((seq_len, KEY_DIM), F32),
            pltpu.VMEM((seq_len, VALUE_DIM), F32),
        ],
        cost_estimate=pl.CostEstimate(
            flops=2 * heads * seq_len * seq_len * (3 * KEY_DIM + 2 * VALUE_DIM),
            bytes_accessed=12 * seq_len * heads * HEAD_COLS,
            transcendentals=0,
        ),
        compiler_params=kernel_params(16 + seq_len // 48),
        name="retention_back",
    )(
        rates, segments.reshape(seq_len, 1), segments.reshape(1, seq_len),
        product, product, product, product, retained, grad_gated,
    )


def mlp_kernel(steps, rows, cot, pair_w, down_w, *refs):
    pair_out, inner_out, down_terms, back_terms, down_total, back_total = refs[-6:]
    at = pl.program_id(0)
    half = down_w.shape[1]
    pair = matmul(rows[...], pair_w[...])
    gate, up = pair[:, :half], pair[:, half:]
    grad_inner = matmul(cot[...], down_w[...]).astype(BF16).astype(F32)
    below = 0.5 * (1.0 + lax.erf(gate * (0.5**0.5)))
    slope = below + gate * (jnp.exp(-0.5 * gate * gate) * 0.3989422804014327)
    bent = gate * below
    inner = (bent * up).astype(BF16)
    grad_pair = jnp.concatenate(
        [(grad_inner * up * slope).astype(BF16), (grad_inner * bent).astype(BF16)], 1
    )
    inner_out[...] = inner
    pair_out[...] = grad_pair
    down_part = matmul(inner, down_w[...], 1, 1)
    back_part = matmul(grad_pair, pair_w[...], 1, 1)

    @pl.when(at == 0)
    def _():
        down_total[...] = down_part
        back_total[...] = back_part

    @pl.when(at > 0)
    def _():
        down_total[...] += down_part
        back_total[...] += back_part

    @pl.when(at == steps - 1)
    def _():
        down_terms[...] = down_total[...].astype(down_terms.dtype)
        back_terms[...] = back_total[...].astype(back_terms.dtype)


def mlp_block(rows, cot, weights, slot, count, buffers=None):
    height, depth = rows.shape
    hidden = weights.shape[1] // 3
    step = min(256, hidden)
    steps = hidden // step
    row_spec = pl.BlockSpec((height, depth), lambda j: (0, 0))
    in_specs = [
        row_spec,
        row_spec,
        pl.BlockSpec((depth, 2 * step), lambda j: (0, j)),
        pl.BlockSpec((depth, step), lambda j: (0, 2 * steps + j)),
    ]
    operands = [rows, cot, weights, weights]
    aliases = {}
    if buffers is not None:
        operands += list(buffers)
        in_specs += [pl.BlockSpec(memory_space=pl.ANY)] * 4
        aliases = {4: 0, 5: 1, 6: 2, 7: 3}
    wide_spec = pl.BlockSpec((height, depth), lambda j: (slot, 0))
    return pl.pallas_call(
        functools.partial(mlp_kernel, steps),
        grid=(steps,),
        in_specs=in_specs,
        out_specs=[
            pl.BlockSpec((height, 2 * step), lambda j: (slot, j)),
            pl.BlockSpec((height, step), lambda j: (slot, j)),
            wide_spec,
            wide_spec,
        ],
        out_shape=[
            jax.ShapeDtypeStruct((count * height, 2 * hidden), BF16),
            jax.ShapeDtypeStruct((count * height, hidden), BF16),
            jax.ShapeDtypeStruct((count * height, depth), BF16),
            jax.ShapeDtypeStruct((count * height, depth), BF16),
        ],
        scratch_shapes=[pltpu.VMEM((height, depth), F32)] * 2,
        input_output_aliases=aliases,
        cost_estimate=pl.CostEstimate(
            flops=12 * height * depth * hidden,
            bytes_accessed=6 * depth * hidden + 20 * height * depth,
            transcendentals=0,
        ),
        compiler_params=kernel_params(32),
        name="mlp_block",
    )(*operands)


class Gather:
    def __init__(self, block, count):
        self.count = count
        self.from_left, self.from_right, self.slots = [block], [block], [block]

    def step(self, *ready):
        count, step = self.count, len(self.slots)
        place = lax.axis_index("tensor")
        left, right = self.from_left[-1], self.from_right[-1]
        if ready:
            left, right = lax.optimization_barrier((left, right, *ready))[:2]
        self.from_left.append(
            lax.ppermute(left, "tensor", [(i, i + 1) for i in range(step - 1, count - 1)])
        )
        self.from_right.append(
            lax.ppermute(right, "tensor", [(i + 1, i) for i in range(count - step)])
        )
        chosen = None
        for owner in range(count):
            rights = count - 1 - owner
            if owner < count // 2:
                wanted = self.from_right[step] if step <= rights else self.from_left[step - rights]
            else:
                wanted = self.from_left[step] if step <= owner else self.from_right[step - owner]
            chosen = wanted if chosen is None else jnp.where(place >= owner, wanted, chosen)
        self.slots.append(chosen)
        return self.arrived(step)

    def arrived(self, step):
        return (self.from_left[step], self.from_right[step])


class Scatter:
    def __init__(self, block_of, count):
        self.block_of, self.count, self.steps = block_of, count, 0
        self.to_right = self.to_left = None

    def step(self, *ready):
        count = self.count
        place = lax.axis_index("tensor")
        self.steps += 1
        step = self.steps
        ahead = count - step
        right = self.block_of(jnp.minimum(place + ahead, count - 1), step).astype(F32)
        left = self.block_of(jnp.maximum(place - ahead, 0), step).astype(F32)
        if step > 1:
            right = right + self.to_right.astype(F32)
            left = left + self.to_left.astype(F32)
        right, left = right.astype(BF16), left.astype(BF16)
        if ready:
            right, left = lax.optimization_barrier((right, left, *ready))[:2]
        self.to_right = lax.ppermute(right, "tensor", [(i, i + 1) for i in range(step)])
        self.to_left = lax.ppermute(
            left, "tensor", [(i + 1, i) for i in range(count - 1 - step, count - 1)]
        )
        return (self.to_right, self.to_left)

    def total(self):
        own = self.block_of(lax.axis_index("tensor"), self.count).astype(F32)
        if self.steps:
            own = own + (self.to_right.astype(F32) + self.to_left.astype(F32))
        return own


def slot_owner(place, slot, count):
    rights = count - 1 - place
    first_half = jnp.where(slot <= rights, place + slot, place - (slot - rights))
    second_half = jnp.where(slot <= place, place - slot, slot)
    return jnp.where(place < count // 2, first_half, second_half)


def owner_slot(place, owner, count):
    rights = count - 1 - place
    first_half = jnp.where(owner >= place, owner - place, rights + place - owner)
    second_half = jnp.where(owner <= place, place - owner, owner)
    return jnp.where(place < count // 2, first_half, second_half)


def sum_everywhere(values, sizes):
    for axis, size in sizes:
        bit = 1
        while bit < size:
            values = values + lax.ppermute(values, axis, [(i, i ^ bit) for i in range(size)])
            bit *= 2
    return values


def per_head(parts, heads):
    pieces = []
    for head in range(heads):
        for part in parts:
            size = part.shape[1] // heads
            pieces.append(part[:, head * size : (head + 1) * size])
    return jnp.concatenate(pieces, 1)


def body(
    tokens,
    segments,
    cotangent,
    attn_norm_gain,
    attn_norm_shift,
    w_query,
    w_key,
    w_value,
    w_gate,
    w_output,
    ffn_norm_gain,
    ffn_norm_shift,
    w_ffn_gate,
    w_ffn_up,
    w_ffn_down,
):
    seq_len = segments.shape[0]
    rows = tokens.shape[0]
    count = seq_len // rows
    dp_count = lax.axis_size("dp")
    place = lax.axis_index("tensor")
    hk = w_query.shape[1]
    ff = w_ffn_gate.shape[1]
    heads = hk // KEY_DIM
    mlp_step = min(256, ff)
    mlp_steps = ff // mlp_step
    head_ids = (place * heads + jnp.arange(heads, dtype=jnp.int32)).astype(F32)
    rates = jnp.log1p(-jnp.exp2(-5.0 - head_ids))

    def rows_of(stacked):
        return lambda owner, step: lax.dynamic_slice_in_dim(stacked, owner * rows, rows, 0)

    def slots_of(stacked):
        return lambda owner, step: rows_of(stacked)(owner_slot(place, owner, count), step)

    last = count - 1
    residual = tokens.astype(F32)
    normed, first_pull = jax.vjp(layer_norm, residual, attn_norm_gain, attn_norm_shift)
    mixer_full = lax.all_gather(
        per_head([w_query, w_key, w_value, w_gate], heads), "dp", axis=0, tiled=True
    )
    first = Gather(normed.astype(BF16), count)
    for step in range(1, count):
        first.step()
    output_full = lax.all_gather(
        after(w_output.T, *first.arrived(min(2, last))), "dp", axis=0, tiled=True
    )
    ffn_full = lax.all_gather(
        after(
            jnp.concatenate([per_head([w_ffn_gate, w_ffn_up], mlp_steps), w_ffn_down.T], 1),
            *first.arrived(last),
        ),
        "dp",
        axis=0,
        tiled=True,
    )

    buffers = None
    for slot in range(count):
        block = first.slots[slot]
        if slot == last and buffers is not None:
            block = after(block, *buffers)
        buffers = place_product(
            block, mixer_full, slot_owner(place, slot, count), count, F32, buffers
        )
    product, whole_normed = buffers

    cots = Gather(cotangent, count)
    cots.step(*first.arrived(last))
    gated_low, retained = retention(product, segments, rates)
    mixer = Scatter(rows_of(matmul(gated_low, output_full, 1, 1).astype(BF16)), count)
    for step in range(1, count):
        mixer.step(*cots.arrived(step))
        if step < last:
            cots.step()
    hidden = residual + mixer.total()
    normed_two, second_pull = jax.vjp(layer_norm, hidden, ffn_norm_gain, ffn_norm_shift)

    second = Gather(normed_two.astype(BF16), count)
    buffers = None
    for slot in range(count):
        block = second.slots[slot]
        if slot < last:
            second.step(*([] if slot == 0 else buffers))
        elif buffers is not None:
            block = after(block, *buffers)
        buffers = mlp_block(block, cots.slots[slot], ffn_full, slot, count, buffers)
    grad_pairs, inner, down_terms, back_terms = buffers

    back = Scatter(slots_of(back_terms), count)
    started = back.step()
    pair_part = matmul(
        after(jnp.concatenate(second.slots, 0), *started), grad_pairs, 0, 0
    ).astype(BF16)
    down_part = matmul(
        after(jnp.concatenate(cots.slots, 0), *started), inner, 0, 0
    ).astype(BF16)
    pair_grad = lax.psum_scatter(pair_part, "dp", scatter_dimension=0, tiled=True)
    down_grad = lax.psum_scatter(down_part, "dp", scatter_dimension=0, tiled=True)
    for step in range(2, count):
        back.step(*([pair_part, down_part] if step == last else []))
    grad_from_two, grad_ffn_gain_part, grad_ffn_shift_part = second_pull(back.total())
    grad_hidden = cotangent.astype(F32) + grad_from_two

    branch = Gather(grad_hidden.astype(BF16), count)
    down = Scatter(slots_of(down_terms), count)
    buffers = None
    for slot in range(count):
        block = branch.slots[slot]
        if slot < last:
            arrived = branch.step(*([] if slot == 0 else buffers))
            if slot + 1 < last:
                down_sent = down.step(*arrived)
        elif buffers is not None:
            block = after(block, *buffers)
        buffers = place_product(
            block, output_full, slot_owner(place, slot, count), count, BF16, buffers
        )
    grad_gated, whole_branch = buffers
    down_sent = down.step(grad_gated)
    layer_output = (hidden + down.total()).astype(BF16)
    output_part = matmul(whole_branch, gated_low, 0, 0).astype(BF16)
    output_grad = lax.psum_scatter(output_part, "dp", scatter_dimension=0, tiled=True)
    grads = retention_back(product, segments, rates, retained, after(grad_gated, output_part))

    normed_terms = []

    def far_of(owner, step):
        index = count - 1 - owner_slot(place, owner, count)
        chosen = normed_terms[0]
        for other in range(1, step):
            chosen = jnp.where(index >= other, normed_terms[other], chosen)
        return chosen

    last_scatter = Scatter(far_of, count)
    source = after(grads, *down_sent)
    mixer_part = None
    for index in range(count):
        normed_terms.append(
            back_product(source, mixer_full, slot_owner(place, count - 1 - index, count), rows)
        )
        if index == 0:
            mixer_part = matmul(whole_normed, after(grads, normed_terms[0]), 0, 0).astype(BF16)
            source = after(source, mixer_part)
        if index < last:
            last_scatter.step()
    mixer_grad = lax.psum_scatter(mixer_part, "dp", scatter_dimension=0, tiled=True)
    grad_from_one, grad_attn_gain_part, grad_attn_shift_part = first_pull(last_scatter.total())
    grad_tokens = grad_hidden + grad_from_one

    gains = sum_everywhere(
        jnp.stack(
            [grad_attn_gain_part, grad_attn_shift_part, grad_ffn_gain_part, grad_ffn_shift_part]
        ),
        (("dp", dp_count), ("tensor", count)),
    )

    def columns(grad, groups, first, size):
        stride = grad.shape[1] // groups
        parts = [grad[:, g * stride + first : g * stride + first + size] for g in range(groups)]
        return jnp.concatenate(parts, 1).astype(F32)

    return (
        layer_output,
        grad_tokens,
        gains[0],
        gains[1],
        columns(mixer_grad, heads, 0, KEY_DIM),
        columns(mixer_grad, heads, KEY_DIM, KEY_DIM),
        columns(mixer_grad, heads, 2 * KEY_DIM, VALUE_DIM),
        columns(mixer_grad, heads, 2 * KEY_DIM + VALUE_DIM, VALUE_DIM),
        output_grad.astype(F32).T,
        gains[2],
        gains[3],
        columns(pair_grad, mlp_steps, 0, mlp_step),
        columns(pair_grad, mlp_steps, mlp_step, mlp_step),
        down_grad.astype(F32).T,
    )


def solution(mesh):
    split = P(("dp", "tensor"), None)
    weight = P("dp", "tensor")
    turned = P("tensor", "dp")
    return jax.shard_map(
        body,
        mesh=mesh,
        in_specs=(
            split, P("dp"), split, P(), P(), weight, weight, weight, weight, turned,
            P(), P(), weight, weight, turned,
        ),
        out_specs=(
            split, split, P(), P(), weight, weight, weight, weight, turned,
            P(), P(), weight, weight, turned,
        ),
        check_vma=False,
    )
```

```python
import functools

import jax
import jax.numpy as jnp
from jax import lax
from jax.experimental import pallas as pl
from jax.experimental.pallas import tpu as pltpu
from jax.sharding import PartitionSpec as P

KEY_DIM = 256
VALUE_DIM = 512
HEAD_COLS = 2 * KEY_DIM + 2 * VALUE_DIM
BLOCK = 256
F32 = jnp.float32
BF16 = jnp.bfloat16
MIB = 1024 * 1024


def layer_norm(values, gain, shift):
    centred = values - jnp.mean(values, -1, keepdims=True)
    spread = jnp.mean(centred * centred, -1, keepdims=True)
    return centred * lax.rsqrt(spread + 1e-05) * gain + shift


def matmul(left, right, left_dim=1, right_dim=0):
    return lax.dot_general(
        left, right, (((left_dim,), (right_dim,)), ((), ())), preferred_element_type=F32
    )


def after(value, *others):
    return lax.optimization_barrier((value, *others))[0]


def kernel_params(mib):
    return pltpu.CompilerParams(vmem_limit_bytes=mib * MIB)


def place_kernel(owner, rows_ref, weight_ref, *refs):
    product_ref, kept_ref = refs[-2:]
    product_ref[...] = matmul(rows_ref[...], weight_ref[...]).astype(product_ref.dtype)

    @pl.when(pl.program_id(0) == 0)
    def _():
        kept_ref[...] = rows_ref[...]


def place_product(rows, weight, owner, count, kind, buffers=()):
    height, depth = rows.shape
    width = weight.shape[1]
    step = min(512, width)
    row_spec = pl.BlockSpec((height, depth), lambda j, at: (0, 0))
    in_specs = [row_spec, pl.BlockSpec((depth, step), lambda j, at: (0, j))]
    operands = [owner.reshape(1), rows, weight]
    aliases = {}
    if buffers:
        operands += list(buffers)
        in_specs += [pl.BlockSpec(memory_space=pl.ANY)] * 2
        aliases = {3: 0, 4: 1}
    return pl.pallas_call(
        place_kernel,
        grid_spec=pltpu.PrefetchScalarGridSpec(
            num_scalar_prefetch=1,
            grid=(width // step,),
            in_specs=in_specs,
            out_specs=[
                pl.BlockSpec((height, step), lambda j, at: (at[0], j)),
                pl.BlockSpec((height, depth), lambda j, at: (at[0], 0)),
            ],
        ),
        out_shape=[
            jax.ShapeDtypeStruct((count * height, width), kind),
            jax.ShapeDtypeStruct((count * height, depth), BF16),
        ],
        input_output_aliases=aliases,
        cost_estimate=pl.CostEstimate(
            flops=2 * height * depth * width,
            bytes_accessed=2 * depth * width + 8 * height * width,
            transcendentals=0,
        ),
        compiler_params=kernel_params(44),
        name="place_product",
    )(*operands)


def back_kernel(owner, rows_ref, weight_ref, out_ref):
    out_ref[...] = matmul(rows_ref[...], weight_ref[...], 1, 1).astype(out_ref.dtype)


def back_product(source, weight, owner, height):
    depth = source.shape[1]
    width = weight.shape[0]
    step = min(512, width)
    return pl.pallas_call(
        back_kernel,
        grid_spec=pltpu.PrefetchScalarGridSpec(
            num_scalar_prefetch=1,
            grid=(width // step,),
            in_specs=[
                pl.BlockSpec((height, depth), lambda j, at: (at[0], 0)),
                pl.BlockSpec((step, depth), lambda j, at: (j, 0)),
            ],
            out_specs=pl.BlockSpec((height, step), lambda j, at: (0, j)),
        ),
        out_shape=jax.ShapeDtypeStruct((height, width), BF16),
        cost_estimate=pl.CostEstimate(
            flops=2 * height * depth * width,
            bytes_accessed=2 * depth * width + 6 * height * width,
            transcendentals=0,
        ),
        compiler_params=kernel_params(16),
        name="back_product",
    )(owner.reshape(1), source, weight)


def decay_block(rate, first, seg_col, seg_row, width):
    height = seg_col.shape[0]
    down = lax.broadcasted_iota(jnp.int32, (height, 1), 0)
    across = lax.broadcasted_iota(jnp.int32, (1, width), 1)
    inside = (down + first >= across) & (seg_col == seg_row)
    factor = jnp.exp(down.astype(F32) * rate) * jnp.exp((first - across).astype(F32) * rate)
    return jnp.where(inside, factor, 0.0)


def retention_kernel(blocks, rates, seg_col, seg_row, query, key, value, gate, gated, retained, keys, values):
    head, at = pl.program_id(0), pl.program_id(1)
    height = query.shape[0]

    @pl.when(at == 0)
    def _():
        keys[...] = key[...].astype(BF16)
        values[...] = value[...].astype(BF16)

    for block in range(blocks):

        @pl.when(at == block)
        def _(block=block):
            width = (block + 1) * height
            decay = decay_block(rates[head], block * height, seg_col[...], seg_row[:, :width], width)
            scores = matmul(query[...].astype(BF16), keys[:width, :], 1, 1)
            mixed = matmul((scores * decay).astype(BF16), values[:width, :])
            retained[...] = mixed
            normal = mixed * lax.rsqrt(jnp.mean(mixed * mixed, -1, keepdims=True) + 1e-06)
            pre = gate[...]
            gated[...] = (pre * jax.nn.sigmoid(pre) * normal).astype(BF16)


def head_specs(seq_len):
    per_head = HEAD_COLS // KEY_DIM
    return [
        pl.BlockSpec(memory_space=pltpu.SMEM),
        pl.BlockSpec((BLOCK, 1), lambda h, i: (i, 0)),
        pl.BlockSpec((1, seq_len), lambda h, i: (0, 0)),
        pl.BlockSpec((BLOCK, KEY_DIM), lambda h, i: (i, per_head * h)),
        pl.BlockSpec((seq_len, KEY_DIM), lambda h, i: (0, per_head * h + 1)),
        pl.BlockSpec((seq_len, VALUE_DIM), lambda h, i: (0, 3 * h + 1)),
        pl.BlockSpec((BLOCK, VALUE_DIM), lambda h, i: (i, 3 * h + 2)),
    ]


def retention(product, segments, rates):
    seq_len = segments.shape[0]
    heads = rates.shape[0]
    blocks = seq_len // BLOCK
    out_spec = pl.BlockSpec((BLOCK, VALUE_DIM), lambda h, i: (i, h))
    return pl.pallas_call(
        functools.partial(retention_kernel, blocks),
        grid=(heads, blocks),
        in_specs=head_specs(seq_len),
        out_specs=[out_spec, out_spec],
        out_shape=[
            jax.ShapeDtypeStruct((seq_len, heads * VALUE_DIM), BF16),
            jax.ShapeDtypeStruct((seq_len, heads * VALUE_DIM), F32),
        ],
        scratch_shapes=[pltpu.VMEM((seq_len, KEY_DIM), BF16), pltpu.VMEM((seq_len, VALUE_DIM), BF16)],
        cost_estimate=pl.CostEstimate(
            flops=2 * heads * seq_len * seq_len * (KEY_DIM + VALUE_DIM),
            bytes_accessed=10 * seq_len * heads * HEAD_COLS,
            transcendentals=0,
        ),
        compiler_params=kernel_params(12 + seq_len // 64),
        name="retention",
    )(rates, segments.reshape(seq_len, 1), segments.reshape(1, seq_len), product, product, product, product)


def retention_back_kernel(
    blocks, rates, seg_col, seg_row, query, key, value, gate, retained, grad_gated, grads, keys, values, key_total, value_total
):
    head, at = pl.program_id(0), pl.program_id(1)
    height = query.shape[0]

    @pl.when(at == 0)
    def _():
        keys[...] = key[...].astype(BF16)
        values[...] = value[...].astype(BF16)
        key_total[...] = jnp.zeros_like(key_total)
        value_total[...] = jnp.zeros_like(value_total)

    for block in range(blocks):

        @pl.when(at == block)
        def _(block=block):
            width = (block + 1) * height
            here = slice(block * height, width)
            mixed = retained[...]
            scale = lax.rsqrt(jnp.mean(mixed * mixed, -1, keepdims=True) + 1e-06)
            normal = mixed * scale
            pre = gate[...]
            grad = grad_gated[...].astype(F32)
            open_part = jax.nn.sigmoid(pre)
            grads[here, 2 * KEY_DIM + VALUE_DIM :] = (
                grad * normal * (open_part * (1.0 + pre * (1.0 - open_part)))
            ).astype(BF16)
            grad_normal = grad * (pre * open_part)
            grad_mixed = (
                scale * (grad_normal - normal * jnp.mean(grad_normal * normal, -1, keepdims=True))
            ).astype(BF16)
            decay = decay_block(rates[head], block * height, seg_col[...], seg_row[:, :width], width)
            query_low = query[...].astype(BF16)
            weights = (matmul(query_low, keys[:width, :], 1, 1) * decay).astype(BF16)
            grad_scores = (matmul(grad_mixed, values[:width, :], 1, 1) * decay).astype(BF16)
            grads[here, :KEY_DIM] = matmul(grad_scores, keys[:width, :]).astype(BF16)
            key_total[:width, :] += matmul(grad_scores, query_low, 0, 0)
            value_total[:width, :] += matmul(weights, grad_mixed, 0, 0)

    @pl.when(at == blocks - 1)
    def _():
        grads[:, KEY_DIM : 2 * KEY_DIM] = key_total[...].astype(BF16)
        grads[:, 2 * KEY_DIM : 2 * KEY_DIM + VALUE_DIM] = value_total[...].astype(BF16)


def retention_back(product, segments, rates, retained, grad_gated):
    seq_len = segments.shape[0]
    heads = rates.shape[0]
    blocks = seq_len // BLOCK
    side_spec = pl.BlockSpec((BLOCK, VALUE_DIM), lambda h, i: (i, h))
    return pl.pallas_call(
        functools.partial(retention_back_kernel, blocks),
        grid=(heads, blocks),
        in_specs=head_specs(seq_len) + [side_spec, side_spec],
        out_specs=pl.BlockSpec((seq_len, HEAD_COLS), lambda h, i: (0, h)),
        out_shape=jax.ShapeDtypeStruct((seq_len, heads * HEAD_COLS), BF16),
        scratch_shapes=[
            pltpu.VMEM((seq_len, KEY_DIM), BF16),
            pltpu.VMEM((seq_len, VALUE_DIM), BF16),
            pltpu.VMEM((seq_len, KEY_DIM), F32),
            pltpu.VMEM((seq_len, VALUE_DIM), F32),
        ],
        cost_estimate=pl.CostEstimate(
            flops=2 * heads * seq_len * seq_len * (3 * KEY_DIM + 2 * VALUE_DIM),
            bytes_accessed=12 * seq_len * heads * HEAD_COLS,
            transcendentals=0,
        ),
        compiler_params=kernel_params(16 + seq_len // 48),
        name="retention_back",
    )(
        rates, segments.reshape(seq_len, 1), segments.reshape(1, seq_len),
        product, product, product, product, retained, grad_gated,
    )


def mlp_kernel(steps, rows, cot, pair_w, down_w, *refs):
    pair_out, inner_out, down_terms, back_terms, down_total, back_total = refs[-6:]
    at = pl.program_id(0)
    half = down_w.shape[1]
    pair = matmul(rows[...], pair_w[...])
    gate, up = pair[:, :half], pair[:, half:]
    grad_inner = matmul(cot[...], down_w[...]).astype(BF16).astype(F32)
    below = 0.5 * (1.0 + lax.erf(gate * (0.5**0.5)))
    slope = below + gate * (jnp.exp(-0.5 * gate * gate) * 0.3989422804014327)
    bent = gate * below
    inner = (bent * up).astype(BF16)
    grad_pair = jnp.concatenate(
        [(grad_inner * up * slope).astype(BF16), (grad_inner * bent).astype(BF16)], 1
    )
    inner_out[...] = inner
    pair_out[...] = grad_pair
    down_part = matmul(inner, down_w[...], 1, 1)
    back_part = matmul(grad_pair, pair_w[...], 1, 1)

    @pl.when(at == 0)
    def _():
        down_total[...] = down_part
        back_total[...] = back_part

    @pl.when(at > 0)
    def _():
        down_total[...] += down_part
        back_total[...] += back_part

    @pl.when(at == steps - 1)
    def _():
        down_terms[...] = down_total[...].astype(down_terms.dtype)
        back_terms[...] = back_total[...].astype(back_terms.dtype)


def mlp_block(rows, cot, weights, slot, count, buffers=()):
    height, depth = rows.shape
    hidden = weights.shape[1] // 3
    step = min(256, hidden)
    steps = hidden // step
    row_spec = pl.BlockSpec((height, depth), lambda j: (0, 0))
    in_specs = [
        row_spec,
        row_spec,
        pl.BlockSpec((depth, 2 * step), lambda j: (0, j)),
        pl.BlockSpec((depth, step), lambda j: (0, 2 * steps + j)),
    ]
    operands = [rows, cot, weights, weights]
    aliases = {}
    if buffers:
        operands += list(buffers)
        in_specs += [pl.BlockSpec(memory_space=pl.ANY)] * 4
        aliases = {4: 0, 5: 1, 6: 2, 7: 3}
    wide_spec = pl.BlockSpec((height, depth), lambda j: (slot, 0))
    return pl.pallas_call(
        functools.partial(mlp_kernel, steps),
        grid=(steps,),
        in_specs=in_specs,
        out_specs=[
            pl.BlockSpec((height, 2 * step), lambda j: (slot, j)),
            pl.BlockSpec((height, step), lambda j: (slot, j)),
            wide_spec,
            wide_spec,
        ],
        out_shape=[
            jax.ShapeDtypeStruct((count * height, 2 * hidden), BF16),
            jax.ShapeDtypeStruct((count * height, hidden), BF16),
            jax.ShapeDtypeStruct((count * height, depth), BF16),
            jax.ShapeDtypeStruct((count * height, depth), BF16),
        ],
        scratch_shapes=[pltpu.VMEM((height, depth), F32)] * 2,
        input_output_aliases=aliases,
        cost_estimate=pl.CostEstimate(
            flops=12 * height * depth * hidden,
            bytes_accessed=6 * depth * hidden + 20 * height * depth,
            transcendentals=0,
        ),
        compiler_params=kernel_params(46),
        name="mlp_block",
    )(*operands)


class Gather:
    def __init__(self, block, count):
        self.count = count
        self.from_left, self.from_right, self.slots = [block], [block], [block]

    def step(self, *ready):
        count, step = self.count, len(self.slots)
        place = lax.axis_index("tensor")
        left, right = self.from_left[-1], self.from_right[-1]
        if ready:
            left, right = lax.optimization_barrier((left, right, *ready))[:2]
        self.from_left.append(
            lax.ppermute(left, "tensor", [(i, i + 1) for i in range(step - 1, count - 1)])
        )
        self.from_right.append(
            lax.ppermute(right, "tensor", [(i + 1, i) for i in range(count - step)])
        )
        chosen = None
        for owner in range(count):
            rights = count - 1 - owner
            if owner < count // 2:
                wanted = self.from_right[step] if step <= rights else self.from_left[step - rights]
            else:
                wanted = self.from_left[step] if step <= owner else self.from_right[step - owner]
            chosen = wanted if chosen is None else jnp.where(place >= owner, wanted, chosen)
        self.slots.append(chosen)
        return self.arrived(step)

    def arrived(self, step):
        return (self.from_left[step], self.from_right[step])


class Scatter:
    def __init__(self, block_of, count):
        self.block_of, self.count, self.steps = block_of, count, 0
        self.to_right = self.to_left = None

    def step(self, *ready):
        count = self.count
        place = lax.axis_index("tensor")
        self.steps += 1
        step = self.steps
        ahead = count - step
        right = self.block_of(jnp.minimum(place + ahead, count - 1), step).astype(F32)
        left = self.block_of(jnp.maximum(place - ahead, 0), step).astype(F32)
        if step > 1:
            right = right + self.to_right.astype(F32)
            left = left + self.to_left.astype(F32)
        right, left = right.astype(BF16), left.astype(BF16)
        if ready:
            right, left = lax.optimization_barrier((right, left, *ready))[:2]
        self.to_right = lax.ppermute(right, "tensor", [(i, i + 1) for i in range(step)])
        self.to_left = lax.ppermute(
            left, "tensor", [(i + 1, i) for i in range(count - 1 - step, count - 1)]
        )
        return (self.to_right, self.to_left)

    def total(self):
        own = self.block_of(lax.axis_index("tensor"), self.count).astype(F32)
        if self.steps:
            own = own + (self.to_right.astype(F32) + self.to_left.astype(F32))
        return own


def slot_owner(place, slot, count):
    rights = count - 1 - place
    first_half = jnp.where(slot <= rights, place + slot, place - (slot - rights))
    second_half = jnp.where(slot <= place, place - slot, slot)
    return jnp.where(place < count // 2, first_half, second_half)


def owner_slot(place, owner, count):
    rights = count - 1 - place
    first_half = jnp.where(owner >= place, owner - place, rights + place - owner)
    second_half = jnp.where(owner <= place, place - owner, owner)
    return jnp.where(place < count // 2, first_half, second_half)


def dp_scatter(part):
    return lax.psum_scatter(part, "dp", scatter_dimension=0, tiled=True)


def sum_everywhere(values, sizes):
    for axis, size in sizes:
        bit = 1
        while bit < size:
            values = values + lax.ppermute(values, axis, [(i, i ^ bit) for i in range(size)])
            bit *= 2
    return values


def per_head(parts, heads):
    pieces = []
    for head in range(heads):
        for part in parts:
            size = part.shape[1] // heads
            pieces.append(part[:, head * size : (head + 1) * size])
    return jnp.concatenate(pieces, 1)


def body(
    tokens,
    segments,
    cotangent,
    attn_norm_gain,
    attn_norm_shift,
    w_query,
    w_key,
    w_value,
    w_gate,
    w_output,
    ffn_norm_gain,
    ffn_norm_shift,
    w_ffn_gate,
    w_ffn_up,
    w_ffn_down,
):
    seq_len = segments.shape[0]
    rows = tokens.shape[0]
    count = seq_len // rows
    dp_count = lax.axis_size("dp")
    place = lax.axis_index("tensor")
    hk = w_query.shape[1]
    ff = w_ffn_gate.shape[1]
    heads = hk // KEY_DIM
    mlp_step = min(256, ff)
    mlp_steps = ff // mlp_step
    head_ids = (place * heads + jnp.arange(heads, dtype=jnp.int32)).astype(F32)
    rates = jnp.log1p(-jnp.exp2(-5.0 - head_ids))

    def rows_of(stacked):
        return lambda owner, step: lax.dynamic_slice_in_dim(stacked, owner * rows, rows, 0)

    def slots_of(stacked):
        return lambda owner, step: rows_of(stacked)(owner_slot(place, owner, count), step)

    last = count - 1
    residual = tokens.astype(F32)
    normed, first_pull = jax.vjp(layer_norm, residual, attn_norm_gain, attn_norm_shift)
    mixer_full = lax.all_gather(
        per_head([w_query, w_key, w_value, w_gate], heads), "dp", axis=0, tiled=True
    )
    first = Gather(normed.astype(BF16), count)
    for step in range(1, count):
        first.step()
    output_full = lax.all_gather(
        after(w_output.T, *first.arrived(min(2, last))), "dp", axis=0, tiled=True
    )
    ffn_full = lax.all_gather(
        after(
            jnp.concatenate([per_head([w_ffn_gate, w_ffn_up], mlp_steps), w_ffn_down.T], 1),
            *first.arrived(last),
        ),
        "dp",
        axis=0,
        tiled=True,
    )

    buffers = ()
    for slot in range(count):
        block = first.slots[slot]
        earlier = buffers
        if slot == last:
            block = after(block, *earlier)
        buffers = place_product(
            block, mixer_full, slot_owner(place, slot, count), count, F32, buffers
        )
    product, whole_normed = buffers

    cots = Gather(cotangent, count)
    cots.step(*first.arrived(last), *earlier)
    gated_low, retained = retention(product, segments, rates)
    mixer = Scatter(rows_of(matmul(gated_low, output_full, 1, 1).astype(BF16)), count)
    for step in range(1, count):
        mixer.step(*cots.arrived(step))
        if step < last:
            cots.step()
    hidden = residual + mixer.total()
    normed_two, second_pull = jax.vjp(layer_norm, hidden, ffn_norm_gain, ffn_norm_shift)

    second = Gather(normed_two.astype(BF16), count)
    buffers = ()
    for slot in range(count):
        block = second.slots[slot]
        if slot < last:
            second.step(*buffers)
        else:
            block = after(block, *buffers)
        buffers = mlp_block(block, cots.slots[slot], ffn_full, slot, count, buffers)
    grad_pairs, inner, down_terms, back_terms = buffers

    back = Scatter(slots_of(back_terms), count)
    started = back.step()
    pair_part = matmul(jnp.concatenate(second.slots, 0), grad_pairs, 0, 0).astype(BF16)
    down_part = matmul(
        after(jnp.concatenate(cots.slots, 0), pair_part), inner, 0, 0
    ).astype(BF16)
    pair_grad = dp_scatter(after(pair_part, *started))
    down_grad = dp_scatter(after(down_part, *started))
    for step in range(2, count):
        back.step()
    grad_from_two, grad_ffn_gain_part, grad_ffn_shift_part = second_pull(back.total())
    grad_hidden = cotangent.astype(F32) + grad_from_two

    branch = Gather(grad_hidden.astype(BF16), count)
    down = Scatter(slots_of(down_terms), count)
    buffers, sent = (), ()
    for slot in range(count):
        block = branch.slots[slot]
        if slot < last:
            branch.step(*buffers, *sent)
            sent = down.step(*branch.arrived(slot)) if slot > 0 else ()
        else:
            block = after(block, *buffers, *sent)
        buffers = place_product(
            block, output_full, slot_owner(place, slot, count), count, BF16, buffers
        )
    grad_gated, whole_branch = buffers
    output_part = matmul(whole_branch, gated_low, 0, 0).astype(BF16)
    output_grad = dp_scatter(output_part)
    grads = retention_back(product, segments, rates, retained, after(grad_gated, output_part))
    sent = down.step()
    layer_output = (hidden + down.total()).astype(BF16)

    normed_terms = []

    def far_of(owner, step):
        index = count - 1 - owner_slot(place, owner, count)
        chosen = normed_terms[0]
        for other in range(1, step):
            chosen = jnp.where(index >= other, normed_terms[other], chosen)
        return chosen

    last_scatter = Scatter(far_of, count)
    source = after(grads, *sent)
    mixer_part = None
    for index in range(count):
        normed_terms.append(
            back_product(source, mixer_full, slot_owner(place, count - 1 - index, count), rows)
        )
        if index == 0:
            mixer_part = matmul(whole_normed, after(grads, normed_terms[0]), 0, 0).astype(BF16)
            source = after(source, mixer_part)
        if index < last:
            sent = last_scatter.step()
        if index == 0:
            mixer_grad = dp_scatter(after(mixer_part, *sent))
    grad_from_one, grad_attn_gain_part, grad_attn_shift_part = first_pull(last_scatter.total())
    grad_tokens = grad_hidden + grad_from_one

    gains = sum_everywhere(
        jnp.stack(
            [grad_attn_gain_part, grad_attn_shift_part, grad_ffn_gain_part, grad_ffn_shift_part]
        ),
        (("dp", dp_count), ("tensor", count)),
    )

    def columns(grad, groups, first, size):
        stride = grad.shape[1] // groups
        parts = [grad[:, g * stride + first : g * stride + first + size] for g in range(groups)]
        return jnp.concatenate(parts, 1).astype(F32)

    return (
        layer_output,
        grad_tokens,
        gains[0],
        gains[1],
        columns(mixer_grad, heads, 0, KEY_DIM),
        columns(mixer_grad, heads, KEY_DIM, KEY_DIM),
        columns(mixer_grad, heads, 2 * KEY_DIM, VALUE_DIM),
        columns(mixer_grad, heads, 2 * KEY_DIM + VALUE_DIM, VALUE_DIM),
        output_grad.astype(F32).T,
        gains[2],
        gains[3],
        columns(pair_grad, mlp_steps, 0, mlp_step),
        columns(pair_grad, mlp_steps, mlp_step, mlp_step),
        down_grad.astype(F32).T,
    )


def solution(mesh):
    split = P(("dp", "tensor"), None)
    weight = P("dp", "tensor")
    turned = P("tensor", "dp")
    return jax.shard_map(
        body,
        mesh=mesh,
        in_specs=(
            split, P("dp"), split, P(), P(), weight, weight, weight, weight, turned,
            P(), P(), weight, weight, turned,
        ),
        out_specs=(
            split, split, P(), P(), weight, weight, weight, weight, turned,
            P(), P(), weight, weight, turned,
        ),
        check_vma=False,
    )
```

```python
import functools

import jax
import jax.numpy as jnp
from jax import lax
from jax.experimental import pallas as pl
from jax.experimental.pallas import tpu as pltpu
from jax.sharding import PartitionSpec as P

KEY_DIM = 256
VALUE_DIM = 512
HEAD_COLS = 2 * KEY_DIM + 2 * VALUE_DIM
BLOCK = 256
F32 = jnp.float32
BF16 = jnp.bfloat16
MIB = 1024 * 1024


def layer_norm(values, gain, shift):
    centred = values - jnp.mean(values, -1, keepdims=True)
    spread = jnp.mean(centred * centred, -1, keepdims=True)
    return centred * lax.rsqrt(spread + 1e-05) * gain + shift


def matmul(left, right, left_dim=1, right_dim=0):
    return lax.dot_general(
        left, right, (((left_dim,), (right_dim,)), ((), ())), preferred_element_type=F32
    )


def after(value, *others):
    return lax.optimization_barrier((value, *others))[0]


def kernel_params(mib):
    return pltpu.CompilerParams(vmem_limit_bytes=mib * MIB)


def place_kernel(owner, rows_ref, weight_ref, *refs):
    product_ref, kept_ref = refs[-2:]
    product_ref[...] = matmul(rows_ref[...], weight_ref[...]).astype(product_ref.dtype)

    @pl.when(pl.program_id(0) == 0)
    def _():
        kept_ref[...] = rows_ref[...]


def place_product(rows, weight, owner, count, kind, buffers=()):
    height, depth = rows.shape
    width = weight.shape[1]
    step = min(512, width)
    row_spec = pl.BlockSpec((height, depth), lambda j, at: (0, 0))
    in_specs = [row_spec, pl.BlockSpec((depth, step), lambda j, at: (0, j))]
    operands = [owner.reshape(1), rows, weight]
    aliases = {}
    if buffers:
        operands += list(buffers)
        in_specs += [pl.BlockSpec(memory_space=pl.ANY)] * 2
        aliases = {3: 0, 4: 1}
    return pl.pallas_call(
        place_kernel,
        grid_spec=pltpu.PrefetchScalarGridSpec(
            num_scalar_prefetch=1,
            grid=(width // step,),
            in_specs=in_specs,
            out_specs=[
                pl.BlockSpec((height, step), lambda j, at: (at[0], j)),
                pl.BlockSpec((height, depth), lambda j, at: (at[0], 0)),
            ],
        ),
        out_shape=[
            jax.ShapeDtypeStruct((count * height, width), kind),
            jax.ShapeDtypeStruct((count * height, depth), BF16),
        ],
        input_output_aliases=aliases,
        cost_estimate=pl.CostEstimate(
            flops=2 * height * depth * width,
            bytes_accessed=2 * depth * width + 8 * height * width,
            transcendentals=0,
        ),
        compiler_params=kernel_params(12),
        name="place_product",
    )(*operands)


def project_kernel(owners, *refs):
    count = len(refs) - 3
    weight_ref, product_ref, kept_ref = refs[count:]
    height = refs[0].shape[0]
    for slot in range(count):
        here = pl.ds(pl.multiple_of(owners[slot] * height, height), height)
        product_ref[here, :] = matmul(refs[slot][...], weight_ref[...])

        @pl.when(pl.program_id(0) == 0)
        def _(slot=slot, here=here):
            kept_ref[here, :] = refs[slot][...]


def project(slots, weight, owners):
    count = len(slots)
    height, depth = slots[0].shape
    width = weight.shape[1]
    step = min(512, width)
    row_spec = pl.BlockSpec((height, depth), lambda j, at: (0, 0))
    return pl.pallas_call(
        project_kernel,
        grid_spec=pltpu.PrefetchScalarGridSpec(
            num_scalar_prefetch=1,
            grid=(width // step,),
            in_specs=[row_spec] * count + [pl.BlockSpec((depth, step), lambda j, at: (0, j))],
            out_specs=[
                pl.BlockSpec((count * height, step), lambda j, at: (0, j)),
                pl.BlockSpec((count * height, depth), lambda j, at: (0, 0)),
            ],
        ),
        out_shape=[
            jax.ShapeDtypeStruct((count * height, width), F32),
            jax.ShapeDtypeStruct((count * height, depth), BF16),
        ],
        cost_estimate=pl.CostEstimate(
            flops=2 * count * height * depth * width,
            bytes_accessed=2 * depth * width + 4 * count * height * width,
            transcendentals=0,
        ),
        compiler_params=kernel_params(4 + 6 * count),
        name="project",
    )(jnp.stack(owners), *slots, weight)


def back_kernel(owner, rows_ref, weight_ref, out_ref):
    out_ref[...] = matmul(rows_ref[...], weight_ref[...], 1, 1).astype(out_ref.dtype)


def back_product(source, weight, owner, height):
    depth = source.shape[1]
    width = weight.shape[0]
    step = min(512, width)
    return pl.pallas_call(
        back_kernel,
        grid_spec=pltpu.PrefetchScalarGridSpec(
            num_scalar_prefetch=1,
            grid=(width // step,),
            in_specs=[
                pl.BlockSpec((height, depth), lambda j, at: (at[0], 0)),
                pl.BlockSpec((step, depth), lambda j, at: (j, 0)),
            ],
            out_specs=pl.BlockSpec((height, step), lambda j, at: (0, j)),
        ),
        out_shape=jax.ShapeDtypeStruct((height, width), BF16),
        cost_estimate=pl.CostEstimate(
            flops=2 * height * depth * width,
            bytes_accessed=2 * depth * width + 6 * height * width,
            transcendentals=0,
        ),
        compiler_params=kernel_params(12),
        name="back_product",
    )(owner.reshape(1), source, weight)


def decay_block(rate, first, seg_col, seg_row, width):
    height = seg_col.shape[0]
    down = lax.broadcasted_iota(jnp.int32, (height, 1), 0)
    across = lax.broadcasted_iota(jnp.int32, (1, width), 1)
    inside = (down + first >= across) & (seg_col == seg_row)
    factor = jnp.exp(down.astype(F32) * rate) * jnp.exp((first - across).astype(F32) * rate)
    return jnp.where(inside, factor, 0.0)


def retention_kernel(blocks, rates, seg_col, seg_row, query, key, value, gate, gated, retained, keys, values):
    head, at = pl.program_id(0), pl.program_id(1)
    height = query.shape[0]

    @pl.when(at == 0)
    def _():
        keys[...] = key[...].astype(BF16)
        values[...] = value[...].astype(BF16)

    for block in range(blocks):

        @pl.when(at == block)
        def _(block=block):
            width = (block + 1) * height
            decay = decay_block(rates[head], block * height, seg_col[...], seg_row[:, :width], width)
            scores = matmul(query[...].astype(BF16), keys[:width, :], 1, 1)
            mixed = matmul((scores * decay).astype(BF16), values[:width, :])
            retained[...] = mixed
            normal = mixed * lax.rsqrt(jnp.mean(mixed * mixed, -1, keepdims=True) + 1e-06)
            pre = gate[...]
            gated[...] = (pre * jax.nn.sigmoid(pre) * normal).astype(BF16)


def head_specs(seq_len):
    per_head = HEAD_COLS // KEY_DIM
    return [
        pl.BlockSpec(memory_space=pltpu.SMEM),
        pl.BlockSpec((BLOCK, 1), lambda h, i: (i, 0)),
        pl.BlockSpec((1, seq_len), lambda h, i: (0, 0)),
        pl.BlockSpec((BLOCK, KEY_DIM), lambda h, i: (i, per_head * h)),
        pl.BlockSpec((seq_len, KEY_DIM), lambda h, i: (0, per_head * h + 1)),
        pl.BlockSpec((seq_len, VALUE_DIM), lambda h, i: (0, 3 * h + 1)),
        pl.BlockSpec((BLOCK, VALUE_DIM), lambda h, i: (i, 3 * h + 2)),
    ]


def retention(product, segments, rates):
    seq_len = segments.shape[0]
    heads = rates.shape[0]
    blocks = seq_len // BLOCK
    out_spec = pl.BlockSpec((BLOCK, VALUE_DIM), lambda h, i: (i, h))
    return pl.pallas_call(
        functools.partial(retention_kernel, blocks),
        grid=(heads, blocks),
        in_specs=head_specs(seq_len),
        out_specs=[out_spec, out_spec],
        out_shape=[
            jax.ShapeDtypeStruct((seq_len, heads * VALUE_DIM), BF16),
            jax.ShapeDtypeStruct((seq_len, heads * VALUE_DIM), F32),
        ],
        scratch_shapes=[pltpu.VMEM((seq_len, KEY_DIM), BF16), pltpu.VMEM((seq_len, VALUE_DIM), BF16)],
        cost_estimate=pl.CostEstimate(
            flops=2 * heads * seq_len * seq_len * (KEY_DIM + VALUE_DIM),
            bytes_accessed=10 * seq_len * heads * HEAD_COLS,
            transcendentals=0,
        ),
        compiler_params=kernel_params(10 + seq_len // 128),
        name="retention",
    )(rates, segments.reshape(seq_len, 1), segments.reshape(1, seq_len), product, product, product, product)


def retention_back_kernel(
    blocks, rates, seg_col, seg_row, query, key, value, gate, retained, grad_gated, grads, keys, values, key_total, value_total
):
    head, at = pl.program_id(0), pl.program_id(1)
    height = query.shape[0]

    @pl.when(at == 0)
    def _():
        keys[...] = key[...].astype(BF16)
        values[...] = value[...].astype(BF16)
        key_total[...] = jnp.zeros_like(key_total)
        value_total[...] = jnp.zeros_like(value_total)

    for block in range(blocks):

        @pl.when(at == block)
        def _(block=block):
            width = (block + 1) * height
            here = slice(block * height, width)
            mixed = retained[...]
            scale = lax.rsqrt(jnp.mean(mixed * mixed, -1, keepdims=True) + 1e-06)
            normal = mixed * scale
            pre = gate[...]
            grad = grad_gated[...].astype(F32)
            open_part = jax.nn.sigmoid(pre)
            grads[here, 2 * KEY_DIM + VALUE_DIM :] = (
                grad * normal * (open_part * (1.0 + pre * (1.0 - open_part)))
            ).astype(BF16)
            grad_normal = grad * (pre * open_part)
            grad_mixed = (
                scale * (grad_normal - normal * jnp.mean(grad_normal * normal, -1, keepdims=True))
            ).astype(BF16)
            decay = decay_block(rates[head], block * height, seg_col[...], seg_row[:, :width], width)
            query_low = query[...].astype(BF16)
            weights = (matmul(query_low, keys[:width, :], 1, 1) * decay).astype(BF16)
            grad_scores = (matmul(grad_mixed, values[:width, :], 1, 1) * decay).astype(BF16)
            grads[here, :KEY_DIM] = matmul(grad_scores, keys[:width, :]).astype(BF16)
            key_total[:width, :] += matmul(grad_scores, query_low, 0, 0)
            value_total[:width, :] += matmul(weights, grad_mixed, 0, 0)

    @pl.when(at == blocks - 1)
    def _():
        grads[:, KEY_DIM : 2 * KEY_DIM] = key_total[...].astype(BF16)
        grads[:, 2 * KEY_DIM : 2 * KEY_DIM + VALUE_DIM] = value_total[...].astype(BF16)


def retention_back(product, segments, rates, retained, grad_gated):
    seq_len = segments.shape[0]
    heads = rates.shape[0]
    blocks = seq_len // BLOCK
    side_spec = pl.BlockSpec((BLOCK, VALUE_DIM), lambda h, i: (i, h))
    return pl.pallas_call(
        functools.partial(retention_back_kernel, blocks),
        grid=(heads, blocks),
        in_specs=head_specs(seq_len) + [side_spec, side_spec],
        out_specs=pl.BlockSpec((seq_len, HEAD_COLS), lambda h, i: (0, h)),
        out_shape=jax.ShapeDtypeStruct((seq_len, heads * HEAD_COLS), BF16),
        scratch_shapes=[
            pltpu.VMEM((seq_len, KEY_DIM), BF16),
            pltpu.VMEM((seq_len, VALUE_DIM), BF16),
            pltpu.VMEM((seq_len, KEY_DIM), F32),
            pltpu.VMEM((seq_len, VALUE_DIM), F32),
        ],
        cost_estimate=pl.CostEstimate(
            flops=2 * heads * seq_len * seq_len * (3 * KEY_DIM + 2 * VALUE_DIM),
            bytes_accessed=12 * seq_len * heads * HEAD_COLS,
            transcendentals=0,
        ),
        compiler_params=kernel_params(10 + seq_len // 45),
        name="retention_back",
    )(
        rates, segments.reshape(seq_len, 1), segments.reshape(1, seq_len),
        product, product, product, product, retained, grad_gated,
    )


def mlp_kernel(steps, rows, cot, pair_w, down_w, *refs):
    pair_out, inner_out, down_terms, back_terms, down_total, back_total = refs[-6:]
    at = pl.program_id(0)
    half = down_w.shape[1]
    pair = matmul(rows[...], pair_w[...])
    gate, up = pair[:, :half], pair[:, half:]
    grad_inner = matmul(cot[...], down_w[...]).astype(BF16).astype(F32)
    below = 0.5 * (1.0 + lax.erf(gate * (0.5**0.5)))
    slope = below + gate * (jnp.exp(-0.5 * gate * gate) * 0.3989422804014327)
    bent = gate * below
    inner = (bent * up).astype(BF16)
    grad_pair = jnp.concatenate(
        [(grad_inner * up * slope).astype(BF16), (grad_inner * bent).astype(BF16)], 1
    )
    inner_out[...] = inner
    pair_out[...] = grad_pair
    down_part = matmul(inner, down_w[...], 1, 1)
    back_part = matmul(grad_pair, pair_w[...], 1, 1)

    @pl.when(at == 0)
    def _():
        down_total[...] = down_part
        back_total[...] = back_part

    @pl.when(at > 0)
    def _():
        down_total[...] += down_part
        back_total[...] += back_part

    @pl.when(at == steps - 1)
    def _():
        down_terms[...] = down_total[...].astype(down_terms.dtype)
        back_terms[...] = back_total[...].astype(back_terms.dtype)


def mlp_block(rows, cot, weights, slot, count, buffers=()):
    height, depth = rows.shape
    hidden = weights.shape[1] // 3
    step = min(256, hidden)
    steps = hidden // step
    row_spec = pl.BlockSpec((height, depth), lambda j: (0, 0))
    in_specs = [
        row_spec,
        row_spec,
        pl.BlockSpec((depth, 2 * step), lambda j: (0, j)),
        pl.BlockSpec((depth, step), lambda j: (0, 2 * steps + j)),
    ]
    operands = [rows, cot, weights, weights]
    aliases = {}
    if buffers:
        operands += list(buffers)
        in_specs += [pl.BlockSpec(memory_space=pl.ANY)] * 4
        aliases = {4: 0, 5: 1, 6: 2, 7: 3}
    wide_spec = pl.BlockSpec((height, depth), lambda j: (slot, 0))
    return pl.pallas_call(
        functools.partial(mlp_kernel, steps),
        grid=(steps,),
        in_specs=in_specs,
        out_specs=[
            pl.BlockSpec((height, 2 * step), lambda j: (slot, j)),
            pl.BlockSpec((height, step), lambda j: (slot, j)),
            wide_spec,
            wide_spec,
        ],
        out_shape=[
            jax.ShapeDtypeStruct((count * height, 2 * hidden), BF16),
            jax.ShapeDtypeStruct((count * height, hidden), BF16),
            jax.ShapeDtypeStruct((count * height, depth), BF16),
            jax.ShapeDtypeStruct((count * height, depth), BF16),
        ],
        scratch_shapes=[pltpu.VMEM((height, depth), F32)] * 2,
        input_output_aliases=aliases,
        cost_estimate=pl.CostEstimate(
            flops=12 * height * depth * hidden,
            bytes_accessed=6 * depth * hidden + 20 * height * depth,
            transcendentals=0,
        ),
        compiler_params=kernel_params(28),
        name="mlp_block",
    )(*operands)


class Gather:
    def __init__(self, block, count):
        self.count = count
        self.from_left, self.from_right, self.slots = [block], [block], [block]

    def step(self, *ready):
        count, step = self.count, len(self.slots)
        place = lax.axis_index("tensor")
        left, right = self.from_left[-1], self.from_right[-1]
        if ready:
            left, right = lax.optimization_barrier((left, right, *ready))[:2]
        self.from_left.append(
            lax.ppermute(left, "tensor", [(i, i + 1) for i in range(step - 1, count - 1)])
        )
        self.from_right.append(
            lax.ppermute(right, "tensor", [(i + 1, i) for i in range(count - step)])
        )
        chosen = None
        for owner in range(count):
            rights = count - 1 - owner
            if owner < count // 2:
                wanted = self.from_right[step] if step <= rights else self.from_left[step - rights]
            else:
                wanted = self.from_left[step] if step <= owner else self.from_right[step - owner]
            chosen = wanted if chosen is None else jnp.where(place >= owner, wanted, chosen)
        self.slots.append(chosen)
        return self.arrived(step)

    def arrived(self, step):
        return (self.from_left[step], self.from_right[step])


class Scatter:
    def __init__(self, block_of, count):
        self.block_of, self.count, self.steps = block_of, count, 0
        self.to_right = self.to_left = None

    def step(self, *ready):
        count = self.count
        place = lax.axis_index("tensor")
        self.steps += 1
        step = self.steps
        ahead = count - step
        right = self.block_of(jnp.minimum(place + ahead, count - 1), step).astype(F32)
        left = self.block_of(jnp.maximum(place - ahead, 0), step).astype(F32)
        if step > 1:
            right = right + self.to_right.astype(F32)
            left = left + self.to_left.astype(F32)
        right, left = right.astype(BF16), left.astype(BF16)
        if ready:
            right, left = lax.optimization_barrier((right, left, *ready))[:2]
        self.to_right = lax.ppermute(right, "tensor", [(i, i + 1) for i in range(step)])
        self.to_left = lax.ppermute(
            left, "tensor", [(i + 1, i) for i in range(count - 1 - step, count - 1)]
        )
        return (self.to_right, self.to_left)

    def total(self):
        own = self.block_of(lax.axis_index("tensor"), self.count).astype(F32)
        if self.steps:
            own = own + (self.to_right.astype(F32) + self.to_left.astype(F32))
        return own


def slot_owner(place, slot, count):
    rights = count - 1 - place
    first_half = jnp.where(slot <= rights, place + slot, place - (slot - rights))
    second_half = jnp.where(slot <= place, place - slot, slot)
    return jnp.where(place < count // 2, first_half, second_half)


def owner_slot(place, owner, count):
    rights = count - 1 - place
    first_half = jnp.where(owner >= place, owner - place, rights + place - owner)
    second_half = jnp.where(owner <= place, place - owner, owner)
    return jnp.where(place < count // 2, first_half, second_half)


def dp_scatter(part):
    return lax.psum_scatter(part, "dp", scatter_dimension=0, tiled=True)


def sum_everywhere(values, sizes):
    for axis, size in sizes:
        bit = 1
        while bit < size:
            values = values + lax.ppermute(values, axis, [(i, i ^ bit) for i in range(size)])
            bit *= 2
    return values


def per_head(parts, heads):
    pieces = []
    for head in range(heads):
        for part in parts:
            size = part.shape[1] // heads
            pieces.append(part[:, head * size : (head + 1) * size])
    return jnp.concatenate(pieces, 1)


def body(
    tokens,
    segments,
    cotangent,
    attn_norm_gain,
    attn_norm_shift,
    w_query,
    w_key,
    w_value,
    w_gate,
    w_output,
    ffn_norm_gain,
    ffn_norm_shift,
    w_ffn_gate,
    w_ffn_up,
    w_ffn_down,
):
    seq_len = segments.shape[0]
    rows = tokens.shape[0]
    count = seq_len // rows
    dp_count = lax.axis_size("dp")
    place = lax.axis_index("tensor")
    hk = w_query.shape[1]
    ff = w_ffn_gate.shape[1]
    heads = hk // KEY_DIM
    mlp_step = min(256, ff)
    mlp_steps = ff // mlp_step
    head_ids = (place * heads + jnp.arange(heads, dtype=jnp.int32)).astype(F32)
    rates = jnp.log1p(-jnp.exp2(-5.0 - head_ids))

    def rows_of(stacked):
        return lambda owner, step: lax.dynamic_slice_in_dim(stacked, owner * rows, rows, 0)

    def slots_of(stacked):
        return lambda owner, step: rows_of(stacked)(owner_slot(place, owner, count), step)

    last = count - 1
    residual = tokens.astype(F32)
    normed, first_pull = jax.vjp(layer_norm, residual, attn_norm_gain, attn_norm_shift)
    mixer_full = lax.all_gather(
        per_head([w_query, w_key, w_value, w_gate], heads), "dp", axis=0, tiled=True
    )
    output_turned = w_output.T
    ffn_shard = jnp.concatenate([per_head([w_ffn_gate, w_ffn_up], mlp_steps), w_ffn_down.T], 1)
    first = Gather(normed.astype(BF16), count)
    for step in range(1, count):
        first.step(*([output_turned, ffn_shard] if step == 2 else []))
    output_full = lax.all_gather(
        after(output_turned, *first.arrived(1)), "dp", axis=0, tiled=True
    )
    ffn_full = lax.all_gather(
        after(ffn_shard, *first.arrived(min(2, last))), "dp", axis=0, tiled=True
    )

    product, whole_normed = project(
        first.slots, mixer_full, [slot_owner(place, slot, count) for slot in range(count)]
    )

    cots = Gather(cotangent, count)
    cots.step(*first.arrived(last))
    gated_low, retained = retention(product, segments, rates)
    mixer = Scatter(rows_of(matmul(gated_low, output_full, 1, 1).astype(BF16)), count)
    for step in range(1, count):
        mixer.step(*cots.arrived(step))
        if step < last:
            cots.step()
    hidden = residual + mixer.total()
    normed_two, second_pull = jax.vjp(layer_norm, hidden, ffn_norm_gain, ffn_norm_shift)

    second = Gather(normed_two.astype(BF16), count)
    buffers = ()
    for slot in range(count):
        block = second.slots[slot]
        if slot < last:
            second.step(*buffers)
        else:
            block = after(block, *buffers)
        buffers = mlp_block(block, cots.slots[slot], ffn_full, slot, count, buffers)
    grad_pairs, inner, down_terms, back_terms = buffers

    back = Scatter(slots_of(back_terms), count)
    started = back.step()
    pair_part = matmul(jnp.concatenate(second.slots, 0), grad_pairs, 0, 0).astype(BF16)
    down_part = matmul(
        after(jnp.concatenate(cots.slots, 0), pair_part), inner, 0, 0
    ).astype(BF16)
    pair_grad = dp_scatter(after(pair_part, *started))
    down_grad = dp_scatter(after(down_part, *started))
    for step in range(2, count):
        back.step()
    grad_from_two, grad_ffn_gain_part, grad_ffn_shift_part = second_pull(back.total())
    grad_hidden = cotangent.astype(F32) + grad_from_two

    branch = Gather(grad_hidden.astype(BF16), count)
    down = Scatter(slots_of(down_terms), count)
    buffers, sent = (), ()
    for slot in range(count):
        block = branch.slots[slot]
        if slot < last:
            branch.step(*buffers, *sent)
            sent = down.step(*branch.arrived(slot)) if slot > 0 else ()
        else:
            block = after(block, *buffers, *sent)
        buffers = place_product(
            block, output_full, slot_owner(place, slot, count), count, BF16, buffers
        )
    grad_gated, whole_branch = buffers
    output_part = matmul(whole_branch, gated_low, 0, 0).astype(BF16)
    output_grad = dp_scatter(output_part)
    grads = retention_back(product, segments, rates, retained, after(grad_gated, output_part))
    sent = down.step()
    layer_output = (hidden + down.total()).astype(BF16)

    normed_terms = []

    def far_of(owner, step):
        index = count - 1 - owner_slot(place, owner, count)
        chosen = normed_terms[0]
        for other in range(1, step):
            chosen = jnp.where(index >= other, normed_terms[other], chosen)
        return chosen

    def columns(grad, groups, first, size):
        stride = grad.shape[1] // groups
        parts = [grad[:, g * stride + first : g * stride + first + size] for g in range(groups)]
        return jnp.concatenate(parts, 1).astype(F32)

    done_early = (
        layer_output,
        output_grad.astype(F32).T,
        columns(pair_grad, mlp_steps, 0, mlp_step),
        columns(pair_grad, mlp_steps, mlp_step, mlp_step),
        down_grad.astype(F32).T,
    )
    last_scatter = Scatter(far_of, count)
    source = after(grads, *sent)
    mixer_part = None
    for index in range(count):
        normed_terms.append(
            back_product(source, mixer_full, slot_owner(place, count - 1 - index, count), rows)
        )
        if index == 0:
            mixer_part = matmul(whole_normed, after(grads, normed_terms[0]), 0, 0).astype(BF16)
            source = after(source, mixer_part)
        if index < last:
            sent = last_scatter.step(*(done_early if index == last - 1 else ()))
        if index == 0:
            mixer_grad = dp_scatter(after(mixer_part, *sent))
    grad_from_one, grad_attn_gain_part, grad_attn_shift_part = first_pull(last_scatter.total())
    grad_tokens = grad_hidden + grad_from_one

    gains = sum_everywhere(
        jnp.stack(
            [grad_attn_gain_part, grad_attn_shift_part, grad_ffn_gain_part, grad_ffn_shift_part]
        ),
        (("dp", dp_count), ("tensor", count)),
    )

    return (
        layer_output,
        grad_tokens,
        gains[0],
        gains[1],
        columns(mixer_grad, heads, 0, KEY_DIM),
        columns(mixer_grad, heads, KEY_DIM, KEY_DIM),
        columns(mixer_grad, heads, 2 * KEY_DIM, VALUE_DIM),
        columns(mixer_grad, heads, 2 * KEY_DIM + VALUE_DIM, VALUE_DIM),
        done_early[1],
        gains[2],
        gains[3],
        *done_early[2:],
    )


def solution(mesh):
    split = P(("dp", "tensor"), None)
    weight = P("dp", "tensor")
    turned = P("tensor", "dp")
    return jax.shard_map(
        body,
        mesh=mesh,
        in_specs=(
            split, P("dp"), split, P(), P(), weight, weight, weight, weight, turned,
            P(), P(), weight, weight, turned,
        ),
        out_specs=(
            split, split, P(), P(), weight, weight, weight, weight, turned,
            P(), P(), weight, weight, turned,
        ),
        check_vma=False,
    )
```

```python
import functools

import jax
import jax.numpy as jnp
from jax import lax
from jax.experimental import pallas as pl
from jax.experimental.pallas import tpu as pltpu
from jax.sharding import PartitionSpec as P

KEY_DIM = 256
VALUE_DIM = 512
HEAD_COLS = 2 * KEY_DIM + 2 * VALUE_DIM
BLOCK = 256
F32 = jnp.float32
BF16 = jnp.bfloat16
MIB = 1024 * 1024


def layer_norm(values, gain, shift):
    centred = values - jnp.mean(values, -1, keepdims=True)
    spread = jnp.mean(centred * centred, -1, keepdims=True)
    return centred * lax.rsqrt(spread + 1e-05) * gain + shift


def matmul(left, right, left_dim=1, right_dim=0):
    return lax.dot_general(
        left, right, (((left_dim,), (right_dim,)), ((), ())), preferred_element_type=F32
    )


def after(value, *others):
    return lax.optimization_barrier((value, *others))[0]


def kernel_params(mib):
    return pltpu.CompilerParams(vmem_limit_bytes=mib * MIB)


def pack_kernel(plan, *refs):
    *parts, out = refs
    for part, first, to, size, turned in plan:
        piece = parts[part][first : first + size, :].T if turned else parts[part][:, first : first + size]
        out[:, to : to + size] = piece


def pack(parts, plan, width):
    height = parts[0].shape[0]
    return pl.pallas_call(
        functools.partial(pack_kernel, plan),
        out_shape=jax.ShapeDtypeStruct((height, width), BF16),
        cost_estimate=pl.CostEstimate(flops=0, bytes_accessed=4 * height * width, transcendentals=0),
        compiler_params=kernel_params(16),
        name="pack",
    )(*parts)


def pack_mixer(w_query, w_key, w_value, w_gate, w_output, heads):
    plan = []
    for head in range(heads):
        to = head * HEAD_COLS
        plan += [
            (0, head * KEY_DIM, to, KEY_DIM, False),
            (1, head * KEY_DIM, to + KEY_DIM, KEY_DIM, False),
            (2, head * VALUE_DIM, to + 2 * KEY_DIM, VALUE_DIM, False),
            (3, head * VALUE_DIM, to + 2 * KEY_DIM + VALUE_DIM, VALUE_DIM, False),
        ]
    hv = w_output.shape[0]
    plan.append((4, 0, heads * HEAD_COLS, hv, True))
    return pack([w_query, w_key, w_value, w_gate, w_output], tuple(plan), heads * HEAD_COLS + hv)


def pack_mlp(w_gate, w_up, w_down, step):
    hidden = w_down.shape[0]
    plan = []
    for at in range(0, hidden, step):
        plan += [(0, at, 2 * at, step, False), (1, at, 2 * at + step, step, False)]
    plan.append((2, 0, 2 * hidden, hidden, True))
    return pack([w_gate, w_up, w_down], tuple(plan), 3 * hidden)


def place_kernel(owner, rows_ref, weight_ref, *refs):
    product_ref, kept_ref = refs[-2:]
    product_ref[...] = matmul(rows_ref[...], weight_ref[...]).astype(product_ref.dtype)

    @pl.when(pl.program_id(0) == 0)
    def _():
        kept_ref[...] = rows_ref[...]


def place_product(rows, weight, first, width, owner, count, kind, buffers=()):
    height, depth = rows.shape
    step = min(512, width)
    row_spec = pl.BlockSpec((height, depth), lambda j, at: (0, 0))
    in_specs = [row_spec, pl.BlockSpec((depth, step), lambda j, at: (0, first // step + j))]
    operands = [owner.reshape(1), rows, weight]
    aliases = {}
    if buffers:
        operands += list(buffers)
        in_specs += [pl.BlockSpec(memory_space=pl.ANY)] * 2
        aliases = {3: 0, 4: 1}
    return pl.pallas_call(
        place_kernel,
        grid_spec=pltpu.PrefetchScalarGridSpec(
            num_scalar_prefetch=1,
            grid=(width // step,),
            in_specs=in_specs,
            out_specs=[
                pl.BlockSpec((height, step), lambda j, at: (at[0], j)),
                pl.BlockSpec((height, depth), lambda j, at: (at[0], 0)),
            ],
        ),
        out_shape=[
            jax.ShapeDtypeStruct((count * height, width), kind),
            jax.ShapeDtypeStruct((count * height, depth), BF16),
        ],
        input_output_aliases=aliases,
        cost_estimate=pl.CostEstimate(
            flops=2 * height * depth * width,
            bytes_accessed=2 * depth * width + 8 * height * width,
            transcendentals=0,
        ),
        compiler_params=kernel_params(12),
        name="place_product",
    )(*operands)


def project_kernel(owners, *refs):
    count = len(refs) - 3
    weight_ref, product_ref, kept_ref = refs[count:]
    height = refs[0].shape[0]
    for slot in range(count):
        here = pl.ds(pl.multiple_of(owners[slot] * height, height), height)
        product_ref[here, :] = matmul(refs[slot][...], weight_ref[...])

        @pl.when(pl.program_id(0) == 0)
        def _(slot=slot, here=here):
            kept_ref[here, :] = refs[slot][...]


def project(slots, weight, width, owners):
    count = len(slots)
    height, depth = slots[0].shape
    step = min(512, width)
    row_spec = pl.BlockSpec((height, depth), lambda j, at: (0, 0))
    return pl.pallas_call(
        project_kernel,
        grid_spec=pltpu.PrefetchScalarGridSpec(
            num_scalar_prefetch=1,
            grid=(width // step,),
            in_specs=[row_spec] * count + [pl.BlockSpec((depth, step), lambda j, at: (0, j))],
            out_specs=[
                pl.BlockSpec((count * height, step), lambda j, at: (0, j)),
                pl.BlockSpec((count * height, depth), lambda j, at: (0, 0)),
            ],
        ),
        out_shape=[
            jax.ShapeDtypeStruct((count * height, width), F32),
            jax.ShapeDtypeStruct((count * height, depth), BF16),
        ],
        cost_estimate=pl.CostEstimate(
            flops=2 * count * height * depth * width,
            bytes_accessed=2 * depth * width + 4 * count * height * width,
            transcendentals=0,
        ),
        compiler_params=kernel_params(4 + 6 * count),
        name="project",
    )(jnp.stack(owners), *slots, weight)


def back_kernel(owner, rows_ref, weight_ref, out_ref):
    out_ref[...] = matmul(rows_ref[...], weight_ref[...], 1, 1).astype(out_ref.dtype)


def back_product(source, weight, owner, height):
    depth = source.shape[1]
    width = weight.shape[0]
    step = min(512, width)
    return pl.pallas_call(
        back_kernel,
        grid_spec=pltpu.PrefetchScalarGridSpec(
            num_scalar_prefetch=1,
            grid=(width // step,),
            in_specs=[
                pl.BlockSpec((height, depth), lambda j, at: (at[0], 0)),
                pl.BlockSpec((step, depth), lambda j, at: (j, 0)),
            ],
            out_specs=pl.BlockSpec((height, step), lambda j, at: (0, j)),
        ),
        out_shape=jax.ShapeDtypeStruct((height, width), BF16),
        cost_estimate=pl.CostEstimate(
            flops=2 * height * depth * width,
            bytes_accessed=2 * depth * width + 6 * height * width,
            transcendentals=0,
        ),
        compiler_params=kernel_params(12),
        name="back_product",
    )(owner.reshape(1), source, weight)


def decay_block(rate, first, seg_col, seg_row, width):
    height = seg_col.shape[0]
    down = lax.broadcasted_iota(jnp.int32, (height, 1), 0)
    across = lax.broadcasted_iota(jnp.int32, (1, width), 1)
    inside = (down + first >= across) & (seg_col == seg_row)
    factor = jnp.exp(down.astype(F32) * rate) * jnp.exp((first - across).astype(F32) * rate)
    return jnp.where(inside, factor, 0.0)


def retention_kernel(blocks, rates, seg_col, seg_row, query, key, value, gate, gated, retained, keys, values):
    head, at = pl.program_id(0), pl.program_id(1)
    height = query.shape[0]

    @pl.when(at == 0)
    def _():
        keys[...] = key[...].astype(BF16)
        values[...] = value[...].astype(BF16)

    for block in range(blocks):

        @pl.when(at == block)
        def _(block=block):
            width = (block + 1) * height
            decay = decay_block(rates[head], block * height, seg_col[...], seg_row[:, :width], width)
            scores = matmul(query[...].astype(BF16), keys[:width, :], 1, 1)
            mixed = matmul((scores * decay).astype(BF16), values[:width, :])
            retained[...] = mixed
            normal = mixed * lax.rsqrt(jnp.mean(mixed * mixed, -1, keepdims=True) + 1e-06)
            pre = gate[...]
            gated[...] = (pre * jax.nn.sigmoid(pre) * normal).astype(BF16)


def head_specs(seq_len):
    per_head = HEAD_COLS // KEY_DIM
    return [
        pl.BlockSpec(memory_space=pltpu.SMEM),
        pl.BlockSpec((BLOCK, 1), lambda h, i: (i, 0)),
        pl.BlockSpec((1, seq_len), lambda h, i: (0, 0)),
        pl.BlockSpec((BLOCK, KEY_DIM), lambda h, i: (i, per_head * h)),
        pl.BlockSpec((seq_len, KEY_DIM), lambda h, i: (0, per_head * h + 1)),
        pl.BlockSpec((seq_len, VALUE_DIM), lambda h, i: (0, 3 * h + 1)),
        pl.BlockSpec((BLOCK, VALUE_DIM), lambda h, i: (i, 3 * h + 2)),
    ]


def retention(product, segments, rates):
    seq_len = segments.shape[0]
    heads = rates.shape[0]
    blocks = seq_len // BLOCK
    out_spec = pl.BlockSpec((BLOCK, VALUE_DIM), lambda h, i: (i, h))
    return pl.pallas_call(
        functools.partial(retention_kernel, blocks),
        grid=(heads, blocks),
        in_specs=head_specs(seq_len),
        out_specs=[out_spec, out_spec],
        out_shape=[
            jax.ShapeDtypeStruct((seq_len, heads * VALUE_DIM), BF16),
            jax.ShapeDtypeStruct((seq_len, heads * VALUE_DIM), F32),
        ],
        scratch_shapes=[pltpu.VMEM((seq_len, KEY_DIM), BF16), pltpu.VMEM((seq_len, VALUE_DIM), BF16)],
        cost_estimate=pl.CostEstimate(
            flops=2 * heads * seq_len * seq_len * (KEY_DIM + VALUE_DIM),
            bytes_accessed=10 * seq_len * heads * HEAD_COLS,
            transcendentals=0,
        ),
        compiler_params=kernel_params(10 + seq_len // 128),
        name="retention",
    )(rates, segments.reshape(seq_len, 1), segments.reshape(1, seq_len), product, product, product, product)


def retention_back_kernel(
    blocks, rates, seg_col, seg_row, query, key, value, gate, retained, grad_gated, grads, keys, values, key_total, value_total
):
    head, at = pl.program_id(0), pl.program_id(1)
    height = query.shape[0]

    @pl.when(at == 0)
    def _():
        keys[...] = key[...].astype(BF16)
        values[...] = value[...].astype(BF16)
        key_total[...] = jnp.zeros_like(key_total)
        value_total[...] = jnp.zeros_like(value_total)

    for block in range(blocks):

        @pl.when(at == block)
        def _(block=block):
            width = (block + 1) * height
            here = slice(block * height, width)
            mixed = retained[...]
            scale = lax.rsqrt(jnp.mean(mixed * mixed, -1, keepdims=True) + 1e-06)
            normal = mixed * scale
            pre = gate[...]
            grad = grad_gated[...].astype(F32)
            open_part = jax.nn.sigmoid(pre)
            grads[here, 2 * KEY_DIM + VALUE_DIM :] = (
                grad * normal * (open_part * (1.0 + pre * (1.0 - open_part)))
            ).astype(BF16)
            grad_normal = grad * (pre * open_part)
            grad_mixed = (
                scale * (grad_normal - normal * jnp.mean(grad_normal * normal, -1, keepdims=True))
            ).astype(BF16)
            decay = decay_block(rates[head], block * height, seg_col[...], seg_row[:, :width], width)
            query_low = query[...].astype(BF16)
            weights = (matmul(query_low, keys[:width, :], 1, 1) * decay).astype(BF16)
            grad_scores = (matmul(grad_mixed, values[:width, :], 1, 1) * decay).astype(BF16)
            grads[here, :KEY_DIM] = matmul(grad_scores, keys[:width, :]).astype(BF16)
            key_total[:width, :] += matmul(grad_scores, query_low, 0, 0)
            value_total[:width, :] += matmul(weights, grad_mixed, 0, 0)

    @pl.when(at == blocks - 1)
    def _():
        grads[:, KEY_DIM : 2 * KEY_DIM] = key_total[...].astype(BF16)
        grads[:, 2 * KEY_DIM : 2 * KEY_DIM + VALUE_DIM] = value_total[...].astype(BF16)


def retention_back(product, segments, rates, retained, grad_gated):
    seq_len = segments.shape[0]
    heads = rates.shape[0]
    blocks = seq_len // BLOCK
    side_spec = pl.BlockSpec((BLOCK, VALUE_DIM), lambda h, i: (i, h))
    return pl.pallas_call(
        functools.partial(retention_back_kernel, blocks),
        grid=(heads, blocks),
        in_specs=head_specs(seq_len) + [side_spec, side_spec],
        out_specs=pl.BlockSpec((seq_len, HEAD_COLS), lambda h, i: (0, h)),
        out_shape=jax.ShapeDtypeStruct((seq_len, heads * HEAD_COLS), BF16),
        scratch_shapes=[
            pltpu.VMEM((seq_len, KEY_DIM), BF16),
            pltpu.VMEM((seq_len, VALUE_DIM), BF16),
            pltpu.VMEM((seq_len, KEY_DIM), F32),
            pltpu.VMEM((seq_len, VALUE_DIM), F32),
        ],
        cost_estimate=pl.CostEstimate(
            flops=2 * heads * seq_len * seq_len * (3 * KEY_DIM + 2 * VALUE_DIM),
            bytes_accessed=12 * seq_len * heads * HEAD_COLS,
            transcendentals=0,
        ),
        compiler_params=kernel_params(10 + seq_len // 45),
        name="retention_back",
    )(
        rates, segments.reshape(seq_len, 1), segments.reshape(1, seq_len),
        product, product, product, product, retained, grad_gated,
    )


def mlp_kernel(steps, rows_a, rows_b, cot_a, cot_b, pair_w, down_w, *refs):
    pair_out, inner_out, down_terms, back_terms, rows, cot, down_total, back_total = refs[-8:]
    at = pl.program_id(0)
    half = down_w.shape[1]
    height = rows_a.shape[0]

    @pl.when(at == 0)
    def _():
        rows[:height, :] = rows_a[...]
        rows[height:, :] = rows_b[...]
        cot[:height, :] = cot_a[...]
        cot[height:, :] = cot_b[...]

    pair = matmul(rows[...], pair_w[...])
    gate, up = pair[:, :half], pair[:, half:]
    grad_inner = matmul(cot[...], down_w[...]).astype(BF16).astype(F32)
    below = 0.5 * (1.0 + lax.erf(gate * (0.5**0.5)))
    slope = below + gate * (jnp.exp(-0.5 * gate * gate) * 0.3989422804014327)
    bent = gate * below
    inner = (bent * up).astype(BF16)
    grad_pair = jnp.concatenate(
        [(grad_inner * up * slope).astype(BF16), (grad_inner * bent).astype(BF16)], 1
    )
    for part in range(2):
        here = slice(part * height, (part + 1) * height)
        inner_out[part, 0] = inner[here, :]
        pair_out[part, 0] = grad_pair[here, :]
    down_part = matmul(inner, down_w[...], 1, 1)
    back_part = matmul(grad_pair, pair_w[...], 1, 1)

    @pl.when(at == 0)
    def _():
        down_total[...] = down_part
        back_total[...] = back_part

    @pl.when(at > 0)
    def _():
        down_total[...] += down_part
        back_total[...] += back_part

    @pl.when(at == steps - 1)
    def _():
        for part in range(2):
            here = slice(part * height, (part + 1) * height)
            down_terms[part, 0] = down_total[here, :].astype(BF16)
            back_terms[part, 0] = back_total[here, :].astype(BF16)


def mlp_blocks(rows, cots, weights, slot, slots, step, buffers=()):
    height, depth = rows[0].shape
    hidden = weights.shape[1] // 3
    steps = hidden // step
    row_spec = pl.BlockSpec((height, depth), lambda j: (0, 0))
    in_specs = [row_spec] * 4 + [
        pl.BlockSpec((depth, 2 * step), lambda j: (0, j)),
        pl.BlockSpec((depth, step), lambda j: (0, 2 * steps + j)),
    ]
    operands = [*rows, *cots, weights, weights]
    aliases = {}
    if buffers:
        operands += list(buffers)
        in_specs += [pl.BlockSpec(memory_space=pl.ANY)] * 4
        aliases = {6: 0, 7: 1, 8: 2, 9: 3}
    wide_spec = pl.BlockSpec((2, 1, height, depth), lambda j: (0, slot, 0, 0))
    return pl.pallas_call(
        functools.partial(mlp_kernel, steps),
        grid=(steps,),
        in_specs=in_specs,
        out_specs=[
            pl.BlockSpec((2, 1, height, 2 * step), lambda j: (0, slot, 0, j)),
            pl.BlockSpec((2, 1, height, step), lambda j: (0, slot, 0, j)),
            wide_spec,
            wide_spec,
        ],
        out_shape=[
            jax.ShapeDtypeStruct((2, slots, height, 2 * hidden), BF16),
            jax.ShapeDtypeStruct((2, slots, height, hidden), BF16),
            jax.ShapeDtypeStruct((2, slots, height, depth), BF16),
            jax.ShapeDtypeStruct((2, slots, height, depth), BF16),
        ],
        scratch_shapes=[pltpu.VMEM((2 * height, depth), BF16)] * 2
        + [pltpu.VMEM((2 * height, depth), F32)] * 2,
        input_output_aliases=aliases,
        cost_estimate=pl.CostEstimate(
            flops=24 * height * depth * hidden,
            bytes_accessed=6 * depth * hidden + 40 * height * depth,
            transcendentals=0,
        ),
        compiler_params=kernel_params(50),
        name="mlp_blocks",
    )(*operands)


def weight_grad_kernel(left, right, *refs):
    refs[-1][...] = matmul(left[...], right[...], 0, 0).astype(BF16)


def weight_grad(left, right, first, width, buffer=None):
    length, depth = left.shape
    columns = right.shape[1]
    step = min(512, columns)
    in_specs = [
        pl.BlockSpec((length, depth), lambda j: (0, 0)),
        pl.BlockSpec((length, step), lambda j: (0, j)),
    ]
    operands = [left, right]
    aliases = {}
    if buffer is not None:
        operands.append(buffer)
        in_specs.append(pl.BlockSpec(memory_space=pl.ANY))
        aliases = {2: 0}
    return pl.pallas_call(
        weight_grad_kernel,
        grid=(columns // step,),
        in_specs=in_specs,
        out_specs=pl.BlockSpec((depth, step), lambda j: (0, first // step + j)),
        out_shape=jax.ShapeDtypeStruct((depth, width), BF16),
        input_output_aliases=aliases,
        cost_estimate=pl.CostEstimate(
            flops=2 * length * depth * columns,
            bytes_accessed=2 * length * (depth + columns) + 2 * depth * columns,
            transcendentals=0,
        ),
        compiler_params=kernel_params(16 + length // 64),
        name="weight_grad",
    )(*operands)


class Gather:
    def __init__(self, block, count):
        self.count = count
        self.from_left, self.from_right, self.slots = [block], [block], [block]

    def step(self, *ready):
        count, step = self.count, len(self.slots)
        place = lax.axis_index("tensor")
        left, right = self.from_left[-1], self.from_right[-1]
        if ready:
            left, right = lax.optimization_barrier((left, right, *ready))[:2]
        self.from_left.append(
            lax.ppermute(left, "tensor", [(i, i + 1) for i in range(step - 1, count - 1)])
        )
        self.from_right.append(
            lax.ppermute(right, "tensor", [(i + 1, i) for i in range(count - step)])
        )
        chosen = None
        for owner in range(count):
            rights = count - 1 - owner
            if owner < count // 2:
                wanted = self.from_right[step] if step <= rights else self.from_left[step - rights]
            else:
                wanted = self.from_left[step] if step <= owner else self.from_right[step - owner]
            chosen = wanted if chosen is None else jnp.where(place >= owner, wanted, chosen)
        self.slots.append(chosen)
        return self.arrived(step)

    def arrived(self, step):
        return (self.from_left[step], self.from_right[step])


class Scatter:
    def __init__(self, block_of, count):
        self.block_of, self.count, self.steps = block_of, count, 0
        self.to_right = self.to_left = None

    def step(self, *ready):
        count = self.count
        place = lax.axis_index("tensor")
        self.steps += 1
        step = self.steps
        ahead = count - step
        right = self.block_of(jnp.minimum(place + ahead, count - 1), step).astype(F32)
        left = self.block_of(jnp.maximum(place - ahead, 0), step).astype(F32)
        if step > 1:
            right = right + self.to_right.astype(F32)
            left = left + self.to_left.astype(F32)
        right, left = right.astype(BF16), left.astype(BF16)
        if ready:
            right, left = lax.optimization_barrier((right, left, *ready))[:2]
        self.to_right = lax.ppermute(right, "tensor", [(i, i + 1) for i in range(step)])
        self.to_left = lax.ppermute(
            left, "tensor", [(i + 1, i) for i in range(count - 1 - step, count - 1)]
        )
        return (self.to_right, self.to_left)

    def total(self):
        own = self.block_of(lax.axis_index("tensor"), self.count).astype(F32)
        if self.steps:
            own = own + (self.to_right.astype(F32) + self.to_left.astype(F32))
        return own


def slot_owner(place, slot, count):
    rights = count - 1 - place
    first_half = jnp.where(slot <= rights, place + slot, place - (slot - rights))
    second_half = jnp.where(slot <= place, place - slot, slot)
    return jnp.where(place < count // 2, first_half, second_half)


def owner_slot(place, owner, count):
    rights = count - 1 - place
    first_half = jnp.where(owner >= place, owner - place, rights + place - owner)
    second_half = jnp.where(owner <= place, place - owner, owner)
    return jnp.where(place < count // 2, first_half, second_half)


def dp_scatter(part):
    return lax.psum_scatter(part, "dp", scatter_dimension=0, tiled=True)


def core_swap(block):
    return lax.ppermute(block, "dp", [(i, i ^ 1) for i in range(lax.axis_size("dp"))])


def line_swap(block, bit):
    return lax.ppermute(block, "tensor", [(i, i ^ bit) for i in range(lax.axis_size("tensor"))])


def group_bits(half):
    return [1 << k for k in range(half.bit_length() - 1)]


def chip_sums(terms, rows, half):
    swapped = core_swap(terms[half * rows :])
    sums = []
    for member in range(half):
        here = slice(member * rows, (member + 1) * rows)
        sums.append(terms[here].astype(F32) + swapped[here].astype(F32))
    return sums


def group_sum(sums, half, ready=()):
    for bit in reversed(group_bits(half)):
        away = [sums[member + bit].astype(BF16) for member in range(bit)]
        if ready:
            away = lax.optimization_barrier((*away, *ready))[:bit]
        sums = [
            sums[member] + line_swap(away[member], bit).astype(F32) for member in range(bit)
        ]
    return sums[0]


def sum_everywhere(values, sizes):
    for axis, size in sizes:
        bit = 1
        while bit < size:
            values = values + lax.ppermute(values, axis, [(i, i ^ bit) for i in range(size)])
            bit *= 2
    return values


def body(
    tokens,
    segments,
    cotangent,
    attn_norm_gain,
    attn_norm_shift,
    w_query,
    w_key,
    w_value,
    w_gate,
    w_output,
    ffn_norm_gain,
    ffn_norm_shift,
    w_ffn_gate,
    w_ffn_up,
    w_ffn_down,
):
    seq_len = segments.shape[0]
    rows, depth = tokens.shape
    count = seq_len // rows
    half = count // 2
    dp_count = lax.axis_size("dp")
    place = lax.axis_index("tensor")
    core = lax.axis_index("dp") % 2
    hk, hv, ff = w_query.shape[1], w_value.shape[1], w_ffn_gate.shape[1]
    heads = hk // KEY_DIM
    mixer_cols = heads * HEAD_COLS
    mlp_step = min(256, ff)
    head_ids = (place * heads + jnp.arange(heads, dtype=jnp.int32)).astype(F32)
    rates = jnp.log1p(-jnp.exp2(-5.0 - head_ids))
    chips = [list(range(side, dp_count, 2)) for side in range(2)]
    last = count - 1

    def rows_of(stacked):
        return lambda owner, step: lax.dynamic_slice_in_dim(stacked, owner * rows, rows, 0)

    move_a = [(2 * m, m) for m in range(half)] + [(2 * m + 1, m + half) for m in range(half)]
    move_b = [(2 * m + 1, m) for m in range(half)] + [(2 * m, m + half) for m in range(half)]
    straight = core == place // half

    def backwards(pairs):
        return [(to, source) for source, to in pairs]

    residual = tokens.astype(F32)
    normed, first_pull = jax.vjp(layer_norm, residual, attn_norm_gain, attn_norm_shift)
    mixer_full = lax.all_gather(
        pack_mixer(w_query, w_key, w_value, w_gate, w_output, heads), "dp", axis=0, tiled=True
    )
    mlp_shard = pack_mlp(w_ffn_gate, w_ffn_up, w_ffn_down, mlp_step)
    first = Gather(normed.astype(BF16), count)
    for step in range(1, count):
        first.step(*([mlp_shard] if step == 2 else []))
    shard_a = lax.ppermute(after(mlp_shard, *first.arrived(last - 1)), "tensor", move_a)
    shard_b = lax.ppermute(after(mlp_shard, *first.arrived(last)), "tensor", move_b)
    kept = jnp.where(straight, shard_a, shard_b)
    given = core_swap(jnp.where(straight, shard_b, shard_a))
    chip_rows = jnp.where(
        core == 0, jnp.concatenate([kept, given], 0), jnp.concatenate([given, kept], 0)
    )
    mlp_full = lax.all_gather(
        chip_rows, "dp", axis=0, tiled=True, axis_index_groups=chips
    )

    product, whole_normed = project(
        first.slots,
        mixer_full,
        mixer_cols,
        [slot_owner(place, slot, count) for slot in range(count)],
    )
    gated_low, retained = retention(product, segments, rates)
    output_full = mixer_full[:, mixer_cols:]
    mixer = Scatter(rows_of(matmul(gated_low, output_full, 1, 1).astype(BF16)), count)

    cots = [after(cotangent, shard_b)]
    for bit in group_bits(half):
        cots += [line_swap(block, bit) for block in cots]
    cots_other = [core_swap(block) for block in cots]

    for step in range(1, count):
        mixer.step(*(cots if step == 2 else []))
    hidden = residual + mixer.total()
    normed_two, second_pull = jax.vjp(layer_norm, hidden, ffn_norm_gain, ffn_norm_shift)

    seconds = [normed_two.astype(BF16)]
    for bit in group_bits(half):
        seconds += [line_swap(block, bit) for block in seconds]
    seconds_other = [core_swap(block) for block in seconds]
    buffers = ()
    for member in range(half):
        buffers = mlp_blocks(
            (seconds[member], seconds_other[member]),
            (cots[member], cots_other[member]),
            mlp_full,
            member,
            half,
            mlp_step,
            buffers,
        )
    grad_pairs, inner, down_terms, back_terms = (
        array.reshape(seq_len, array.shape[-1]) for array in buffers
    )

    grad_normed_two = group_sum(chip_sums(back_terms, rows, half), half)
    mlp_part = weight_grad(
        jnp.concatenate(seconds + seconds_other, 0), grad_pairs, 0, 3 * ff
    )
    mlp_part = weight_grad(
        jnp.concatenate(cots + cots_other, 0), inner, 2 * ff, 3 * ff, mlp_part
    )
    mlp_grad = lax.psum_scatter(
        after(mlp_part, grad_normed_two),
        "dp",
        scatter_dimension=0,
        tiled=True,
        axis_index_groups=chips,
    )
    grad_from_two, grad_ffn_gain_part, grad_ffn_shift_part = second_pull(grad_normed_two)
    grad_hidden = cotangent.astype(F32) + grad_from_two

    branch = Gather(grad_hidden.astype(BF16), count)
    buffers = ()
    for slot in range(count):
        block = branch.slots[slot]
        if slot < last:
            branch.step(*buffers)
        else:
            block = after(block, *buffers)
        buffers = place_product(
            block,
            mixer_full,
            mixer_cols,
            hv,
            slot_owner(place, slot, count),
            count,
            BF16,
            buffers,
        )
    grad_gated, whole_branch = buffers
    down_sums = chip_sums(after(down_terms, *branch.arrived(1)), rows, half)
    layer_output = (hidden + group_sum(down_sums, half, branch.arrived(last))).astype(BF16)
    grads = retention_back(product, segments, rates, retained, grad_gated)

    normed_terms = []

    def far_of(owner, step):
        index = count - 1 - owner_slot(place, owner, count)
        chosen = normed_terms[0]
        for other in range(1, step):
            chosen = jnp.where(index >= other, normed_terms[other], chosen)
        return chosen

    def columns(grad, groups, first, size):
        stride = grad.shape[1] // groups
        parts = [grad[:, g * stride + first : g * stride + first + size] for g in range(groups)]
        return jnp.concatenate(parts, 1).astype(F32)

    last_scatter = Scatter(far_of, count)
    source = after(grads, layer_output)
    own = lax.dynamic_slice_in_dim(mlp_grad, core * (depth // dp_count), depth // dp_count, 0)
    away = lax.dynamic_slice_in_dim(mlp_grad, (1 - core) * (depth // dp_count), depth // dp_count, 0)
    swapped = core_swap(after(away, grads))
    moved_a = lax.ppermute(jnp.where(straight, own, swapped), "tensor", backwards(move_a))
    moved_b = lax.ppermute(jnp.where(straight, swapped, own), "tensor", backwards(move_b))
    for index in range(count):
        normed_terms.append(
            back_product(source, mixer_full, slot_owner(place, count - 1 - index, count), rows)
        )
        if index < last:
            sent = last_scatter.step(*([moved_a] if index == last - 1 else []))
        if index == 0:
            mixer_part = weight_grad(
                whole_normed, after(grads, normed_terms[0]), 0, mixer_cols + hv
            )
            mixer_part = weight_grad(
                whole_branch, gated_low, mixer_cols, mixer_cols + hv, mixer_part
            )
            source = after(source, mixer_part)
            mixer_grad = dp_scatter(after(mixer_part, *sent))
    mlp_grad = moved_a.astype(F32) + moved_b.astype(F32)
    grad_from_one, grad_attn_gain_part, grad_attn_shift_part = first_pull(last_scatter.total())
    grad_tokens = grad_hidden + grad_from_one

    gains = sum_everywhere(
        jnp.stack(
            [grad_attn_gain_part, grad_attn_shift_part, grad_ffn_gain_part, grad_ffn_shift_part]
        ),
        (("dp", dp_count), ("tensor", count)),
    )
    head_grads, pair_grad = mixer_grad[:, :mixer_cols], mlp_grad[:, : 2 * ff]
    mlp_steps = ff // mlp_step
    return (
        layer_output,
        grad_tokens,
        gains[0],
        gains[1],
        columns(head_grads, heads, 0, KEY_DIM),
        columns(head_grads, heads, KEY_DIM, KEY_DIM),
        columns(head_grads, heads, 2 * KEY_DIM, VALUE_DIM),
        columns(head_grads, heads, 2 * KEY_DIM + VALUE_DIM, VALUE_DIM),
        mixer_grad[:, mixer_cols:].astype(F32).T,
        gains[2],
        gains[3],
        columns(pair_grad, mlp_steps, 0, mlp_step),
        columns(pair_grad, mlp_steps, mlp_step, mlp_step),
        mlp_grad[:, 2 * ff :].T,
    )


def solution(mesh):
    split = P(("dp", "tensor"), None)
    weight = P("dp", "tensor")
    turned = P("tensor", "dp")
    return jax.shard_map(
        body,
        mesh=mesh,
        in_specs=(
            split, P("dp"), split, P(), P(), weight, weight, weight, weight, turned,
            P(), P(), weight, weight, turned,
        ),
        out_specs=(
            split, split, P(), P(), weight, weight, weight, weight, turned,
            P(), P(), weight, weight, turned,
        ),
        check_vma=False,
    )
```

```python
import functools

import jax
import jax.numpy as jnp
from jax import lax
from jax.experimental import pallas as pl
from jax.experimental.pallas import tpu as pltpu
from jax.sharding import PartitionSpec as P

KEY_DIM = 256
VALUE_DIM = 512
HEAD_COLS = 2 * KEY_DIM + 2 * VALUE_DIM
BLOCK = 256
F32 = jnp.float32
BF16 = jnp.bfloat16
MIB = 1024 * 1024


def layer_norm(values, gain, shift):
    centred = values - jnp.mean(values, -1, keepdims=True)
    spread = jnp.mean(centred * centred, -1, keepdims=True)
    return centred * lax.rsqrt(spread + 1e-05) * gain + shift


def matmul(left, right, left_dim=1, right_dim=0):
    return lax.dot_general(
        left, right, (((left_dim,), (right_dim,)), ((), ())), preferred_element_type=F32
    )


def sigmoid(values):
    return 1.0 / (1.0 + jnp.exp(-values))


ERFC_NEAR = (
    2.326819970068386e-2, -1.387039388740657e-1, 3.687424674597105e-1, -5.824733027278666e-1,
    6.210004621745983e-1, -4.944515323274145e-1, 3.404879937665872e-1, -2.741127028184656e-1,
    5.638259427386472e-1,
)
ERFC_FAR = (
    -1.047766399936249e1, 1.297719955372516e1, -7.495518717768503, 2.921019019210786,
    -1.015265279202700, 4.218463358204948e-1, -2.820767439740514e-1, 5.641895067754075e-1,
)


def series(values, coefficients):
    total = jnp.full_like(values, coefficients[0])
    for coefficient in coefficients[1:]:
        total = total * values + coefficient
    return total


def normal_below(values):
    scaled = values * (0.5**0.5)
    size = jnp.abs(scaled)
    bell = jnp.exp(-scaled * scaled)
    inverse = 1.0 / jnp.maximum(size, 1.0)
    square = inverse * inverse
    shape = jnp.where(size < 2.0, series(square, ERFC_NEAR), series(square, ERFC_FAR))
    tail = 0.5 * bell * inverse * shape
    outer = jnp.where(scaled > 0.0, 1.0 - tail, tail)
    return jnp.where(size < 1.0, 0.5 + 0.5 * lax.erf(scaled), outer), bell


def after(value, *others):
    return lax.optimization_barrier((value, *others))[0]


def kernel_params(mib):
    return pltpu.CompilerParams(vmem_limit_bytes=mib * MIB)


def pack_kernel(plan, *refs):
    *parts, out = refs
    for part, first, to, size, turned in plan:
        piece = parts[part][first : first + size, :].T if turned else parts[part][:, first : first + size]
        out[:, to : to + size] = piece


def pack(parts, plan, width):
    height = parts[0].shape[1] if plan[0][4] else parts[0].shape[0]
    return pl.pallas_call(
        functools.partial(pack_kernel, plan),
        out_shape=jax.ShapeDtypeStruct((height, width), BF16),
        cost_estimate=pl.CostEstimate(flops=0, bytes_accessed=4 * height * width, transcendentals=0),
        compiler_params=kernel_params(16),
        name="pack",
    )(*parts)


def pack_mixer(w_query, w_key, w_value, w_gate, heads):
    plan = []
    for head in range(heads):
        to = head * HEAD_COLS
        plan += [
            (0, head * KEY_DIM, to, KEY_DIM, False),
            (1, head * KEY_DIM, to + KEY_DIM, KEY_DIM, False),
            (2, head * VALUE_DIM, to + 2 * KEY_DIM, VALUE_DIM, False),
            (3, head * VALUE_DIM, to + 2 * KEY_DIM + VALUE_DIM, VALUE_DIM, False),
        ]
    return pack([w_query, w_key, w_value, w_gate], tuple(plan), heads * HEAD_COLS)


def pack_turned(weight):
    rows, columns = weight.shape
    return pack([weight], ((0, 0, 0, rows, True),), rows)


def pack_mlp(w_gate, w_up, w_down, step):
    hidden = w_down.shape[0]
    plan = []
    for at in range(0, hidden, step):
        plan += [(0, at, 2 * at, step, False), (1, at, 2 * at + step, step, False)]
    plan.append((2, 0, 2 * hidden, hidden, True))
    return pack([w_gate, w_up, w_down], tuple(plan), 3 * hidden)


def place_kernel(owner, rows_ref, weight_ref, *refs):
    product_ref, kept_ref = refs[-2:]
    product_ref[...] = matmul(rows_ref[...], weight_ref[...]).astype(product_ref.dtype)

    @pl.when(pl.program_id(0) == 0)
    def _():
        kept_ref[...] = rows_ref[...]


def place_product(rows, weight, owner, count, kind, buffers=()):
    height, depth = rows.shape
    width = weight.shape[1]
    step = min(512, width)
    row_spec = pl.BlockSpec((height, depth), lambda j, at: (0, 0))
    in_specs = [row_spec, pl.BlockSpec((depth, step), lambda j, at: (0, j))]
    operands = [owner.reshape(1), rows, weight]
    aliases = {}
    if buffers:
        operands += list(buffers)
        in_specs += [pl.BlockSpec(memory_space=pl.ANY)] * 2
        aliases = {3: 0, 4: 1}
    return pl.pallas_call(
        place_kernel,
        grid_spec=pltpu.PrefetchScalarGridSpec(
            num_scalar_prefetch=1,
            grid=(width // step,),
            in_specs=in_specs,
            out_specs=[
                pl.BlockSpec((height, step), lambda j, at: (at[0], j)),
                pl.BlockSpec((height, depth), lambda j, at: (at[0], 0)),
            ],
        ),
        out_shape=[
            jax.ShapeDtypeStruct((count * height, width), kind),
            jax.ShapeDtypeStruct((count * height, depth), BF16),
        ],
        input_output_aliases=aliases,
        cost_estimate=pl.CostEstimate(
            flops=2 * height * depth * width,
            bytes_accessed=2 * depth * width + 8 * height * width,
            transcendentals=0,
        ),
        compiler_params=kernel_params(12),
        name="place_product",
    )(*operands)


def project_kernel(owners, *refs):
    count = len(refs) - 4
    weight_ref, mixed_ref, gate_ref, kept_ref = refs[count:]
    height = refs[0].shape[0]
    at = pl.program_id(0)
    for slot in range(count):
        here = pl.ds(pl.multiple_of(owners[slot] * height, height), height)
        product = matmul(refs[slot][...], weight_ref[...])

        @pl.when(at % 3 < 2)
        def _(here=here, product=product):
            mixed_ref[here, :] = product.astype(BF16)

        @pl.when(at % 3 == 2)
        def _(here=here, product=product):
            gate_ref[here, :] = product

        @pl.when(at == 0)
        def _(slot=slot, here=here):
            kept_ref[here, :] = refs[slot][...]


def project(slots, weight, owners):
    count = len(slots)
    height, depth = slots[0].shape
    width = weight.shape[1]
    heads = width // HEAD_COLS
    step = VALUE_DIM
    row_spec = pl.BlockSpec((height, depth), lambda j, at: (0, 0))
    return pl.pallas_call(
        project_kernel,
        grid_spec=pltpu.PrefetchScalarGridSpec(
            num_scalar_prefetch=1,
            grid=(3 * heads,),
            in_specs=[row_spec] * count + [pl.BlockSpec((depth, step), lambda j, at: (0, j))],
            out_specs=[
                pl.BlockSpec((count * height, step), lambda j, at: (0, 2 * (j // 3) + jnp.minimum(j % 3, 1))),
                pl.BlockSpec((count * height, step), lambda j, at: (0, j // 3)),
                pl.BlockSpec((count * height, depth), lambda j, at: (0, 0)),
            ],
        ),
        out_shape=[
            jax.ShapeDtypeStruct((count * height, heads * 2 * step), BF16),
            jax.ShapeDtypeStruct((count * height, heads * step), F32),
            jax.ShapeDtypeStruct((count * height, depth), BF16),
        ],
        cost_estimate=pl.CostEstimate(
            flops=2 * count * height * depth * width,
            bytes_accessed=2 * depth * width + 4 * count * height * width,
            transcendentals=0,
        ),
        compiler_params=kernel_params(12 + 4 * count),
        name="project",
    )(jnp.stack(owners), *slots, weight)


def back_kernel(owner, rows_ref, weight_ref, out_ref):
    out_ref[...] = matmul(rows_ref[...], weight_ref[...], 1, 1).astype(out_ref.dtype)


def back_product(source, weight, owner, height):
    depth = source.shape[1]
    width = weight.shape[0]
    step = min(512, width)
    return pl.pallas_call(
        back_kernel,
        grid_spec=pltpu.PrefetchScalarGridSpec(
            num_scalar_prefetch=1,
            grid=(width // step,),
            in_specs=[
                pl.BlockSpec((height, depth), lambda j, at: (at[0], 0)),
                pl.BlockSpec((step, depth), lambda j, at: (j, 0)),
            ],
            out_specs=pl.BlockSpec((height, step), lambda j, at: (0, j)),
        ),
        out_shape=jax.ShapeDtypeStruct((height, width), BF16),
        cost_estimate=pl.CostEstimate(
            flops=2 * height * depth * width,
            bytes_accessed=2 * depth * width + 6 * height * width,
            transcendentals=0,
        ),
        compiler_params=kernel_params(12),
        name="back_product",
    )(owner.reshape(1), source, weight)


def few_kernel(rows_ref, weight_ref, out_ref):
    out_ref[...] = matmul(rows_ref[...], weight_ref[...], 1, 1)


def few_product(rows, weight):
    height, length = rows.shape
    depth = weight.shape[0]
    step = min(512, depth)
    return pl.pallas_call(
        few_kernel,
        grid=(depth // step,),
        in_specs=[
            pl.BlockSpec((height, length), lambda j: (0, 0)),
            pl.BlockSpec((step, length), lambda j: (j, 0)),
        ],
        out_specs=pl.BlockSpec((height, step), lambda j: (0, j)),
        out_shape=jax.ShapeDtypeStruct((height, depth), F32),
        cost_estimate=pl.CostEstimate(
            flops=2 * height * length * depth, bytes_accessed=2 * length * depth, transcendentals=0
        ),
        compiler_params=kernel_params(50),
        name="few_product",
    )(rows, weight)


def decay_block(rate, first, seg_col, seg_row, width):
    height = seg_col.shape[0]
    down = lax.broadcasted_iota(jnp.int32, (height, 1), 0)
    across = lax.broadcasted_iota(jnp.int32, (1, width), 1)
    inside = (down + first >= across) & (seg_col == seg_row)
    factor = jnp.exp(down.astype(F32) * rate) * jnp.exp((first - across).astype(F32) * rate)
    return jnp.where(inside, factor, 0.0)


def retention_kernel(blocks, rates, seg_col, seg_row, query, keys, values, gate, gated, retained):
    head, at = pl.program_id(0), pl.program_id(1)
    height = query.shape[0]

    for block in range(blocks):

        @pl.when(at == block)
        def _(block=block):
            width = (block + 1) * height
            decay = decay_block(rates[head], block * height, seg_col[...], seg_row[:, :width], width)
            scores = matmul(query[...], keys[:width, :], 1, 1)
            mixed = matmul((scores * decay).astype(BF16), values[:width, :])
            retained[...] = mixed
            normal = mixed * lax.rsqrt(jnp.mean(mixed * mixed, -1, keepdims=True) + 1e-06)
            pre = gate[...]
            gated[...] = (pre * sigmoid(pre) * normal).astype(BF16)


def head_specs(seq_len):
    return [
        pl.BlockSpec(memory_space=pltpu.SMEM),
        pl.BlockSpec((BLOCK, 1), lambda h, i: (i, 0)),
        pl.BlockSpec((1, seq_len), lambda h, i: (0, 0)),
        pl.BlockSpec((BLOCK, KEY_DIM), lambda h, i: (i, 4 * h)),
        pl.BlockSpec((seq_len, KEY_DIM), lambda h, i: (0, 4 * h + 1)),
        pl.BlockSpec((seq_len, VALUE_DIM), lambda h, i: (0, 2 * h + 1)),
        pl.BlockSpec((BLOCK, VALUE_DIM), lambda h, i: (i, h)),
    ]


def retention(mixed, gate_pre, segments, rates):
    seq_len = segments.shape[0]
    heads = rates.shape[0]
    blocks = seq_len // BLOCK
    out_spec = pl.BlockSpec((BLOCK, VALUE_DIM), lambda h, i: (i, h))
    return pl.pallas_call(
        functools.partial(retention_kernel, blocks),
        grid=(heads, blocks),
        in_specs=head_specs(seq_len),
        out_specs=[out_spec, out_spec],
        out_shape=[
            jax.ShapeDtypeStruct((seq_len, heads * VALUE_DIM), BF16),
            jax.ShapeDtypeStruct((seq_len, heads * VALUE_DIM), F32),
        ],
        cost_estimate=pl.CostEstimate(
            flops=2 * heads * seq_len * seq_len * (KEY_DIM + VALUE_DIM),
            bytes_accessed=10 * seq_len * heads * HEAD_COLS,
            transcendentals=0,
        ),
        compiler_params=kernel_params(10 + seq_len // 128),
        name="retention",
    )(rates, segments.reshape(seq_len, 1), segments.reshape(1, seq_len), mixed, mixed, mixed, gate_pre)


def retention_back_kernel(
    blocks, rates, seg_col, seg_row, query, keys, values, gate, retained, grad_gated, grads, key_total, value_total
):
    head, at = pl.program_id(0), pl.program_id(1)
    height = query.shape[0]

    @pl.when(at == 0)
    def _():
        key_total[...] = jnp.zeros_like(key_total)
        value_total[...] = jnp.zeros_like(value_total)

    for block in range(blocks):

        @pl.when(at == block)
        def _(block=block):
            width = (block + 1) * height
            here = slice(block * height, width)
            mixed = retained[...]
            scale = lax.rsqrt(jnp.mean(mixed * mixed, -1, keepdims=True) + 1e-06)
            normal = mixed * scale
            pre = gate[...]
            grad = grad_gated[...].astype(F32)
            open_part = sigmoid(pre)
            grads[here, 2 * KEY_DIM + VALUE_DIM :] = (
                grad * normal * (open_part * (1.0 + pre * (1.0 - open_part)))
            ).astype(BF16)
            grad_normal = grad * (pre * open_part)
            grad_mixed = (
                scale * (grad_normal - normal * jnp.mean(grad_normal * normal, -1, keepdims=True))
            ).astype(BF16)
            decay = decay_block(rates[head], block * height, seg_col[...], seg_row[:, :width], width)
            query_low = query[...]
            weights = (matmul(query_low, keys[:width, :], 1, 1) * decay).astype(BF16)
            grad_scores = (matmul(grad_mixed, values[:width, :], 1, 1) * decay).astype(BF16)
            grads[here, :KEY_DIM] = matmul(grad_scores, keys[:width, :]).astype(BF16)
            key_total[:width, :] += matmul(grad_scores, query_low, 0, 0)
            value_total[:width, :] += matmul(weights, grad_mixed, 0, 0)

    @pl.when(at == blocks - 1)
    def _():
        grads[:, KEY_DIM : 2 * KEY_DIM] = key_total[...].astype(BF16)
        grads[:, 2 * KEY_DIM : 2 * KEY_DIM + VALUE_DIM] = value_total[...].astype(BF16)


def retention_back(mixed, gate_pre, segments, rates, retained, grad_gated):
    seq_len = segments.shape[0]
    heads = rates.shape[0]
    blocks = seq_len // BLOCK
    side_spec = pl.BlockSpec((BLOCK, VALUE_DIM), lambda h, i: (i, h))
    return pl.pallas_call(
        functools.partial(retention_back_kernel, blocks),
        grid=(heads, blocks),
        in_specs=head_specs(seq_len) + [side_spec, side_spec],
        out_specs=pl.BlockSpec((seq_len, HEAD_COLS), lambda h, i: (0, h)),
        out_shape=jax.ShapeDtypeStruct((seq_len, heads * HEAD_COLS), BF16),
        scratch_shapes=[
            pltpu.VMEM((seq_len, KEY_DIM), F32),
            pltpu.VMEM((seq_len, VALUE_DIM), F32),
        ],
        cost_estimate=pl.CostEstimate(
            flops=2 * heads * seq_len * seq_len * (3 * KEY_DIM + 2 * VALUE_DIM),
            bytes_accessed=12 * seq_len * heads * HEAD_COLS,
            transcendentals=0,
        ),
        compiler_params=kernel_params(10 + seq_len // 45),
        name="retention_back",
    )(
        rates, segments.reshape(seq_len, 1), segments.reshape(1, seq_len),
        mixed, mixed, mixed, gate_pre, retained, grad_gated,
    )


def mlp_kernel(steps, rows, cot, pair_w, down_w, *refs):
    pair_out, inner_out, down_terms, back_terms, down_total, back_total = refs[-6:]
    at = pl.program_id(0)
    half = down_w.shape[1]
    pair = matmul(rows[...], pair_w[...])
    gate, up = pair[:, :half], pair[:, half:]
    grad_inner = matmul(cot[...], down_w[...]).astype(BF16).astype(F32)
    below, bell = normal_below(gate)
    slope = below + gate * (bell * 0.3989422804014327)
    bent = gate * below
    inner = (bent * up).astype(BF16)
    grad_pair = jnp.concatenate(
        [(grad_inner * up * slope).astype(BF16), (grad_inner * bent).astype(BF16)], 1
    )
    inner_out[...] = inner
    pair_out[...] = grad_pair
    down_part = matmul(inner, down_w[...], 1, 1)
    back_part = matmul(grad_pair, pair_w[...], 1, 1)

    @pl.when(at == 0)
    def _():
        down_total[...] = down_part
        back_total[...] = back_part

    @pl.when(at > 0)
    def _():
        down_total[...] += down_part
        back_total[...] += back_part

    @pl.when(at == steps - 1)
    def _():
        down_terms[...] = down_total[...].astype(down_terms.dtype)
        back_terms[...] = back_total[...].astype(back_terms.dtype)


def mlp_block(rows, cot, weights, slot, count, buffers=()):
    height, depth = rows.shape
    hidden = weights.shape[1] // 3
    step = min(256, hidden)
    steps = hidden // step
    row_spec = pl.BlockSpec((height, depth), lambda j: (0, 0))
    in_specs = [
        row_spec,
        row_spec,
        pl.BlockSpec((depth, 2 * step), lambda j: (0, j)),
        pl.BlockSpec((depth, step), lambda j: (0, 2 * steps + j)),
    ]
    operands = [rows, cot, weights, weights]
    aliases = {}
    if buffers:
        operands += list(buffers)
        in_specs += [pl.BlockSpec(memory_space=pl.ANY)] * 4
        aliases = {4: 0, 5: 1, 6: 2, 7: 3}
    wide_spec = pl.BlockSpec((height, depth), lambda j: (slot, 0))
    return pl.pallas_call(
        functools.partial(mlp_kernel, steps),
        grid=(steps,),
        in_specs=in_specs,
        out_specs=[
            pl.BlockSpec((height, 2 * step), lambda j: (slot, j)),
            pl.BlockSpec((height, step), lambda j: (slot, j)),
            wide_spec,
            wide_spec,
        ],
        out_shape=[
            jax.ShapeDtypeStruct((count * height, 2 * hidden), BF16),
            jax.ShapeDtypeStruct((count * height, hidden), BF16),
            jax.ShapeDtypeStruct((count * height, depth), BF16),
            jax.ShapeDtypeStruct((count * height, depth), BF16),
        ],
        scratch_shapes=[pltpu.VMEM((height, depth), F32)] * 2,
        input_output_aliases=aliases,
        cost_estimate=pl.CostEstimate(
            flops=12 * height * depth * hidden,
            bytes_accessed=6 * depth * hidden + 20 * height * depth,
            transcendentals=0,
        ),
        compiler_params=kernel_params(28),
        name="mlp_block",
    )(*operands)


def weight_grad_kernel(left, right, *refs):
    refs[-1][...] = matmul(left[...], right[...], 0, 0).astype(BF16)


def weight_grad(left, right, first, width, buffer=None):
    length, depth = left.shape
    columns = right.shape[1]
    step = min(512, columns)
    in_specs = [
        pl.BlockSpec((length, depth), lambda j: (0, 0)),
        pl.BlockSpec((length, step), lambda j: (0, j)),
    ]
    operands = [left, right]
    aliases = {}
    if buffer is not None:
        operands.append(buffer)
        in_specs.append(pl.BlockSpec(memory_space=pl.ANY))
        aliases = {2: 0}
    return pl.pallas_call(
        weight_grad_kernel,
        grid=(columns // step,),
        in_specs=in_specs,
        out_specs=pl.BlockSpec((depth, step), lambda j: (0, first // step + j)),
        out_shape=jax.ShapeDtypeStruct((depth, width), BF16),
        input_output_aliases=aliases,
        cost_estimate=pl.CostEstimate(
            flops=2 * length * depth * columns,
            bytes_accessed=2 * length * (depth + columns) + 2 * depth * columns,
            transcendentals=0,
        ),
        compiler_params=kernel_params(16 + length // 64),
        name="weight_grad",
    )(*operands)


class Gather:
    def __init__(self, block, count):
        self.count = count
        self.from_left, self.from_right, self.slots = [block], [block], [block]

    def step(self, *ready):
        count, step = self.count, len(self.slots)
        place = lax.axis_index("tensor")
        left, right = self.from_left[-1], self.from_right[-1]
        if ready:
            left, right = lax.optimization_barrier((left, right, *ready))[:2]
        self.from_left.append(
            lax.ppermute(left, "tensor", [(i, i + 1) for i in range(step - 1, count - 1)])
        )
        self.from_right.append(
            lax.ppermute(right, "tensor", [(i + 1, i) for i in range(count - step)])
        )
        chosen = None
        for owner in range(count):
            rights = count - 1 - owner
            if owner < count // 2:
                wanted = self.from_right[step] if step <= rights else self.from_left[step - rights]
            else:
                wanted = self.from_left[step] if step <= owner else self.from_right[step - owner]
            chosen = wanted if chosen is None else jnp.where(place >= owner, wanted, chosen)
        self.slots.append(chosen)
        return self.arrived(step)

    def arrived(self, step):
        return (self.from_left[step], self.from_right[step])


class Scatter:
    def __init__(self, block_of, count):
        self.block_of, self.count, self.steps = block_of, count, 0
        self.to_right = self.to_left = None

    def step(self, *ready):
        count = self.count
        place = lax.axis_index("tensor")
        self.steps += 1
        step = self.steps
        ahead = count - step
        right = self.block_of(jnp.minimum(place + ahead, count - 1), step).astype(F32)
        left = self.block_of(jnp.maximum(place - ahead, 0), step).astype(F32)
        if step > 1:
            came_right, came_left = lax.optimization_barrier((self.to_right, self.to_left))
            right = right + came_right.astype(F32)
            left = left + came_left.astype(F32)
        right, left = right.astype(BF16), left.astype(BF16)
        if ready:
            right, left = lax.optimization_barrier((right, left, *ready))[:2]
        self.to_right = lax.ppermute(right, "tensor", [(i, i + 1) for i in range(step)])
        self.to_left = lax.ppermute(
            left, "tensor", [(i + 1, i) for i in range(count - 1 - step, count - 1)]
        )
        return (self.to_right, self.to_left)

    def total(self):
        own = self.block_of(lax.axis_index("tensor"), self.count).astype(F32)
        if self.steps:
            own = own + (self.to_right.astype(F32) + self.to_left.astype(F32))
        return own


def slot_owner(place, slot, count):
    rights = count - 1 - place
    first_half = jnp.where(slot <= rights, place + slot, place - (slot - rights))
    second_half = jnp.where(slot <= place, place - slot, slot)
    return jnp.where(place < count // 2, first_half, second_half)


def owner_slot(place, owner, count):
    rights = count - 1 - place
    first_half = jnp.where(owner >= place, owner - place, rights + place - owner)
    second_half = jnp.where(owner <= place, place - owner, owner)
    return jnp.where(place < count // 2, first_half, second_half)


def dp_scatter(part):
    return lax.psum_scatter(part, "dp", scatter_dimension=0, tiled=True)


DOCUMENTS = 3
FEW = 16


def few_rows(stacked, positions):
    picked = [lax.dynamic_slice_in_dim(stacked, position, 1, 0) for position in positions]
    picked.append(jnp.zeros((FEW - len(picked), stacked.shape[1]), stacked.dtype))
    return jnp.concatenate(picked, 0)


def with_rows(total, exact, positions):
    here = lax.broadcasted_iota(jnp.int32, (total.shape[0], 1), 0)
    for number, position in enumerate(positions):
        total = jnp.where(here == position, exact[number : number + 1], total)
    return total


def line_swap(block, bit):
    return lax.ppermute(block, "tensor", [(i, i ^ bit) for i in range(lax.axis_size("tensor"))])


def sum_everywhere(values, sizes):
    for axis, size in sizes:
        bit = 1
        while bit < size:
            values = values + lax.ppermute(values, axis, [(i, i ^ bit) for i in range(size)])
            bit *= 2
    return values


def body(
    tokens,
    segments,
    cotangent,
    attn_norm_gain,
    attn_norm_shift,
    w_query,
    w_key,
    w_value,
    w_gate,
    w_output,
    ffn_norm_gain,
    ffn_norm_shift,
    w_ffn_gate,
    w_ffn_up,
    w_ffn_down,
):
    seq_len = segments.shape[0]
    rows = tokens.shape[0]
    count = seq_len // rows
    dp_count = lax.axis_size("dp")
    place = lax.axis_index("tensor")
    hk = w_query.shape[1]
    ff = w_ffn_gate.shape[1]
    heads = hk // KEY_DIM
    mlp_step = min(256, ff)
    mlp_steps = ff // mlp_step
    head_ids = (place * heads + jnp.arange(heads, dtype=jnp.int32)).astype(F32)
    rates = jnp.log1p(-jnp.exp2(-5.0 - head_ids))

    def rows_of(stacked):
        return lambda owner, step: lax.dynamic_slice_in_dim(stacked, owner * rows, rows, 0)

    def slots_of(stacked):
        return lambda owner, step: rows_of(stacked)(owner_slot(place, owner, count), step)

    starts = [
        jnp.sum((segments < segments[0] + number).astype(jnp.int32)) for number in range(DOCUMENTS)
    ]
    own_starts = [start - place * rows for start in starts]

    last = count - 1
    residual = tokens.astype(F32)
    normed, first_pull = jax.vjp(layer_norm, residual, attn_norm_gain, attn_norm_shift)
    mixer_full = lax.all_gather(
        pack_mixer(w_query, w_key, w_value, w_gate, heads), "dp", axis=0, tiled=True
    )
    output_turned = pack_turned(w_output)
    ffn_shard = pack_mlp(w_ffn_gate, w_ffn_up, w_ffn_down, mlp_step)
    first = Gather(normed.astype(BF16), count)
    for step in range(1, count):
        first.step(*([output_turned, ffn_shard] if step == 2 else []))
    output_full = lax.all_gather(
        after(output_turned, *first.arrived(1)), "dp", axis=0, tiled=True
    )
    ffn_full = lax.all_gather(
        after(ffn_shard, *first.arrived(min(2, last))), "dp", axis=0, tiled=True
    )

    mixed, gate_pre, whole_normed = project(
        first.slots, mixer_full, [slot_owner(place, slot, count) for slot in range(count)]
    )

    cots = Gather(cotangent, count)
    cots.step(*first.arrived(last))
    gated_low, retained = retention(mixed, gate_pre, segments, rates)
    mixer = Scatter(rows_of(matmul(gated_low, output_full, 1, 1).astype(BF16)), count)
    exact = few_product(few_rows(gated_low, starts), output_full)
    bit = 1
    for step in range(1, count):
        mixer.step(*cots.arrived(step), *([exact] if step > 1 else []))
        if step < last:
            cots.step()
        if bit < count:
            exact = exact + line_swap(exact, bit)
            bit *= 2
    hidden = residual + with_rows(mixer.total(), exact, own_starts)
    normed_two, second_pull = jax.vjp(layer_norm, hidden, ffn_norm_gain, ffn_norm_shift)

    second = Gather(normed_two.astype(BF16), count)
    buffers = ()
    for slot in range(count):
        block = second.slots[slot]
        if slot < last:
            second.step(*buffers)
        else:
            block = after(block, *buffers)
        buffers = mlp_block(block, cots.slots[slot], ffn_full, slot, count, buffers)
    grad_pairs, inner, down_terms, back_terms = buffers

    slot_starts = [
        owner_slot(place, start // rows, count) * rows + start % rows for start in starts
    ]
    back = Scatter(slots_of(back_terms), count)
    exact = few_product(few_rows(grad_pairs, slot_starts), ffn_full)
    started = back.step()
    exact = exact + line_swap(exact, 1)
    mlp_part = weight_grad(jnp.concatenate(second.slots, 0), grad_pairs, 0, 3 * ff)
    mlp_part = weight_grad(jnp.concatenate(cots.slots, 0), inner, 2 * ff, 3 * ff, mlp_part)
    mlp_grad = dp_scatter(after(mlp_part, *started))
    bit = 2
    for step in range(2, count):
        back.step(exact, mlp_part)
        if bit < count:
            exact = exact + line_swap(exact, bit)
            bit *= 2
    grad_normed_two = with_rows(back.total(), exact, own_starts)
    grad_from_two, grad_ffn_gain_part, grad_ffn_shift_part = second_pull(grad_normed_two)
    grad_hidden = cotangent.astype(F32) + grad_from_two

    branch = Gather(grad_hidden.astype(BF16), count)
    down = Scatter(slots_of(down_terms), count)
    buffers, sent = (), ()
    for slot in range(count):
        block = branch.slots[slot]
        if slot < last:
            branch.step(*buffers)
        block = after(block, *buffers, *sent)
        if 0 < slot < last:
            sent = down.step(*branch.arrived(slot))
        buffers = place_product(
            block, output_full, slot_owner(place, slot, count), count, BF16, buffers
        )
    grad_gated, whole_branch = buffers
    output_part = weight_grad(whole_branch, gated_low, 0, gated_low.shape[1])
    output_grad = dp_scatter(output_part)
    sent = down.step()
    layer_output = (hidden + down.total()).astype(BF16)
    grads = retention_back(
        mixed, gate_pre, segments, rates, retained, after(grad_gated, output_part, mlp_grad)
    )
    mixer_part = weight_grad(whole_normed, grads, 0, grads.shape[1])
    mixer_grad = dp_scatter(after(mixer_part, *sent))

    normed_terms = []

    def far_of(owner, step):
        index = count - 1 - owner_slot(place, owner, count)
        chosen = normed_terms[0]
        for other in range(1, step):
            chosen = jnp.where(index >= other, normed_terms[other], chosen)
        return chosen

    def columns(grad, groups, first, size):
        stride = grad.shape[1] // groups
        parts = [grad[:, g * stride + first : g * stride + first + size] for g in range(groups)]
        return jnp.concatenate(parts, 1).astype(F32)

    pair_grad = mlp_grad[:, : 2 * ff]
    done_early = (
        layer_output,
        columns(pair_grad, mlp_steps, 0, mlp_step),
        columns(pair_grad, mlp_steps, mlp_step, mlp_step),
        mlp_grad[:, 2 * ff :].astype(F32).T,
        output_grad.astype(F32).T,
    )
    last_scatter = Scatter(far_of, count)
    source = after(grads, mixer_part, *sent)
    for index in range(count):
        normed_terms.append(
            back_product(source, mixer_full, slot_owner(place, count - 1 - index, count), rows)
        )
        if index < last:
            last_scatter.step()
    grad_normed = after(last_scatter.total(), *done_early)
    grad_from_one, grad_attn_gain_part, grad_attn_shift_part = first_pull(grad_normed)
    grad_tokens = grad_hidden + grad_from_one

    gains = sum_everywhere(
        jnp.stack(
            [grad_attn_gain_part, grad_attn_shift_part, grad_ffn_gain_part, grad_ffn_shift_part]
        ),
        (("dp", dp_count), ("tensor", count)),
    )

    mixer_grad = after(mixer_grad, gains)
    return (
        layer_output,
        grad_tokens,
        gains[0],
        gains[1],
        columns(mixer_grad, heads, 0, KEY_DIM),
        columns(mixer_grad, heads, KEY_DIM, KEY_DIM),
        columns(mixer_grad, heads, 2 * KEY_DIM, VALUE_DIM),
        columns(mixer_grad, heads, 2 * KEY_DIM + VALUE_DIM, VALUE_DIM),
        done_early[4],
        gains[2],
        gains[3],
        *done_early[1:4],
    )


def solution(mesh):
    split = P(("dp", "tensor"), None)
    weight = P("dp", "tensor")
    turned = P("tensor", "dp")
    return jax.shard_map(
        body,
        mesh=mesh,
        in_specs=(
            split, P("dp"), split, P(), P(), weight, weight, weight, weight, turned,
            P(), P(), weight, weight, turned,
        ),
        out_specs=(
            split, split, P(), P(), weight, weight, weight, weight, turned,
            P(), P(), weight, weight, turned,
        ),
        check_vma=False,
    )
```

```python
import functools

import jax
import jax.numpy as jnp
from jax import lax
from jax.experimental import pallas as pl
from jax.experimental.pallas import tpu as pltpu
from jax.sharding import PartitionSpec as P

KEY_DIM = 256
VALUE_DIM = 512
HEAD_COLS = 2 * KEY_DIM + 2 * VALUE_DIM
BLOCK = 256
F32 = jnp.float32
BF16 = jnp.bfloat16
MIB = 1024 * 1024


def layer_norm(values, gain, shift):
    centred = values - jnp.mean(values, -1, keepdims=True)
    spread = jnp.mean(centred * centred, -1, keepdims=True)
    return centred * lax.rsqrt(spread + 1e-05) * gain + shift


def matmul(left, right, left_dim=1, right_dim=0):
    return lax.dot_general(
        left, right, (((left_dim,), (right_dim,)), ((), ())), preferred_element_type=F32
    )


def sigmoid(values):
    return 1.0 / (1.0 + jnp.exp(-values))


ERFC_NEAR = (
    2.326819970068386e-2, -1.387039388740657e-1, 3.687424674597105e-1, -5.824733027278666e-1,
    6.210004621745983e-1, -4.944515323274145e-1, 3.404879937665872e-1, -2.741127028184656e-1,
    5.638259427386472e-1,
)
ERFC_FAR = (
    -1.047766399936249e1, 1.297719955372516e1, -7.495518717768503, 2.921019019210786,
    -1.015265279202700, 4.218463358204948e-1, -2.820767439740514e-1, 5.641895067754075e-1,
)


def series(values, coefficients):
    total = jnp.full_like(values, coefficients[0])
    for coefficient in coefficients[1:]:
        total = total * values + coefficient
    return total


def normal_below(values):
    scaled = values * (0.5**0.5)
    size = jnp.abs(scaled)
    bell = jnp.exp(-scaled * scaled)
    inverse = 1.0 / jnp.maximum(size, 1.0)
    square = inverse * inverse
    shape = jnp.where(size < 2.0, series(square, ERFC_NEAR), series(square, ERFC_FAR))
    tail = 0.5 * bell * inverse * shape
    outer = jnp.where(scaled > 0.0, 1.0 - tail, tail)
    return jnp.where(size < 1.0, 0.5 + 0.5 * lax.erf(scaled), outer), bell


def after(value, *others):
    return lax.optimization_barrier((value, *others))[0]


def kernel_params(mib):
    return pltpu.CompilerParams(vmem_limit_bytes=mib * MIB)


def pack_kernel(plan, *refs):
    *parts, out = refs
    for part, first, to, size, turned in plan:
        piece = parts[part][first : first + size, :].T if turned else parts[part][:, first : first + size]
        out[:, to : to + size] = piece


def pack(parts, plan, width):
    height = parts[0].shape[1] if plan[0][4] else parts[0].shape[0]
    return pl.pallas_call(
        functools.partial(pack_kernel, plan),
        out_shape=jax.ShapeDtypeStruct((height, width), BF16),
        cost_estimate=pl.CostEstimate(flops=0, bytes_accessed=4 * height * width, transcendentals=0),
        compiler_params=kernel_params(16),
        name="pack",
    )(*parts)


def pack_mixer(w_query, w_key, w_value, w_gate, heads):
    plan = []
    for head in range(heads):
        to = head * HEAD_COLS
        plan += [
            (0, head * KEY_DIM, to, KEY_DIM, False),
            (1, head * KEY_DIM, to + KEY_DIM, KEY_DIM, False),
            (2, head * VALUE_DIM, to + 2 * KEY_DIM, VALUE_DIM, False),
            (3, head * VALUE_DIM, to + 2 * KEY_DIM + VALUE_DIM, VALUE_DIM, False),
        ]
    return pack([w_query, w_key, w_value, w_gate], tuple(plan), heads * HEAD_COLS)


def pack_turned(weight):
    rows, columns = weight.shape
    return pack([weight], ((0, 0, 0, rows, True),), rows)


def pack_mlp(w_gate, w_up, w_down, step):
    hidden = w_down.shape[0]
    plan = []
    for at in range(0, hidden, step):
        plan += [(0, at, 2 * at, step, False), (1, at, 2 * at + step, step, False)]
    plan.append((2, 0, 2 * hidden, hidden, True))
    return pack([w_gate, w_up, w_down], tuple(plan), 3 * hidden)


def place_kernel(owner, rows_ref, weight_ref, *refs):
    product_ref, kept_ref = refs[-2:]
    product_ref[...] = matmul(rows_ref[...], weight_ref[...]).astype(product_ref.dtype)

    @pl.when(pl.program_id(0) == 0)
    def _():
        kept_ref[...] = rows_ref[...]


def place_product(rows, weight, owner, count, kind, buffers=()):
    height, depth = rows.shape
    width = weight.shape[1]
    step = min(512, width)
    row_spec = pl.BlockSpec((height, depth), lambda j, at: (0, 0))
    in_specs = [row_spec, pl.BlockSpec((depth, step), lambda j, at: (0, j))]
    operands = [owner.reshape(1), rows, weight]
    aliases = {}
    if buffers:
        operands += list(buffers)
        in_specs += [pl.BlockSpec(memory_space=pl.ANY)] * 2
        aliases = {3: 0, 4: 1}
    return pl.pallas_call(
        place_kernel,
        grid_spec=pltpu.PrefetchScalarGridSpec(
            num_scalar_prefetch=1,
            grid=(width // step,),
            in_specs=in_specs,
            out_specs=[
                pl.BlockSpec((height, step), lambda j, at: (at[0], j)),
                pl.BlockSpec((height, depth), lambda j, at: (at[0], 0)),
            ],
        ),
        out_shape=[
            jax.ShapeDtypeStruct((count * height, width), kind),
            jax.ShapeDtypeStruct((count * height, depth), BF16),
        ],
        input_output_aliases=aliases,
        cost_estimate=pl.CostEstimate(
            flops=2 * height * depth * width,
            bytes_accessed=2 * depth * width + 8 * height * width,
            transcendentals=0,
        ),
        compiler_params=kernel_params(12),
        name="place_product",
    )(*operands)


def project_kernel(owners, *refs):
    count = len(refs) - 4
    weight_ref, mixed_ref, gate_ref, kept_ref = refs[count:]
    height = refs[0].shape[0]
    at = pl.program_id(0)
    for slot in range(count):
        here = pl.ds(pl.multiple_of(owners[slot] * height, height), height)
        product = matmul(refs[slot][...], weight_ref[...])

        @pl.when(at % 3 < 2)
        def _(here=here, product=product):
            mixed_ref[here, :] = product.astype(BF16)

        @pl.when(at % 3 == 2)
        def _(here=here, product=product):
            gate_ref[here, :] = product

        @pl.when(at == 0)
        def _(slot=slot, here=here):
            kept_ref[here, :] = refs[slot][...]


def project(slots, weight, owners):
    count = len(slots)
    height, depth = slots[0].shape
    width = weight.shape[1]
    heads = width // HEAD_COLS
    step = VALUE_DIM
    row_spec = pl.BlockSpec((height, depth), lambda j, at: (0, 0))
    return pl.pallas_call(
        project_kernel,
        grid_spec=pltpu.PrefetchScalarGridSpec(
            num_scalar_prefetch=1,
            grid=(3 * heads,),
            in_specs=[row_spec] * count + [pl.BlockSpec((depth, step), lambda j, at: (0, j))],
            out_specs=[
                pl.BlockSpec((count * height, step), lambda j, at: (0, 2 * (j // 3) + jnp.minimum(j % 3, 1))),
                pl.BlockSpec((count * height, step), lambda j, at: (0, j // 3)),
                pl.BlockSpec((count * height, depth), lambda j, at: (0, 0)),
            ],
        ),
        out_shape=[
            jax.ShapeDtypeStruct((count * height, heads * 2 * step), BF16),
            jax.ShapeDtypeStruct((count * height, heads * step), F32),
            jax.ShapeDtypeStruct((count * height, depth), BF16),
        ],
        cost_estimate=pl.CostEstimate(
            flops=2 * count * height * depth * width,
            bytes_accessed=2 * depth * width + 4 * count * height * width,
            transcendentals=0,
        ),
        compiler_params=kernel_params(max(52, 12 + 4 * count)),
        name="project",
    )(jnp.stack(owners), *slots, weight)


def back_kernel(owner, rows_ref, weight_ref, out_ref):
    out_ref[...] = matmul(rows_ref[...], weight_ref[...], 1, 1).astype(out_ref.dtype)


def back_product(source, weight, owner, height):
    depth = source.shape[1]
    width = weight.shape[0]
    step = min(512, width)
    return pl.pallas_call(
        back_kernel,
        grid_spec=pltpu.PrefetchScalarGridSpec(
            num_scalar_prefetch=1,
            grid=(width // step,),
            in_specs=[
                pl.BlockSpec((height, depth), lambda j, at: (at[0], 0)),
                pl.BlockSpec((step, depth), lambda j, at: (j, 0)),
            ],
            out_specs=pl.BlockSpec((height, step), lambda j, at: (0, j)),
        ),
        out_shape=jax.ShapeDtypeStruct((height, width), BF16),
        cost_estimate=pl.CostEstimate(
            flops=2 * height * depth * width,
            bytes_accessed=2 * depth * width + 6 * height * width,
            transcendentals=0,
        ),
        compiler_params=kernel_params(50),
        name="back_product",
    )(owner.reshape(1), source, weight)


def few_kernel(rows_ref, weight_ref, out_ref):
    out_ref[...] = matmul(rows_ref[...], weight_ref[...], 1, 1)


def few_product(rows, weight):
    height, length = rows.shape
    depth = weight.shape[0]
    step = min(512, depth)
    return pl.pallas_call(
        few_kernel,
        grid=(depth // step,),
        in_specs=[
            pl.BlockSpec((height, length), lambda j: (0, 0)),
            pl.BlockSpec((step, length), lambda j: (j, 0)),
        ],
        out_specs=pl.BlockSpec((height, step), lambda j: (0, j)),
        out_shape=jax.ShapeDtypeStruct((height, depth), F32),
        cost_estimate=pl.CostEstimate(
            flops=2 * height * length * depth, bytes_accessed=2 * length * depth, transcendentals=0
        ),
        compiler_params=kernel_params(50),
        name="few_product",
    )(rows, weight)


def decay_block(rate, first, seg_col, seg_row, width):
    height = seg_col.shape[0]
    down = lax.broadcasted_iota(jnp.int32, (height, 1), 0)
    across = lax.broadcasted_iota(jnp.int32, (1, width), 1)
    inside = (down + first >= across) & (seg_col == seg_row)
    factor = jnp.exp(down.astype(F32) * rate) * jnp.exp((first - across).astype(F32) * rate)
    return jnp.where(inside, factor, 0.0)


def retention_kernel(blocks, rates, seg_col, seg_row, query, keys, values, gate, gated, retained):
    head, at = pl.program_id(0), pl.program_id(1)
    height = query.shape[0]

    for block in range(blocks):

        @pl.when(at == block)
        def _(block=block):
            width = (block + 1) * height
            decay = decay_block(rates[head], block * height, seg_col[...], seg_row[:, :width], width)
            scores = matmul(query[...], keys[:width, :], 1, 1)
            mixed = matmul((scores * decay).astype(BF16), values[:width, :])
            retained[...] = mixed
            normal = mixed * lax.rsqrt(jnp.mean(mixed * mixed, -1, keepdims=True) + 1e-06)
            pre = gate[...]
            gated[...] = (pre * sigmoid(pre) * normal).astype(BF16)


def head_specs(seq_len):
    return [
        pl.BlockSpec(memory_space=pltpu.SMEM),
        pl.BlockSpec((BLOCK, 1), lambda h, i: (i, 0)),
        pl.BlockSpec((1, seq_len), lambda h, i: (0, 0)),
        pl.BlockSpec((BLOCK, KEY_DIM), lambda h, i: (i, 4 * h)),
        pl.BlockSpec((seq_len, KEY_DIM), lambda h, i: (0, 4 * h + 1)),
        pl.BlockSpec((seq_len, VALUE_DIM), lambda h, i: (0, 2 * h + 1)),
        pl.BlockSpec((BLOCK, VALUE_DIM), lambda h, i: (i, h)),
    ]


def retention(mixed, gate_pre, segments, rates):
    seq_len = segments.shape[0]
    heads = rates.shape[0]
    blocks = seq_len // BLOCK
    out_spec = pl.BlockSpec((BLOCK, VALUE_DIM), lambda h, i: (i, h))
    return pl.pallas_call(
        functools.partial(retention_kernel, blocks),
        grid=(heads, blocks),
        in_specs=head_specs(seq_len),
        out_specs=[out_spec, out_spec],
        out_shape=[
            jax.ShapeDtypeStruct((seq_len, heads * VALUE_DIM), BF16),
            jax.ShapeDtypeStruct((seq_len, heads * VALUE_DIM), F32),
        ],
        cost_estimate=pl.CostEstimate(
            flops=2 * heads * seq_len * seq_len * (KEY_DIM + VALUE_DIM),
            bytes_accessed=10 * seq_len * heads * HEAD_COLS,
            transcendentals=0,
        ),
        compiler_params=kernel_params(50),
        name="retention",
    )(rates, segments.reshape(seq_len, 1), segments.reshape(1, seq_len), mixed, mixed, mixed, gate_pre)


def retention_back_kernel(
    blocks, rates, seg_col, seg_row, query, keys, values, gate, retained, grad_gated, grads, key_total, value_total
):
    head, at = pl.program_id(0), pl.program_id(1)
    height = query.shape[0]

    @pl.when(at == 0)
    def _():
        key_total[...] = jnp.zeros_like(key_total)
        value_total[...] = jnp.zeros_like(value_total)

    for block in range(blocks):

        @pl.when(at == block)
        def _(block=block):
            width = (block + 1) * height
            here = slice(block * height, width)
            mixed = retained[...]
            scale = lax.rsqrt(jnp.mean(mixed * mixed, -1, keepdims=True) + 1e-06)
            normal = mixed * scale
            pre = gate[...]
            grad = grad_gated[...].astype(F32)
            open_part = sigmoid(pre)
            grads[here, 2 * KEY_DIM + VALUE_DIM :] = (
                grad * normal * (open_part * (1.0 + pre * (1.0 - open_part)))
            ).astype(BF16)
            grad_normal = grad * (pre * open_part)
            grad_mixed = (
                scale * (grad_normal - normal * jnp.mean(grad_normal * normal, -1, keepdims=True))
            ).astype(BF16)
            decay = decay_block(rates[head], block * height, seg_col[...], seg_row[:, :width], width)
            query_low = query[...]
            weights = (matmul(query_low, keys[:width, :], 1, 1) * decay).astype(BF16)
            grad_scores = (matmul(grad_mixed, values[:width, :], 1, 1) * decay).astype(BF16)
            grads[here, :KEY_DIM] = matmul(grad_scores, keys[:width, :]).astype(BF16)
            key_total[:width, :] += matmul(grad_scores, query_low, 0, 0)
            value_total[:width, :] += matmul(weights, grad_mixed, 0, 0)

    @pl.when(at == blocks - 1)
    def _():
        grads[:, KEY_DIM : 2 * KEY_DIM] = key_total[...].astype(BF16)
        grads[:, 2 * KEY_DIM : 2 * KEY_DIM + VALUE_DIM] = value_total[...].astype(BF16)


def retention_back(mixed, gate_pre, segments, rates, retained, grad_gated):
    seq_len = segments.shape[0]
    heads = rates.shape[0]
    blocks = seq_len // BLOCK
    side_spec = pl.BlockSpec((BLOCK, VALUE_DIM), lambda h, i: (i, h))
    return pl.pallas_call(
        functools.partial(retention_back_kernel, blocks),
        grid=(heads, blocks),
        in_specs=head_specs(seq_len) + [side_spec, side_spec],
        out_specs=pl.BlockSpec((seq_len, HEAD_COLS), lambda h, i: (0, h)),
        out_shape=jax.ShapeDtypeStruct((seq_len, heads * HEAD_COLS), BF16),
        scratch_shapes=[
            pltpu.VMEM((seq_len, KEY_DIM), F32),
            pltpu.VMEM((seq_len, VALUE_DIM), F32),
        ],
        cost_estimate=pl.CostEstimate(
            flops=2 * heads * seq_len * seq_len * (3 * KEY_DIM + 2 * VALUE_DIM),
            bytes_accessed=12 * seq_len * heads * HEAD_COLS,
            transcendentals=0,
        ),
        compiler_params=kernel_params(max(50, 10 + seq_len // 45)),
        name="retention_back",
    )(
        rates, segments.reshape(seq_len, 1), segments.reshape(1, seq_len),
        mixed, mixed, mixed, gate_pre, retained, grad_gated,
    )


def mlp_kernel(steps, rows, cot, pair_w, down_w, *refs):
    pair_out, inner_out, down_terms, back_terms, down_total, back_total = refs[-6:]
    at = pl.program_id(0)
    half = down_w.shape[1]
    pair = matmul(rows[...], pair_w[...])
    gate, up = pair[:, :half], pair[:, half:]
    grad_inner = matmul(cot[...], down_w[...]).astype(BF16).astype(F32)
    below, bell = normal_below(gate)
    slope = below + gate * (bell * 0.3989422804014327)
    bent = gate * below
    inner = (bent * up).astype(BF16)
    grad_pair = jnp.concatenate(
        [(grad_inner * up * slope).astype(BF16), (grad_inner * bent).astype(BF16)], 1
    )
    inner_out[...] = inner
    pair_out[...] = grad_pair
    down_part = matmul(inner, down_w[...], 1, 1)
    back_part = matmul(grad_pair, pair_w[...], 1, 1)

    @pl.when(at == 0)
    def _():
        down_total[...] = down_part
        back_total[...] = back_part

    @pl.when(at > 0)
    def _():
        down_total[...] += down_part
        back_total[...] += back_part

    @pl.when(at == steps - 1)
    def _():
        down_terms[...] = down_total[...].astype(down_terms.dtype)
        back_terms[...] = back_total[...].astype(back_terms.dtype)


def mlp_block(rows, cot, weights, slot, count, buffers=()):
    height, depth = rows.shape
    hidden = weights.shape[1] // 3
    step = min(256, hidden)
    steps = hidden // step
    row_spec = pl.BlockSpec((height, depth), lambda j: (0, 0))
    in_specs = [
        row_spec,
        row_spec,
        pl.BlockSpec((depth, 2 * step), lambda j: (0, j)),
        pl.BlockSpec((depth, step), lambda j: (0, 2 * steps + j)),
    ]
    operands = [rows, cot, weights, weights]
    aliases = {}
    if buffers:
        operands += list(buffers)
        in_specs += [pl.BlockSpec(memory_space=pl.ANY)] * 4
        aliases = {4: 0, 5: 1, 6: 2, 7: 3}
    wide_spec = pl.BlockSpec((height, depth), lambda j: (slot, 0))
    return pl.pallas_call(
        functools.partial(mlp_kernel, steps),
        grid=(steps,),
        in_specs=in_specs,
        out_specs=[
            pl.BlockSpec((height, 2 * step), lambda j: (slot, j)),
            pl.BlockSpec((height, step), lambda j: (slot, j)),
            wide_spec,
            wide_spec,
        ],
        out_shape=[
            jax.ShapeDtypeStruct((count * height, 2 * hidden), BF16),
            jax.ShapeDtypeStruct((count * height, hidden), BF16),
            jax.ShapeDtypeStruct((count * height, depth), BF16),
            jax.ShapeDtypeStruct((count * height, depth), BF16),
        ],
        scratch_shapes=[pltpu.VMEM((height, depth), F32)] * 2,
        input_output_aliases=aliases,
        cost_estimate=pl.CostEstimate(
            flops=12 * height * depth * hidden,
            bytes_accessed=6 * depth * hidden + 20 * height * depth,
            transcendentals=0,
        ),
        compiler_params=kernel_params(28),
        name="mlp_block",
    )(*operands)


def weight_grad_kernel(left, right, *refs):
    refs[-1][...] = matmul(left[...], right[...], 0, 0).astype(BF16)


def weight_grad(left, right, first, width, buffer=None):
    length, depth = left.shape
    columns = right.shape[1]
    step = min(512, columns)
    in_specs = [
        pl.BlockSpec((length, depth), lambda j: (0, 0)),
        pl.BlockSpec((length, step), lambda j: (0, j)),
    ]
    operands = [left, right]
    aliases = {}
    if buffer is not None:
        operands.append(buffer)
        in_specs.append(pl.BlockSpec(memory_space=pl.ANY))
        aliases = {2: 0}
    return pl.pallas_call(
        weight_grad_kernel,
        grid=(columns // step,),
        in_specs=in_specs,
        out_specs=pl.BlockSpec((depth, step), lambda j: (0, first // step + j)),
        out_shape=jax.ShapeDtypeStruct((depth, width), BF16),
        input_output_aliases=aliases,
        cost_estimate=pl.CostEstimate(
            flops=2 * length * depth * columns,
            bytes_accessed=2 * length * (depth + columns) + 2 * depth * columns,
            transcendentals=0,
        ),
        compiler_params=kernel_params(16 + length // 64),
        name="weight_grad",
    )(*operands)


class Gather:
    def __init__(self, block, count):
        self.count = count
        self.from_left, self.from_right, self.slots = [block], [block], [block]

    def step(self, *ready):
        count, step = self.count, len(self.slots)
        place = lax.axis_index("tensor")
        left, right = self.from_left[-1], self.from_right[-1]
        if ready:
            left, right = lax.optimization_barrier((left, right, *ready))[:2]
        self.from_left.append(
            lax.ppermute(left, "tensor", [(i, i + 1) for i in range(step - 1, count - 1)])
        )
        self.from_right.append(
            lax.ppermute(right, "tensor", [(i + 1, i) for i in range(count - step)])
        )
        chosen = None
        for owner in range(count):
            rights = count - 1 - owner
            if owner < count // 2:
                wanted = self.from_right[step] if step <= rights else self.from_left[step - rights]
            else:
                wanted = self.from_left[step] if step <= owner else self.from_right[step - owner]
            chosen = wanted if chosen is None else jnp.where(place >= owner, wanted, chosen)
        self.slots.append(chosen)
        return self.arrived(step)

    def arrived(self, step):
        return (self.from_left[step], self.from_right[step])


class Scatter:
    def __init__(self, block_of, count):
        self.block_of, self.count, self.steps = block_of, count, 0
        self.to_right = self.to_left = None

    def step(self, *ready):
        count = self.count
        place = lax.axis_index("tensor")
        self.steps += 1
        step = self.steps
        ahead = count - step
        right = self.block_of(jnp.minimum(place + ahead, count - 1), step).astype(F32)
        left = self.block_of(jnp.maximum(place - ahead, 0), step).astype(F32)
        if step > 1:
            came_right, came_left = lax.optimization_barrier((self.to_right, self.to_left))
            right = right + came_right.astype(F32)
            left = left + came_left.astype(F32)
        right, left = right.astype(BF16), left.astype(BF16)
        if ready:
            right, left = lax.optimization_barrier((right, left, *ready))[:2]
        self.to_right = lax.ppermute(right, "tensor", [(i, i + 1) for i in range(step)])
        self.to_left = lax.ppermute(
            left, "tensor", [(i + 1, i) for i in range(count - 1 - step, count - 1)]
        )
        return (self.to_right, self.to_left)

    def total(self):
        own = self.block_of(lax.axis_index("tensor"), self.count).astype(F32)
        if self.steps:
            own = own + (self.to_right.astype(F32) + self.to_left.astype(F32))
        return own


def slot_owner(place, slot, count):
    rights = count - 1 - place
    first_half = jnp.where(slot <= rights, place + slot, place - (slot - rights))
    second_half = jnp.where(slot <= place, place - slot, slot)
    return jnp.where(place < count // 2, first_half, second_half)


def owner_slot(place, owner, count):
    rights = count - 1 - place
    first_half = jnp.where(owner >= place, owner - place, rights + place - owner)
    second_half = jnp.where(owner <= place, place - owner, owner)
    return jnp.where(place < count // 2, first_half, second_half)


def dp_scatter(part):
    return lax.psum_scatter(part, "dp", scatter_dimension=0, tiled=True)


DOCUMENTS = 3
FEW = 16


def few_rows(stacked, positions):
    picked = [lax.dynamic_slice_in_dim(stacked, position, 1, 0) for position in positions]
    picked.append(jnp.zeros((FEW - len(picked), stacked.shape[1]), stacked.dtype))
    return jnp.concatenate(picked, 0)


def with_rows(total, exact, positions):
    here = lax.broadcasted_iota(jnp.int32, (total.shape[0], 1), 0)
    for number, position in enumerate(positions):
        total = jnp.where(here == position, exact[number : number + 1], total)
    return total


def line_sum(block):
    count = lax.axis_size("tensor")
    total = block
    for bits in range(1, count):
        total = total + lax.ppermute(block, "tensor", [(i, i ^ bits) for i in range(count)])
    return total


def sum_everywhere(values, sizes):
    for axis, size in sizes:
        bit = 1
        while bit < size:
            values = values + lax.ppermute(values, axis, [(i, i ^ bit) for i in range(size)])
            bit *= 2
    return values


def body(
    tokens,
    segments,
    cotangent,
    attn_norm_gain,
    attn_norm_shift,
    w_query,
    w_key,
    w_value,
    w_gate,
    w_output,
    ffn_norm_gain,
    ffn_norm_shift,
    w_ffn_gate,
    w_ffn_up,
    w_ffn_down,
):
    seq_len = segments.shape[0]
    rows = tokens.shape[0]
    count = seq_len // rows
    dp_count = lax.axis_size("dp")
    place = lax.axis_index("tensor")
    hk = w_query.shape[1]
    ff = w_ffn_gate.shape[1]
    heads = hk // KEY_DIM
    mlp_step = min(256, ff)
    mlp_steps = ff // mlp_step
    head_ids = (place * heads + jnp.arange(heads, dtype=jnp.int32)).astype(F32)
    rates = jnp.log1p(-jnp.exp2(-5.0 - head_ids))

    def rows_of(stacked):
        return lambda owner, step: lax.dynamic_slice_in_dim(stacked, owner * rows, rows, 0)

    def slots_of(stacked):
        return lambda owner, step: rows_of(stacked)(owner_slot(place, owner, count), step)

    starts = [
        jnp.sum((segments < segments[0] + number).astype(jnp.int32)) for number in range(DOCUMENTS)
    ]
    own_starts = [start - place * rows for start in starts]

    last = count - 1
    residual = tokens.astype(F32)
    normed, first_pull = jax.vjp(layer_norm, residual, attn_norm_gain, attn_norm_shift)
    mixer_full = lax.all_gather(
        pack_mixer(w_query, w_key, w_value, w_gate, heads), "dp", axis=0, tiled=True
    )
    output_turned = pack_turned(w_output)
    ffn_shard = pack_mlp(w_ffn_gate, w_ffn_up, w_ffn_down, mlp_step)
    first = Gather(normed.astype(BF16), count)
    for step in range(1, count):
        first.step(*([output_turned, ffn_shard] if step == 2 else []))
    output_full = lax.all_gather(
        after(output_turned, *first.arrived(1)), "dp", axis=0, tiled=True
    )
    ffn_full = lax.all_gather(
        after(ffn_shard, *first.arrived(min(2, last))), "dp", axis=0, tiled=True
    )

    mixed, gate_pre, whole_normed = project(
        first.slots, mixer_full, [slot_owner(place, slot, count) for slot in range(count)]
    )

    cots = Gather(cotangent, count)
    cots.step(*first.arrived(last))
    gated_low, retained = retention(mixed, gate_pre, segments, rates)
    mixer = Scatter(rows_of(matmul(gated_low, output_full, 1, 1).astype(BF16)), count)
    few = few_product(few_rows(gated_low, starts), output_full)
    exact = line_sum(few)
    cots.step(whole_normed)
    for step in range(1, count):
        mixer.step(*cots.arrived(min(step + 1, last)), *([few] if step == last else []))
        if step < last - 1:
            cots.step()
    hidden = residual + with_rows(mixer.total(), exact, own_starts)
    normed_two, second_pull = jax.vjp(layer_norm, hidden, ffn_norm_gain, ffn_norm_shift)

    second = Gather(normed_two.astype(BF16), count)
    buffers = ()
    for slot in range(count):
        block = second.slots[slot]
        if slot < last:
            second.step(*buffers)
        else:
            block = after(block, *buffers)
        buffers = mlp_block(block, cots.slots[slot], ffn_full, slot, count, buffers)
    grad_pairs, inner, down_terms, back_terms = buffers

    slot_starts = [
        owner_slot(place, start // rows, count) * rows + start % rows for start in starts
    ]
    back = Scatter(slots_of(back_terms), count)
    few = few_product(few_rows(grad_pairs, slot_starts), ffn_full)
    started = back.step()
    exact = line_sum(few)
    mlp_part = weight_grad(jnp.concatenate(second.slots, 0), grad_pairs, 0, 3 * ff)
    mlp_part = weight_grad(jnp.concatenate(cots.slots, 0), inner, 2 * ff, 3 * ff, mlp_part)
    mlp_grad = dp_scatter(after(mlp_part, *started))
    for step in range(2, count):
        back.step(mlp_part, *([few] if step == last else []))
    grad_normed_two = with_rows(back.total(), exact, own_starts)
    grad_from_two, grad_ffn_gain_part, grad_ffn_shift_part = second_pull(grad_normed_two)
    grad_hidden = cotangent.astype(F32) + grad_from_two

    branch = Gather(grad_hidden.astype(BF16), count)
    down = Scatter(slots_of(down_terms), count)
    buffers, sent = (), ()
    for slot in range(count):
        block = branch.slots[slot]
        if slot < last:
            branch.step(*buffers)
        block = after(block, *buffers, *sent)
        if 0 < slot < last:
            sent = down.step(*branch.arrived(slot))
        buffers = place_product(
            block, output_full, slot_owner(place, slot, count), count, BF16, buffers
        )
    grad_gated, whole_branch = buffers
    output_part = weight_grad(whole_branch, gated_low, 0, gated_low.shape[1])
    output_grad = dp_scatter(output_part)
    sent = down.step()
    layer_output = (hidden + down.total()).astype(BF16)
    grads = retention_back(
        mixed, gate_pre, segments, rates, retained, after(grad_gated, output_part, mlp_grad)
    )

    normed_terms = []

    def far_of(owner, step):
        index = count - 1 - owner_slot(place, owner, count)
        chosen = normed_terms[0]
        for other in range(1, step):
            chosen = jnp.where(index >= other, normed_terms[other], chosen)
        return chosen

    def columns(grad, groups, first, size):
        stride = grad.shape[1] // groups
        parts = [grad[:, g * stride + first : g * stride + first + size] for g in range(groups)]
        return jnp.concatenate(parts, 1).astype(F32)

    pair_grad = mlp_grad[:, : 2 * ff]
    done_early = (
        layer_output,
        columns(pair_grad, mlp_steps, 0, mlp_step),
        columns(pair_grad, mlp_steps, mlp_step, mlp_step),
        mlp_grad[:, 2 * ff :].astype(F32).T,
        output_grad.astype(F32).T,
    )
    last_scatter = Scatter(far_of, count)
    source = after(grads, *sent)
    for index in range(count):
        normed_terms.append(
            back_product(source, mixer_full, slot_owner(place, count - 1 - index, count), rows)
        )
        if index < last:
            sent = last_scatter.step()
        if index == 0:
            mixer_part = weight_grad(
                whole_normed, after(grads, normed_terms[0]), 0, grads.shape[1]
            )
            mixer_grad = dp_scatter(after(mixer_part, *sent))
            source = after(grads, mixer_part)
    grad_normed = after(last_scatter.total(), *done_early)
    grad_from_one, grad_attn_gain_part, grad_attn_shift_part = first_pull(grad_normed)
    grad_tokens = grad_hidden + grad_from_one

    gains = sum_everywhere(
        jnp.stack(
            [grad_attn_gain_part, grad_attn_shift_part, grad_ffn_gain_part, grad_ffn_shift_part]
        ),
        (("dp", dp_count),),
    )
    mixer_grad = after(mixer_grad, gains)
    gains = sum_everywhere(after(gains, grad_tokens), (("tensor", count),))

    return (
        layer_output,
        grad_tokens,
        gains[0],
        gains[1],
        columns(mixer_grad, heads, 0, KEY_DIM),
        columns(mixer_grad, heads, KEY_DIM, KEY_DIM),
        columns(mixer_grad, heads, 2 * KEY_DIM, VALUE_DIM),
        columns(mixer_grad, heads, 2 * KEY_DIM + VALUE_DIM, VALUE_DIM),
        done_early[4],
        gains[2],
        gains[3],
        *done_early[1:4],
    )


def solution(mesh):
    split = P(("dp", "tensor"), None)
    weight = P("dp", "tensor")
    turned = P("tensor", "dp")
    return jax.shard_map(
        body,
        mesh=mesh,
        in_specs=(
            split, P("dp"), split, P(), P(), weight, weight, weight, weight, turned,
            P(), P(), weight, weight, turned,
        ),
        out_specs=(
            split, split, P(), P(), weight, weight, weight, weight, turned,
            P(), P(), weight, weight, turned,
        ),
        check_vma=False,
    )
```

```python
import functools

import jax
import jax.numpy as jnp
from jax import lax
from jax.experimental import pallas as pl
from jax.experimental.pallas import tpu as pltpu
from jax.sharding import PartitionSpec as P

KEY_DIM = 256
VALUE_DIM = 512
HEAD_COLS = 2 * KEY_DIM + 2 * VALUE_DIM
BLOCK = 256
F32 = jnp.float32
BF16 = jnp.bfloat16
MIB = 1024 * 1024


def layer_norm(values, gain, shift):
    centred = values - jnp.mean(values, -1, keepdims=True)
    spread = jnp.mean(centred * centred, -1, keepdims=True)
    return centred * lax.rsqrt(spread + 1e-05) * gain + shift


def matmul(left, right, left_dim=1, right_dim=0):
    return lax.dot_general(
        left, right, (((left_dim,), (right_dim,)), ((), ())), preferred_element_type=F32
    )


def sigmoid(values):
    return 1.0 / (1.0 + jnp.exp(-values))


ERFC_NEAR = (
    2.326819970068386e-2, -1.387039388740657e-1, 3.687424674597105e-1, -5.824733027278666e-1,
    6.210004621745983e-1, -4.944515323274145e-1, 3.404879937665872e-1, -2.741127028184656e-1,
    5.638259427386472e-1,
)
ERFC_FAR = (
    -1.047766399936249e1, 1.297719955372516e1, -7.495518717768503, 2.921019019210786,
    -1.015265279202700, 4.218463358204948e-1, -2.820767439740514e-1, 5.641895067754075e-1,
)


def series(values, coefficients):
    total = jnp.full_like(values, coefficients[0])
    for coefficient in coefficients[1:]:
        total = total * values + coefficient
    return total


def normal_below(values):
    scaled = values * (0.5**0.5)
    size = jnp.abs(scaled)
    bell = jnp.exp(-scaled * scaled)
    inverse = 1.0 / jnp.maximum(size, 1.0)
    square = inverse * inverse
    shape = jnp.where(size < 2.0, series(square, ERFC_NEAR), series(square, ERFC_FAR))
    tail = 0.5 * bell * inverse * shape
    outer = jnp.where(scaled > 0.0, 1.0 - tail, tail)
    return jnp.where(size < 1.0, 0.5 + 0.5 * lax.erf(scaled), outer), bell


def after(value, *others):
    return lax.optimization_barrier((value, *others))[0]


def kernel_params(mib):
    return pltpu.CompilerParams(vmem_limit_bytes=mib * MIB)


def pack_kernel(plan, *refs):
    *parts, out = refs
    for part, first, to, size, turned in plan:
        piece = parts[part][first : first + size, :].T if turned else parts[part][:, first : first + size]
        out[:, to : to + size] = piece


def pack(parts, plan, width):
    height = parts[0].shape[1] if plan[0][4] else parts[0].shape[0]
    return pl.pallas_call(
        functools.partial(pack_kernel, plan),
        out_shape=jax.ShapeDtypeStruct((height, width), BF16),
        cost_estimate=pl.CostEstimate(flops=0, bytes_accessed=4 * height * width, transcendentals=0),
        compiler_params=kernel_params(16),
        name="pack",
    )(*parts)


def pack_mixer(w_query, w_key, w_value, w_gate, heads):
    plan = []
    for head in range(heads):
        to = head * HEAD_COLS
        plan += [
            (0, head * KEY_DIM, to, KEY_DIM, False),
            (1, head * KEY_DIM, to + KEY_DIM, KEY_DIM, False),
            (2, head * VALUE_DIM, to + 2 * KEY_DIM, VALUE_DIM, False),
            (3, head * VALUE_DIM, to + 2 * KEY_DIM + VALUE_DIM, VALUE_DIM, False),
        ]
    return pack([w_query, w_key, w_value, w_gate], tuple(plan), heads * HEAD_COLS)


def pack_turned(weight):
    rows, columns = weight.shape
    return pack([weight], ((0, 0, 0, rows, True),), rows)


def pack_mlp(w_gate, w_up, w_down, step):
    hidden = w_down.shape[0]
    plan = []
    for at in range(0, hidden, step):
        plan += [(0, at, 2 * at, step, False), (1, at, 2 * at + step, step, False)]
    plan.append((2, 0, 2 * hidden, hidden, True))
    return pack([w_gate, w_up, w_down], tuple(plan), 3 * hidden)


def place_kernel(owner, rows_ref, weight_ref, *refs):
    product_ref, kept_ref = refs[-2:]
    product_ref[...] = matmul(rows_ref[...], weight_ref[...]).astype(product_ref.dtype)

    @pl.when(pl.program_id(0) == 0)
    def _():
        kept_ref[...] = rows_ref[...]


def place_product(rows, weight, owner, count, kind, buffers=()):
    height, depth = rows.shape
    width = weight.shape[1]
    step = min(512, width)
    row_spec = pl.BlockSpec((height, depth), lambda j, at: (0, 0))
    in_specs = [row_spec, pl.BlockSpec((depth, step), lambda j, at: (0, j))]
    operands = [owner.reshape(1), rows, weight]
    aliases = {}
    if buffers:
        operands += list(buffers)
        in_specs += [pl.BlockSpec(memory_space=pl.ANY)] * 2
        aliases = {3: 0, 4: 1}
    return pl.pallas_call(
        place_kernel,
        grid_spec=pltpu.PrefetchScalarGridSpec(
            num_scalar_prefetch=1,
            grid=(width // step,),
            in_specs=in_specs,
            out_specs=[
                pl.BlockSpec((height, step), lambda j, at: (at[0], j)),
                pl.BlockSpec((height, depth), lambda j, at: (at[0], 0)),
            ],
        ),
        out_shape=[
            jax.ShapeDtypeStruct((count * height, width), kind),
            jax.ShapeDtypeStruct((count * height, depth), BF16),
        ],
        input_output_aliases=aliases,
        cost_estimate=pl.CostEstimate(
            flops=2 * height * depth * width,
            bytes_accessed=2 * depth * width + 8 * height * width,
            transcendentals=0,
        ),
        compiler_params=kernel_params(12),
        name="place_product",
    )(*operands)


def project_kernel(owners, *refs):
    count = len(refs) - 4
    weight_ref, mixed_ref, gate_ref, kept_ref = refs[count:]
    height = refs[0].shape[0]
    at = pl.program_id(0)
    for slot in range(count):
        here = pl.ds(pl.multiple_of(owners[slot] * height, height), height)
        product = matmul(refs[slot][...], weight_ref[...])

        @pl.when(at % 3 < 2)
        def _(here=here, product=product):
            mixed_ref[here, :] = product.astype(BF16)

        @pl.when(at % 3 == 2)
        def _(here=here, product=product):
            gate_ref[here, :] = product

        @pl.when(at == 0)
        def _(slot=slot, here=here):
            kept_ref[here, :] = refs[slot][...]


def project(slots, weight, owners):
    count = len(slots)
    height, depth = slots[0].shape
    width = weight.shape[1]
    heads = width // HEAD_COLS
    step = VALUE_DIM
    row_spec = pl.BlockSpec((height, depth), lambda j, at: (0, 0))
    return pl.pallas_call(
        project_kernel,
        grid_spec=pltpu.PrefetchScalarGridSpec(
            num_scalar_prefetch=1,
            grid=(3 * heads,),
            in_specs=[row_spec] * count + [pl.BlockSpec((depth, step), lambda j, at: (0, j))],
            out_specs=[
                pl.BlockSpec((count * height, step), lambda j, at: (0, 2 * (j // 3) + jnp.minimum(j % 3, 1))),
                pl.BlockSpec((count * height, step), lambda j, at: (0, j // 3)),
                pl.BlockSpec((count * height, depth), lambda j, at: (0, 0)),
            ],
        ),
        out_shape=[
            jax.ShapeDtypeStruct((count * height, heads * 2 * step), BF16),
            jax.ShapeDtypeStruct((count * height, heads * step), F32),
            jax.ShapeDtypeStruct((count * height, depth), BF16),
        ],
        cost_estimate=pl.CostEstimate(
            flops=2 * count * height * depth * width,
            bytes_accessed=2 * depth * width + 4 * count * height * width,
            transcendentals=0,
        ),
        compiler_params=kernel_params(max(52, 12 + 4 * count)),
        name="project",
    )(jnp.stack(owners), *slots, weight)


def back_kernel(owner, rows_ref, weight_ref, out_ref):
    out_ref[...] = matmul(rows_ref[...], weight_ref[...], 1, 1).astype(out_ref.dtype)


def back_product(source, weight, owner, height):
    depth = source.shape[1]
    width = weight.shape[0]
    step = min(512, width)
    return pl.pallas_call(
        back_kernel,
        grid_spec=pltpu.PrefetchScalarGridSpec(
            num_scalar_prefetch=1,
            grid=(width // step,),
            in_specs=[
                pl.BlockSpec((height, depth), lambda j, at: (at[0], 0)),
                pl.BlockSpec((step, depth), lambda j, at: (j, 0)),
            ],
            out_specs=pl.BlockSpec((height, step), lambda j, at: (0, j)),
        ),
        out_shape=jax.ShapeDtypeStruct((height, width), BF16),
        cost_estimate=pl.CostEstimate(
            flops=2 * height * depth * width,
            bytes_accessed=2 * depth * width + 6 * height * width,
            transcendentals=0,
        ),
        compiler_params=kernel_params(50),
        name="back_product",
    )(owner.reshape(1), source, weight)


def few_kernel(rows_ref, weight_ref, out_ref):
    out_ref[...] = matmul(rows_ref[...], weight_ref[...], 1, 1)


def few_product(rows, weight):
    height, length = rows.shape
    depth = weight.shape[0]
    step = min(512, depth)
    return pl.pallas_call(
        few_kernel,
        grid=(depth // step,),
        in_specs=[
            pl.BlockSpec((height, length), lambda j: (0, 0)),
            pl.BlockSpec((step, length), lambda j: (j, 0)),
        ],
        out_specs=pl.BlockSpec((height, step), lambda j: (0, j)),
        out_shape=jax.ShapeDtypeStruct((height, depth), F32),
        cost_estimate=pl.CostEstimate(
            flops=2 * height * length * depth, bytes_accessed=2 * length * depth, transcendentals=0
        ),
        compiler_params=kernel_params(50),
        name="few_product",
    )(rows, weight)


def decay_block(rate, first, seg_col, seg_row, width):
    height = seg_col.shape[0]
    down = lax.broadcasted_iota(jnp.int32, (height, 1), 0)
    across = lax.broadcasted_iota(jnp.int32, (1, width), 1)
    inside = (down + first >= across) & (seg_col == seg_row)
    distance = jnp.where(inside, down + first - across, 0).astype(F32)
    return jnp.where(inside, jnp.exp(distance * rate), 0.0)


def retention_kernel(blocks, rates, seg_col, seg_row, query, keys, values, gate, gated, retained):
    head, at = pl.program_id(0), pl.program_id(1)
    height = query.shape[0]

    for block in range(blocks):

        @pl.when(at == block)
        def _(block=block):
            width = (block + 1) * height
            decay = decay_block(rates[head], block * height, seg_col[...], seg_row[:, :width], width)
            scores = matmul(query[...], keys[:width, :], 1, 1)
            mixed = matmul((scores * decay).astype(BF16), values[:width, :])
            retained[...] = mixed
            normal = mixed * lax.rsqrt(jnp.mean(mixed * mixed, -1, keepdims=True) + 1e-06)
            pre = gate[...]
            gated[...] = (pre * sigmoid(pre) * normal).astype(BF16)


def head_specs(seq_len):
    return [
        pl.BlockSpec(memory_space=pltpu.SMEM),
        pl.BlockSpec((BLOCK, 1), lambda h, i: (i, 0)),
        pl.BlockSpec((1, seq_len), lambda h, i: (0, 0)),
        pl.BlockSpec((BLOCK, KEY_DIM), lambda h, i: (i, 4 * h)),
        pl.BlockSpec((seq_len, KEY_DIM), lambda h, i: (0, 4 * h + 1)),
        pl.BlockSpec((seq_len, VALUE_DIM), lambda h, i: (0, 2 * h + 1)),
        pl.BlockSpec((BLOCK, VALUE_DIM), lambda h, i: (i, h)),
    ]


def retention(mixed, gate_pre, segments, rates):
    seq_len = segments.shape[0]
    heads = rates.shape[0]
    blocks = seq_len // BLOCK
    out_spec = pl.BlockSpec((BLOCK, VALUE_DIM), lambda h, i: (i, h))
    return pl.pallas_call(
        functools.partial(retention_kernel, blocks),
        grid=(heads, blocks),
        in_specs=head_specs(seq_len),
        out_specs=[out_spec, out_spec],
        out_shape=[
            jax.ShapeDtypeStruct((seq_len, heads * VALUE_DIM), BF16),
            jax.ShapeDtypeStruct((seq_len, heads * VALUE_DIM), F32),
        ],
        cost_estimate=pl.CostEstimate(
            flops=2 * heads * seq_len * seq_len * (KEY_DIM + VALUE_DIM),
            bytes_accessed=10 * seq_len * heads * HEAD_COLS,
            transcendentals=0,
        ),
        compiler_params=kernel_params(50),
        name="retention",
    )(rates, segments.reshape(seq_len, 1), segments.reshape(1, seq_len), mixed, mixed, mixed, gate_pre)


def retention_back_kernel(
    blocks, rates, seg_col, seg_row, query, keys, values, gate, retained, grad_gated, grads, key_total, value_total
):
    head, at = pl.program_id(0), pl.program_id(1)
    height = query.shape[0]

    @pl.when(at == 0)
    def _():
        key_total[...] = jnp.zeros_like(key_total)
        value_total[...] = jnp.zeros_like(value_total)

    for block in range(blocks):

        @pl.when(at == block)
        def _(block=block):
            width = (block + 1) * height
            here = slice(block * height, width)
            mixed = retained[...]
            scale = lax.rsqrt(jnp.mean(mixed * mixed, -1, keepdims=True) + 1e-06)
            normal = mixed * scale
            pre = gate[...]
            grad = grad_gated[...].astype(F32)
            open_part = sigmoid(pre)
            grads[here, 2 * KEY_DIM + VALUE_DIM :] = (
                grad * normal * (open_part * (1.0 + pre * (1.0 - open_part)))
            ).astype(BF16)
            grad_normal = grad * (pre * open_part)
            grad_mixed = (
                scale * (grad_normal - normal * jnp.mean(grad_normal * normal, -1, keepdims=True))
            ).astype(BF16)
            decay = decay_block(rates[head], block * height, seg_col[...], seg_row[:, :width], width)
            query_low = query[...]
            weights = (matmul(query_low, keys[:width, :], 1, 1) * decay).astype(BF16)
            grad_scores = (matmul(grad_mixed, values[:width, :], 1, 1) * decay).astype(BF16)
            grads[here, :KEY_DIM] = matmul(grad_scores, keys[:width, :]).astype(BF16)
            key_total[:width, :] += matmul(grad_scores, query_low, 0, 0)
            value_total[:width, :] += matmul(weights, grad_mixed, 0, 0)

    @pl.when(at == blocks - 1)
    def _():
        grads[:, KEY_DIM : 2 * KEY_DIM] = key_total[...].astype(BF16)
        grads[:, 2 * KEY_DIM : 2 * KEY_DIM + VALUE_DIM] = value_total[...].astype(BF16)


def retention_back(mixed, gate_pre, segments, rates, retained, grad_gated):
    seq_len = segments.shape[0]
    heads = rates.shape[0]
    blocks = seq_len // BLOCK
    side_spec = pl.BlockSpec((BLOCK, VALUE_DIM), lambda h, i: (i, h))
    return pl.pallas_call(
        functools.partial(retention_back_kernel, blocks),
        grid=(heads, blocks),
        in_specs=head_specs(seq_len) + [side_spec, side_spec],
        out_specs=pl.BlockSpec((seq_len, HEAD_COLS), lambda h, i: (0, h)),
        out_shape=jax.ShapeDtypeStruct((seq_len, heads * HEAD_COLS), BF16),
        scratch_shapes=[
            pltpu.VMEM((seq_len, KEY_DIM), F32),
            pltpu.VMEM((seq_len, VALUE_DIM), F32),
        ],
        cost_estimate=pl.CostEstimate(
            flops=2 * heads * seq_len * seq_len * (3 * KEY_DIM + 2 * VALUE_DIM),
            bytes_accessed=12 * seq_len * heads * HEAD_COLS,
            transcendentals=0,
        ),
        compiler_params=kernel_params(max(50, 10 + seq_len // 45)),
        name="retention_back",
    )(
        rates, segments.reshape(seq_len, 1), segments.reshape(1, seq_len),
        mixed, mixed, mixed, gate_pre, retained, grad_gated,
    )


def mlp_kernel(steps, rows, cot, pair_w, down_w, *refs):
    pair_out, inner_out, down_terms, back_terms, down_total, back_total = refs[-6:]
    at = pl.program_id(0)
    half = down_w.shape[1]
    pair = matmul(rows[...], pair_w[...])
    gate, up = pair[:, :half], pair[:, half:]
    grad_inner = matmul(cot[...], down_w[...]).astype(BF16).astype(F32)
    below, bell = normal_below(gate)
    slope = below + gate * (bell * 0.3989422804014327)
    bent = gate * below
    inner = (bent * up).astype(BF16)
    grad_pair = jnp.concatenate(
        [(grad_inner * up * slope).astype(BF16), (grad_inner * bent).astype(BF16)], 1
    )
    inner_out[...] = inner
    pair_out[...] = grad_pair
    down_part = matmul(inner, down_w[...], 1, 1)
    back_part = matmul(grad_pair, pair_w[...], 1, 1)

    @pl.when(at == 0)
    def _():
        down_total[...] = down_part
        back_total[...] = back_part

    @pl.when(at > 0)
    def _():
        down_total[...] += down_part
        back_total[...] += back_part

    @pl.when(at == steps - 1)
    def _():
        down_terms[...] = down_total[...].astype(down_terms.dtype)
        back_terms[...] = back_total[...].astype(back_terms.dtype)


def mlp_block(rows, cot, weights, slot, count, buffers=()):
    height, depth = rows.shape
    hidden = weights.shape[1] // 3
    step = min(256, hidden)
    steps = hidden // step
    row_spec = pl.BlockSpec((height, depth), lambda j: (0, 0))
    in_specs = [
        row_spec,
        row_spec,
        pl.BlockSpec((depth, 2 * step), lambda j: (0, j)),
        pl.BlockSpec((depth, step), lambda j: (0, 2 * steps + j)),
    ]
    operands = [rows, cot, weights, weights]
    aliases = {}
    if buffers:
        operands += list(buffers)
        in_specs += [pl.BlockSpec(memory_space=pl.ANY)] * 4
        aliases = {4: 0, 5: 1, 6: 2, 7: 3}
    wide_spec = pl.BlockSpec((height, depth), lambda j: (slot, 0))
    return pl.pallas_call(
        functools.partial(mlp_kernel, steps),
        grid=(steps,),
        in_specs=in_specs,
        out_specs=[
            pl.BlockSpec((height, 2 * step), lambda j: (slot, j)),
            pl.BlockSpec((height, step), lambda j: (slot, j)),
            wide_spec,
            wide_spec,
        ],
        out_shape=[
            jax.ShapeDtypeStruct((count * height, 2 * hidden), BF16),
            jax.ShapeDtypeStruct((count * height, hidden), BF16),
            jax.ShapeDtypeStruct((count * height, depth), BF16),
            jax.ShapeDtypeStruct((count * height, depth), BF16),
        ],
        scratch_shapes=[pltpu.VMEM((height, depth), F32)] * 2,
        input_output_aliases=aliases,
        cost_estimate=pl.CostEstimate(
            flops=12 * height * depth * hidden,
            bytes_accessed=6 * depth * hidden + 20 * height * depth,
            transcendentals=0,
        ),
        compiler_params=kernel_params(28),
        name="mlp_block",
    )(*operands)


def weight_grad_kernel(left, right, *refs):
    refs[-1][...] = matmul(left[...], right[...], 0, 0).astype(BF16)


def weight_grad(left, right, first, width, buffer=None):
    length, depth = left.shape
    columns = right.shape[1]
    step = min(512, columns)
    in_specs = [
        pl.BlockSpec((length, depth), lambda j: (0, 0)),
        pl.BlockSpec((length, step), lambda j: (0, j)),
    ]
    operands = [left, right]
    aliases = {}
    if buffer is not None:
        operands.append(buffer)
        in_specs.append(pl.BlockSpec(memory_space=pl.ANY))
        aliases = {2: 0}
    return pl.pallas_call(
        weight_grad_kernel,
        grid=(columns // step,),
        in_specs=in_specs,
        out_specs=pl.BlockSpec((depth, step), lambda j: (0, first // step + j)),
        out_shape=jax.ShapeDtypeStruct((depth, width), BF16),
        input_output_aliases=aliases,
        cost_estimate=pl.CostEstimate(
            flops=2 * length * depth * columns,
            bytes_accessed=2 * length * (depth + columns) + 2 * depth * columns,
            transcendentals=0,
        ),
        compiler_params=kernel_params(16 + length // 64),
        name="weight_grad",
    )(*operands)


class Gather:
    def __init__(self, block, count):
        self.count = count
        self.from_left, self.from_right, self.slots = [block], [block], [block]

    def step(self, *ready):
        count, step = self.count, len(self.slots)
        place = lax.axis_index("tensor")
        left, right = self.from_left[-1], self.from_right[-1]
        if ready:
            left, right = lax.optimization_barrier((left, right, *ready))[:2]
        self.from_left.append(
            lax.ppermute(left, "tensor", [(i, i + 1) for i in range(step - 1, count - 1)])
        )
        self.from_right.append(
            lax.ppermute(right, "tensor", [(i + 1, i) for i in range(count - step)])
        )
        chosen = None
        for owner in range(count):
            rights = count - 1 - owner
            if owner < count // 2:
                wanted = self.from_right[step] if step <= rights else self.from_left[step - rights]
            else:
                wanted = self.from_left[step] if step <= owner else self.from_right[step - owner]
            chosen = wanted if chosen is None else jnp.where(place >= owner, wanted, chosen)
        self.slots.append(chosen)
        return self.arrived(step)

    def arrived(self, step):
        return (self.from_left[step], self.from_right[step])


class Scatter:
    def __init__(self, block_of, count):
        self.block_of, self.count, self.steps = block_of, count, 0
        self.to_right = self.to_left = None

    def step(self, *ready):
        count = self.count
        place = lax.axis_index("tensor")
        self.steps += 1
        step = self.steps
        ahead = count - step
        right = self.block_of(jnp.minimum(place + ahead, count - 1), step).astype(F32)
        left = self.block_of(jnp.maximum(place - ahead, 0), step).astype(F32)
        if step > 1:
            came_right, came_left = lax.optimization_barrier((self.to_right, self.to_left))
            right = right + came_right.astype(F32)
            left = left + came_left.astype(F32)
        right, left = right.astype(BF16), left.astype(BF16)
        if ready:
            right, left = lax.optimization_barrier((right, left, *ready))[:2]
        self.to_right = lax.ppermute(right, "tensor", [(i, i + 1) for i in range(step)])
        self.to_left = lax.ppermute(
            left, "tensor", [(i + 1, i) for i in range(count - 1 - step, count - 1)]
        )
        return (self.to_right, self.to_left)

    def total(self):
        own = self.block_of(lax.axis_index("tensor"), self.count).astype(F32)
        if self.steps:
            own = own + (self.to_right.astype(F32) + self.to_left.astype(F32))
        return own


def slot_owner(place, slot, count):
    rights = count - 1 - place
    first_half = jnp.where(slot <= rights, place + slot, place - (slot - rights))
    second_half = jnp.where(slot <= place, place - slot, slot)
    return jnp.where(place < count // 2, first_half, second_half)


def owner_slot(place, owner, count):
    rights = count - 1 - place
    first_half = jnp.where(owner >= place, owner - place, rights + place - owner)
    second_half = jnp.where(owner <= place, place - owner, owner)
    return jnp.where(place < count // 2, first_half, second_half)


def dp_scatter(part):
    return lax.psum_scatter(part, "dp", scatter_dimension=0, tiled=True)


DOCUMENTS = 3
FEW = 16


def few_rows(stacked, positions):
    picked = [lax.dynamic_slice_in_dim(stacked, position, 1, 0) for position in positions]
    picked.append(jnp.zeros((FEW - len(picked), stacked.shape[1]), stacked.dtype))
    return jnp.concatenate(picked, 0)


def with_rows(total, exact, positions):
    here = lax.broadcasted_iota(jnp.int32, (total.shape[0], 1), 0)
    for number, position in enumerate(positions):
        total = jnp.where(here == position, exact[number : number + 1], total)
    return total


def line_sum(block):
    count = lax.axis_size("tensor")
    total = block
    for bits in range(1, count):
        total = total + lax.ppermute(block, "tensor", [(i, i ^ bits) for i in range(count)])
    return total


def sum_everywhere(values, sizes):
    for axis, size in sizes:
        bit = 1
        while bit < size:
            values = values + lax.ppermute(values, axis, [(i, i ^ bit) for i in range(size)])
            bit *= 2
    return values


def body(
    tokens,
    segments,
    cotangent,
    attn_norm_gain,
    attn_norm_shift,
    w_query,
    w_key,
    w_value,
    w_gate,
    w_output,
    ffn_norm_gain,
    ffn_norm_shift,
    w_ffn_gate,
    w_ffn_up,
    w_ffn_down,
):
    seq_len = segments.shape[0]
    rows = tokens.shape[0]
    count = seq_len // rows
    dp_count = lax.axis_size("dp")
    place = lax.axis_index("tensor")
    hk = w_query.shape[1]
    ff = w_ffn_gate.shape[1]
    heads = hk // KEY_DIM
    mlp_step = min(256, ff)
    mlp_steps = ff // mlp_step
    head_ids = (place * heads + jnp.arange(heads, dtype=jnp.int32)).astype(F32)
    rates = jnp.log1p(-jnp.exp2(-5.0 - head_ids))

    def rows_of(stacked):
        return lambda owner, step: lax.dynamic_slice_in_dim(stacked, owner * rows, rows, 0)

    def slots_of(stacked):
        return lambda owner, step: rows_of(stacked)(owner_slot(place, owner, count), step)

    starts = [
        jnp.sum((segments < segments[0] + number).astype(jnp.int32)) for number in range(DOCUMENTS)
    ]
    own_starts = [start - place * rows for start in starts]

    last = count - 1
    residual = tokens.astype(F32)
    normed, first_pull = jax.vjp(layer_norm, residual, attn_norm_gain, attn_norm_shift)
    normed_low = normed.astype(BF16)
    mixer_full = lax.all_gather(
        pack_mixer(after(w_query, normed_low), w_key, w_value, w_gate, heads), "dp", axis=0, tiled=True
    )
    output_turned = pack_turned(w_output)
    ffn_shard = pack_mlp(w_ffn_gate, w_ffn_up, w_ffn_down, mlp_step)
    first = Gather(normed_low, count)
    for step in range(1, count):
        first.step(*([output_turned, ffn_shard] if step == 2 else []))
    output_full = lax.all_gather(
        after(output_turned, *first.arrived(1)), "dp", axis=0, tiled=True
    )
    ffn_full = lax.all_gather(
        after(ffn_shard, *first.arrived(min(2, last))), "dp", axis=0, tiled=True
    )

    mixed, gate_pre, whole_normed = project(
        first.slots, mixer_full, [slot_owner(place, slot, count) for slot in range(count)]
    )

    cots = Gather(cotangent, count)
    cots.step(whole_normed)
    gated_low, retained = retention(mixed, gate_pre, segments, rates)
    mixer = Scatter(rows_of(matmul(gated_low, output_full, 1, 1).astype(BF16)), count)
    few = few_product(few_rows(gated_low, starts), output_full)
    exact = line_sum(few)
    for step in range(1, count):
        mixer.step(*cots.arrived(step), *([few] if step == last else []))
        if step < last:
            cots.step()
    hidden = residual + with_rows(mixer.total(), exact, own_starts)
    normed_two, second_pull = jax.vjp(layer_norm, hidden, ffn_norm_gain, ffn_norm_shift)

    second = Gather(normed_two.astype(BF16), count)
    buffers = ()
    for slot in range(count):
        block = second.slots[slot]
        if slot < last:
            second.step(*buffers)
        else:
            block = after(block, *buffers)
        buffers = mlp_block(block, cots.slots[slot], ffn_full, slot, count, buffers)
    grad_pairs, inner, down_terms, back_terms = buffers

    slot_starts = [
        owner_slot(place, start // rows, count) * rows + start % rows for start in starts
    ]
    back = Scatter(slots_of(back_terms), count)
    few = few_product(few_rows(grad_pairs, slot_starts), ffn_full)
    started = back.step()
    exact = line_sum(few)
    mlp_part = weight_grad(jnp.concatenate(second.slots, 0), grad_pairs, 0, 3 * ff)
    mlp_part = weight_grad(jnp.concatenate(cots.slots, 0), inner, 2 * ff, 3 * ff, mlp_part)
    mlp_grad = dp_scatter(after(mlp_part, *started))
    for step in range(2, count):
        back.step(mlp_part, *([few] if step == last else []))
    grad_normed_two = with_rows(back.total(), exact, own_starts)
    grad_from_two, grad_ffn_gain_part, grad_ffn_shift_part = second_pull(grad_normed_two)
    grad_hidden = cotangent.astype(F32) + grad_from_two

    branch = Gather(grad_hidden.astype(BF16), count)
    down = Scatter(slots_of(down_terms), count)
    buffers, sent = (), ()
    for slot in range(count):
        block = branch.slots[slot]
        if slot < last:
            branch.step(*buffers)
        block = after(block, *buffers, *sent)
        if 0 < slot < last:
            sent = down.step(*branch.arrived(slot))
        buffers = place_product(
            block, output_full, slot_owner(place, slot, count), count, BF16, buffers
        )
    grad_gated, whole_branch = buffers
    output_part = weight_grad(whole_branch, gated_low, 0, gated_low.shape[1])
    output_grad = dp_scatter(output_part)
    sent = down.step()
    layer_output = (hidden + down.total()).astype(BF16)
    grads = retention_back(
        mixed, gate_pre, segments, rates, retained, after(grad_gated, output_part, mlp_grad)
    )

    normed_terms = []

    def far_of(owner, step):
        index = count - 1 - owner_slot(place, owner, count)
        chosen = normed_terms[0]
        for other in range(1, step):
            chosen = jnp.where(index >= other, normed_terms[other], chosen)
        return chosen

    def columns(grad, groups, first, size):
        stride = grad.shape[1] // groups
        parts = [grad[:, g * stride + first : g * stride + first + size] for g in range(groups)]
        return jnp.concatenate(parts, 1).astype(F32)

    pair_grad = mlp_grad[:, : 2 * ff]
    done_early = (
        layer_output,
        columns(pair_grad, mlp_steps, 0, mlp_step),
        columns(pair_grad, mlp_steps, mlp_step, mlp_step),
        mlp_grad[:, 2 * ff :].astype(F32).T,
        output_grad.astype(F32).T,
    )
    last_scatter = Scatter(far_of, count)
    source = after(grads, *sent)
    for index in range(count):
        normed_terms.append(
            back_product(source, mixer_full, slot_owner(place, count - 1 - index, count), rows)
        )
        if index < last:
            sent = last_scatter.step()
        if index == 0:
            mixer_part = weight_grad(
                whole_normed, after(grads, normed_terms[0]), 0, grads.shape[1]
            )
            mixer_grad = dp_scatter(after(mixer_part, *sent))
            source = after(grads, mixer_part)
    grad_normed = after(last_scatter.total(), *done_early)
    grad_from_one, grad_attn_gain_part, grad_attn_shift_part = first_pull(grad_normed)
    grad_tokens = grad_hidden + grad_from_one

    gains = sum_everywhere(
        jnp.stack(
            [grad_attn_gain_part, grad_attn_shift_part, grad_ffn_gain_part, grad_ffn_shift_part]
        ),
        (("dp", dp_count),),
    )
    mixer_grad = after(mixer_grad, gains)
    gains = sum_everywhere(after(gains, grad_tokens), (("tensor", count),))

    return (
        layer_output,
        grad_tokens,
        gains[0],
        gains[1],
        columns(mixer_grad, heads, 0, KEY_DIM),
        columns(mixer_grad, heads, KEY_DIM, KEY_DIM),
        columns(mixer_grad, heads, 2 * KEY_DIM, VALUE_DIM),
        columns(mixer_grad, heads, 2 * KEY_DIM + VALUE_DIM, VALUE_DIM),
        done_early[4],
        gains[2],
        gains[3],
        *done_early[1:4],
    )


def solution(mesh):
    split = P(("dp", "tensor"), None)
    weight = P("dp", "tensor")
    turned = P("tensor", "dp")
    return jax.shard_map(
        body,
        mesh=mesh,
        in_specs=(
            split, P("dp"), split, P(), P(), weight, weight, weight, weight, turned,
            P(), P(), weight, weight, turned,
        ),
        out_specs=(
            split, split, P(), P(), weight, weight, weight, weight, turned,
            P(), P(), weight, weight, turned,
        ),
        check_vma=False,
    )
```
